32 devices in a mesh: dp: 8 (over z, x), tensor: 4 (over y, core).
Axes of the slice: x: 2, y: 2, z: 4, core: 2. Of those that a mesh axis runs over, the one named last changes fastest.
Arguments:
- hidden: bfloat16 [2048, 1024], P('dp'), may hold values from -6 to 6
- positions: int32 [2048], P('dp'), may hold values from 0 to 255, as said below
- out_grad: bfloat16 [2048, 1024], P('dp'), may hold values from -6 to 6
- norm_one: float32 [1024], replicated, may hold values from 0.5 to 1.5
- zx_weight: bfloat16 [1024, 2, 1536], P(None, None, 'tensor'), may hold values from -0.1875 to 0.1875
- bc_weight: bfloat16 [1024, 256], replicated, may hold values from -0.1875 to 0.1875
- dt_weight: bfloat16 [1024, 24], P(None, 'tensor'), may hold values from -0.1875 to 0.1875
- conv_inner: float32 [5, 1536], P(None, 'tensor'), may hold values from -0.5 to 0.5
- conv_state: float32 [5, 256], replicated, may hold values from -0.5 to 0.5
- decay_log: float32 [24], P('tensor'), may hold values from 0 to 2.77
- dt_bias: float32 [24], P('tensor'), may hold values from -6 to -2
- skip_gain: float32 [24], P('tensor'), may hold values from 0.5 to 1.5
- gated_gain: float32 [1536], P('tensor'), may hold values from 0.5 to 1.5
- out_weight: bfloat16 [1536, 1024], P('tensor'), may hold values from -0.15625 to 0.15625
- q_weight: bfloat16 [1024, 512], P(None, 'tensor'), may hold values from -0.1875 to 0.1875
- kv_weight: bfloat16 [1024, 2, 128], replicated, may hold values from -0.1875 to 0.1875
- o_weight: bfloat16 [512, 1024], P('tensor'), may hold values from -1 to 1
- norm_two: float32 [1024], replicated, may hold values from 0.5 to 1.5
- gu_weight: bfloat16 [1024, 2, 2048], P(None, None, 'tensor'), may hold values from -0.1875 to 0.1875
- down_weight: bfloat16 [2048, 1024], P('tensor'), may hold values from -0.125 to 0.125
Outputs:
- layer_out: bfloat16 [2048, 1024], P('dp')
- input_grad: bfloat16 [2048, 1024], P('dp')
- norm_one_grad: float32 [1024], replicated
- zx_grad: float32 [1024, 2, 1536], P('dp', None, 'tensor')
- bc_grad: float32 [1024, 256], P('dp')
- dt_grad: float32 [1024, 24], P('dp', 'tensor')
- conv_inner_grad: float32 [5, 1536], P(None, 'tensor')
- conv_state_grad: float32 [5, 256], replicated
- decay_log_grad: float32 [24], P('tensor')
- dt_bias_grad: float32 [24], P('tensor')
- skip_gain_grad: float32 [24], P('tensor')
- gated_gain_grad: float32 [1536], P('tensor')
- out_weight_grad: float32 [1536, 1024], P('tensor', 'dp')
- q_grad: float32 [1024, 512], P('dp', 'tensor')
- kv_grad: float32 [1024, 2, 128], P('dp')
- o_weight_grad: float32 [512, 1024], P('tensor', 'dp')
- norm_two_grad: float32 [1024], replicated
- gu_grad: float32 [1024, 2, 2048], P('dp', None, 'tensor')
- down_grad: float32 [2048, 1024], P('tensor', 'dp')
The draws below stay inside these ranges and needn't reach their ends.
Inputs may be any that keep to these rules, and one draw needn't show every extreme that they name: `positions`: each sequence of 256 tokens holds whole documents; a position counts from 0 at a document's first token, and every sequence begins a document; the first sequence is one document.
All inputs are finite; a program needn't handle non-finite values.
Results may differ from the reference program's by a relative error of at most 0.012.
Values sent between devices are 32-bit elements; how exact they have to be, the bound alone decides.
No kernel may reach another device: no remote copies, remote signals or barrier semaphores. Data moves between devices by JAX's collectives and lax.ppermute only.
A program may use at most 128 MiB of HBM per device.

```python
import jax
import jax.numpy as jnp
from jax import lax

D = 1024
HEADS_M = 24
NS = 128
KC = 4
QH = 8
KVH = 2
HD = 64
FF = 2048
TOK_DEV = 256
BLK = 128
INNER = 1536
TOKENS = 2048
N_TENSOR = 4


def draw_positions(key, part):
    key = jax.random.fold_in(key, 11)
    row_count = TOKENS // TOK_DEV
    starts = jax.random.randint(key, (row_count, TOK_DEV), 0, TOK_DEV // 4) == 0
    row_index = lax.broadcasted_iota(jnp.int32, (row_count, TOK_DEV), 0)
    col_index = lax.broadcasted_iota(jnp.int32, (row_count, TOK_DEV), 1)
    starts = starts & (row_index > 0) | (col_index == 0)
    latest = lax.cummax(jnp.where(starts, col_index, 0), axis=1)
    return (col_index - latest).reshape(TOKENS).astype(jnp.int32)


def levels(rng, extent, split, low, top_value):
    level, own = 1.0, jax.random.fold_in(rng, 6)
    for axis_at, blocks in split:
        draws = jnp.exp(jax.random.uniform(jax.random.fold_in(own, axis_at), (blocks,), jnp.float32, low / len(split), top_value / len(split)))
        level = level * jnp.repeat(draws, extent[axis_at] // blocks).reshape([-1 if axis == axis_at else 1 for axis in range(len(extent))])
    return level


def normal_values(rng, dims, deviation, most, pieces=(), kind=jnp.bfloat16):
    loudness = levels(rng, dims, pieces, -0.22, 0.18) if pieces else 1.0
    array = jax.random.normal(rng, dims, jnp.float32) * deviation * loudness
    return jnp.minimum(jnp.maximum(array, -most), most).astype(kind)


def setup_inputs(seed: int = 0) -> dict:
    seeds = jax.random.split(jax.random.key(seed), 21)
    return {
        "hidden": normal_values(seeds[0], (TOKENS, D), 1.0, 6.0, ((0, 8),)),
        "positions": draw_positions(jax.random.fold_in(seeds[20], 71), 0),
        "out_grad": normal_values(seeds[2], (TOKENS, D), 1.0, 6.0, ((0, 8),)),
        "norm_one": jnp.clip(1.0 + 0.1 * jax.random.normal(seeds[3], (D,), jnp.float32), 0.5, 1.5),
        "zx_weight": normal_values(seeds[4], (D, 2, INNER), D ** -0.5, 0.1875, ((2, 4),)),
        "bc_weight": normal_values(seeds[5], (D, 2 * NS), D ** -0.5, 0.1875),
        "dt_weight": normal_values(seeds[6], (D, HEADS_M), D ** -0.5, 0.1875, ((1, 4),)),
        "conv_inner": jnp.clip(jax.random.uniform(seeds[7], (KC + 1, INNER), jnp.float32, -0.5, 0.5) * levels(seeds[7], (KC + 1, INNER), ((1, 4),), -0.4, 0.0), -0.5, 0.5),
        "conv_state": jnp.clip(jax.random.uniform(seeds[8], (KC + 1, 2 * NS), jnp.float32, -0.5, 0.5), -0.5, 0.5),
        "decay_log": jnp.clip(2.77 * jax.random.uniform(seeds[9], (HEADS_M,), jnp.float32) ** levels(seeds[9], (HEADS_M,), ((0, 4),), -0.2, 0.2), 0.0, 2.77),
        "dt_bias": jnp.clip(-6.0 + 4.0 * jax.random.uniform(seeds[10], (HEADS_M,), jnp.float32) ** levels(seeds[10], (HEADS_M,), ((0, 4),), -0.2, 0.2), -6.0, -2.0),
        "skip_gain": jnp.clip(0.5 + 1.0 * jax.random.uniform(seeds[11], (HEADS_M,), jnp.float32) ** levels(seeds[11], (HEADS_M,), ((0, 4),), -0.2, 0.2), 0.5, 1.5),
        "gated_gain": jnp.clip(1.0 + 0.1 * jax.random.normal(seeds[12], (INNER,), jnp.float32), 0.5, 1.5),
        "out_weight": normal_values(seeds[13], (INNER, D), INNER ** -0.5, 0.15625, ((0, 4),)),
        "q_weight": normal_values(seeds[14], (D, QH * HD), D ** -0.5, 0.1875, ((1, 4),)),
        "kv_weight": normal_values(seeds[15], (D, 2, KVH * HD), D ** -0.5, 0.1875),
        "o_weight": normal_values(seeds[16], (QH * HD, D), (QH * HD // 16) ** -0.5, 1.0, ((0, 4),)),
        "norm_two": jnp.clip(1.0 + 0.1 * jax.random.normal(seeds[17], (D,), jnp.float32), 0.5, 1.5),
        "gu_weight": normal_values(seeds[18], (D, 2, FF), D ** -0.5, 0.1875, ((2, 4),)),
        "down_weight": normal_values(seeds[19], (FF, D), FF ** -0.5, 0.125, ((0, 4),)),
    }


epsilon = 1e-05
rope_base = 10000.0
highest = lax.Precision.HIGHEST

@jax.custom_vjp
def low(v):
    return lax.optimization_barrier(v.astype(jnp.bfloat16)).astype(jnp.float32)

@jax.custom_vjp
def low_back(v):
    return v

def low_keep(v):
    return (low(v), None)

def low_pass(kept, grad):
    return (grad,)

def back_keep(v):
    return (v, None)

def back_low(kept, grad):
    return (low(grad),)
low.defvjp(low_keep, low_pass)
low_back.defvjp(back_keep, back_low)

def matmul(left, right):
    return jnp.dot(left, right, precision=highest, preferred_element_type=jnp.float32)

def causal_conv(values, kernel, positions):
    length = values.shape[0]
    taps_count = kernel.shape[0] - 1
    result_sum = kernel[taps_count][None, :] + kernel[0][None, :] * values
    for offset in range(1, taps_count):
        shifted = jnp.pad(values, ((offset, 0), (0, 0)))[:length]
        within = (positions >= offset).astype(values.dtype)[:, None]
        result_sum = result_sum + kernel[offset][None, :] * shifted * within
    return result_sum

def state_scan(inputs, rates, b_matrix, c_matrix, segment, block):
    length, head_count, head_size = inputs.shape
    state_size = b_matrix.shape[1]
    block_count = length // block
    inputs_b = inputs.reshape(block_count, block, head_count, head_size).transpose(0, 2, 1, 3)
    rates_b = rates.reshape(block_count, block, head_count).transpose(0, 2, 1)
    b_blocks = b_matrix.reshape(block_count, block, state_size)
    c_blocks = c_matrix.reshape(block_count, block, state_size)
    segments = segment.reshape(block_count, block)
    cumulative = jnp.cumsum(rates_b, axis=2)
    previous = jnp.concatenate([jnp.full((1,), -1, jnp.int32), segments[:-1, -1]])
    row_index = lax.broadcasted_iota(jnp.int32, (block, block), 0)
    col_index = lax.broadcasted_iota(jnp.int32, (block, block), 1)
    inside = ((row_index >= col_index)[None] & (segments[:, :, None] == segments[:, None, :]))[:, None]
    difference = cumulative[:, :, :, None] - cumulative[:, :, None, :]
    decay_mask = jnp.where(inside, jnp.exp(jnp.where(inside, difference, 0.0)), 0.0)
    gram_matrix = jnp.einsum('cin,cjn->cij', c_blocks, b_blocks, precision=highest)
    intra_part = jnp.einsum('chij,chjp->chip', gram_matrix[:, None] * decay_mask, inputs_b, precision=highest)
    last_sum = cumulative[:, :, -1:]
    to_end = jnp.where((segments == segments[:, -1:])[:, None, :], jnp.exp(last_sum - cumulative), 0.0)
    local_state = jnp.einsum('chj,cjn,chjp->chnp', to_end, b_blocks, inputs_b, precision=highest)
    carry_decay = jnp.where((segments[:, -1] == previous)[:, None], jnp.exp(last_sum[:, :, 0]), 0.0)

    def advance(state_now, item_pair):
        decay_now, added_state = item_pair
        return (decay_now[:, None, None] * state_now + added_state, state_now)
    empty_state = jnp.zeros((head_count, state_size, head_size), inputs.dtype)
    _, start_states = lax.scan(advance, empty_state, (carry_decay, local_state))
    read_decay = jnp.where((segments == previous[:, None])[:, None, :], jnp.exp(cumulative), 0.0)
    inter_part = jnp.einsum('cin,chnp->chip', c_blocks, start_states, precision=highest) * read_decay[..., None]
    return (intra_part + inter_part).transpose(0, 2, 1, 3).reshape(length, head_count, head_size)

def mamba_inner(proj_zx, proj_bc, proj_dt, kernel, decay_log, dt_bias, skip_gain, positions, segment):
    length = proj_zx.shape[0]
    inner_cols = proj_zx.shape[2]
    head_count = proj_dt.shape[1]
    head_size = inner_cols // head_count
    state_size = proj_bc.shape[1] // 2
    activated = jax.nn.silu(causal_conv(jnp.concatenate([proj_zx[:, 1], proj_bc], axis=1), kernel, positions))
    x_part = activated[:, :inner_cols]
    b_matrix = activated[:, inner_cols:inner_cols + state_size]
    c_matrix = activated[:, inner_cols + state_size:]
    step_size = jax.nn.softplus(proj_dt + dt_bias[None, :])
    rates = -jnp.exp(decay_log)[None, :] * step_size
    x_heads = x_part.reshape(length, head_count, head_size)
    y_heads = state_scan(x_heads * step_size[:, :, None], rates, b_matrix, c_matrix, segment, BLK)
    y_heads = y_heads + skip_gain[None, :, None] * x_heads
    return y_heads.reshape(length, inner_cols) * jax.nn.silu(proj_zx[:, 0])

def rotate(vectors, positions, direction):
    half_size = vectors.shape[-1] // 2
    frequency = rope_base ** (-jnp.arange(half_size, dtype=jnp.float32) / half_size)
    angles = positions.astype(jnp.float32)[:, None] * frequency[None, :]
    cosine = jnp.cos(angles)[:, None, :]
    sine = jnp.sin(angles)[:, None, :]
    first_half = vectors[..., :half_size]
    second_half = vectors[..., half_size:]
    return jnp.concatenate([first_half * cosine - direction * second_half * sine, second_half * cosine + direction * first_half * sine], axis=-1)

def attend_group(query, key_value, positions, segment):
    length = query.shape[0]
    q_rot = low(rotate(query, positions, 1.0))
    k_rot = low(rotate(key_value[:, 0][:, None, :], positions, 1.0))[:, 0]
    values = low(key_value[:, 1])
    row_index = lax.broadcasted_iota(jnp.int32, (length, length), 0)
    col_index = lax.broadcasted_iota(jnp.int32, (length, length), 1)
    allowed = (col_index <= row_index) & (segment[:, None] == segment[None, :])
    scores = low_back(jnp.einsum('thd,sd->hts', q_rot, k_rot, precision=highest) * HD ** (-0.5))
    probability = low(jax.nn.softmax(jnp.where(allowed[None], scores, -1e+30), axis=-1))
    return jnp.einsum('hts,sd->thd', probability, values, precision=highest)

def rms_scale(values):
    return lax.rsqrt(lax.optimization_barrier(jnp.mean(values * values, axis=-1, keepdims=True)) + epsilon)

def layer_seq(params, inputs, positions):
    norm_one, zx_weight, bc_weight, dt_weight, conv_inner, conv_state, decay_log, dt_bias, skip_gain, gated_gain, out_weight, q_weight, kv_weight, o_weight, norm_two, gu_weight, down_weight = params
    length = inputs.shape[0]
    segment = jnp.cumsum((positions == 0).astype(jnp.int32), dtype=jnp.int32)
    normed = low(inputs * rms_scale(inputs) * norm_one)
    inner_cols = zx_weight.shape[2] // N_TENSOR
    head_cols = dt_weight.shape[1] // N_TENSOR
    query_cols = q_weight.shape[1] // N_TENSOR
    group_q = query_cols // HD
    per_kv = QH // KVH
    gated_pieces = []
    attn_pieces = []
    for group in range(N_TENSOR):
        inner_slice = slice(group * inner_cols, (group + 1) * inner_cols)
        head_slice = slice(group * head_cols, (group + 1) * head_cols)
        proj_zx = low_back(jnp.einsum('td,dkc->tkc', normed, zx_weight[:, :, inner_slice], precision=highest))
        proj_bc = low_back(matmul(normed, bc_weight))
        proj_dt = low_back(matmul(normed, dt_weight[:, head_slice]))
        kernel = jnp.concatenate([conv_inner[:, inner_slice], conv_state], axis=1)
        gated_pieces.append(mamba_inner(proj_zx, proj_bc, proj_dt, kernel, decay_log[head_slice], dt_bias[head_slice], skip_gain[head_slice], positions, segment))
        kv_head = group * group_q // per_kv
        query = low_back(matmul(normed, q_weight[:, group * query_cols:(group + 1) * query_cols]))
        key_value = low_back(jnp.einsum('td,dkc->tkc', normed, kv_weight[:, :, kv_head * HD:(kv_head + 1) * HD], precision=highest))
        attn_pieces.append(attend_group(query.reshape(length, group_q, HD), key_value, positions, segment))
    gated = jnp.concatenate(gated_pieces, axis=1)
    gate_normed = low(gated * rms_scale(gated) * gated_gain)
    attn = low(low_back(jnp.concatenate(attn_pieces, axis=1).reshape(length, -1)))
    mixer_term = low_back(matmul(gate_normed, out_weight) + matmul(attn, o_weight))
    resid = inputs + mixer_term
    normed_two = low(resid * rms_scale(resid) * norm_two)
    gate_up = low_back(jnp.einsum('td,dkf->tkf', normed_two, gu_weight, precision=highest))
    act = low(jax.nn.silu(gate_up[:, 0]) * gate_up[:, 1])
    return resid + matmul(act, down_weight)

def reference(hidden, positions, out_grad, norm_one, zx_weight, bc_weight, dt_weight, conv_inner, conv_state, decay_log, dt_bias, skip_gain, gated_gain, out_weight, q_weight, kv_weight, o_weight, norm_two, gu_weight, down_weight):
    params = tuple((value.astype(jnp.float32) for value in (norm_one, zx_weight, bc_weight, dt_weight, conv_inner, conv_state, decay_log, dt_bias, skip_gain, gated_gain, out_weight, q_weight, kv_weight, o_weight, norm_two, gu_weight, down_weight)))
    seq_inputs = hidden.astype(jnp.float32).reshape(-1, TOK_DEV, D)
    seq_positions = positions.reshape(-1, TOK_DEV)

    def whole_layer(weights, layer_inputs):
        one_sequence = jax.checkpoint(lambda item_pair: layer_seq(weights, item_pair[0], item_pair[1]))
        return lax.map(one_sequence, (layer_inputs, seq_positions))
    layer_values, pullback = jax.vjp(whole_layer, params, seq_inputs)
    weight_grads, input_cot = pullback(out_grad.astype(jnp.float32).reshape(seq_inputs.shape))
    return (layer_values.reshape(-1, D).astype(jnp.bfloat16), input_cot.reshape(-1, D).astype(jnp.bfloat16), weight_grads[0], weight_grads[1], weight_grads[2], weight_grads[3], weight_grads[4], weight_grads[5], weight_grads[6], weight_grads[7], weight_grads[8], weight_grads[9], weight_grads[10], weight_grads[11], weight_grads[12], weight_grads[13], weight_grads[14], weight_grads[15], weight_grads[16])
```

```python
import functools

import jax
import jax.numpy as jnp
from jax import lax
from jax.experimental import pallas as pl
from jax.experimental.pallas import tpu as pltpu
from jax.sharding import PartitionSpec as P

QH = 8
KVH = 2
HD = 64
HEAD_PAD = 8

epsilon = 1e-05
rope_base = 10000.0
highest = lax.Precision.HIGHEST
bf16 = jnp.bfloat16
f32 = jnp.float32
params = pltpu.CompilerParams(vmem_limit_bytes=48 * 1024 * 1024)


def dot(left, right, dims, precision=None):
    return lax.dot_general(
        left,
        right,
        ((dims[:1], dims[1:]), ((), ())),
        precision=precision,
        preferred_element_type=f32,
    )


def rms_scale(values):
    return lax.rsqrt(jnp.mean(values * values, axis=-1, keepdims=True) + epsilon)


def sigmoid(values):
    return 1.0 / (1.0 + jnp.exp(-values))


def rounded(values):
    return values.astype(bf16).astype(f32)


def cost(flops, read, exps=0):
    return pl.CostEstimate(flops=flops, bytes_accessed=read, transcendentals=exps)


def swap(values, axis, mask):
    pairs = [(index, index ^ mask) for index in range(lax.axis_size(axis))]
    return lax.ppermute(values, axis, pairs)


def sum_tensor_small(values):
    near = values + swap(values, "tensor", 1)
    return near + swap(near, "tensor", 2)


def sum_tensor_rows(product, tokens):
    half = tokens // 2
    core = lax.axis_index("tensor") % 2
    other = product((1 - core) * half, half)
    received = swap(other, "tensor", 1)
    mine = product(core * half, half) + received
    mine = mine + swap(mine, "tensor", 2)
    other = swap(mine, "tensor", 1)
    first = jnp.where(core == 0, mine, other)
    second = jnp.where(core == 0, other, mine)
    return jnp.concatenate([first, second], axis=0)


def rows(values, start, size):
    return lax.dynamic_slice_in_dim(values, start, size, 0)


def sum_dp(values):
    bit = 1
    while bit < lax.axis_size("dp"):
        values = values + swap(values, "dp", bit)
        bit *= 2
    return values


def share_columns(values):
    me = lax.axis_index("tensor")
    width = values.shape[1] // 4

    def block(offset):
        return lax.dynamic_slice_in_dim(values, (me ^ offset) * width, width, 1)

    near = swap(jnp.concatenate([block(1), block(3)], axis=1), "tensor", 1)
    far = swap(block(2) + near[:, width:], "tensor", 2)
    return block(0) + near[:, :width] + far


def gather_columns(values):
    me = lax.axis_index("tensor")
    near = jnp.stack([values, swap(values, "tensor", 1)])
    far = swap(near, "tensor", 2)
    stacked = jnp.concatenate([near, far], axis=0)
    return [
        lax.dynamic_index_in_dim(stacked, me ^ block, 0, keepdims=False) for block in range(4)
    ]


def halving_order(size):
    order, bits, bit = [0], [], 2
    while bit < size:
        bits.append(bit)
        bit *= 2
    for bit in reversed(bits):
        order = [index ^ bit for index in order] + order
    return order, bits


def pick_blocks(values, offsets):
    width = values.shape[1] // lax.axis_size("dp")
    me = lax.axis_index("dp")
    return jnp.concatenate(
        [
            lax.dynamic_slice_in_dim(values, (me ^ offset) * width, width, 1)
            for offset in offsets
        ],
        axis=1,
    )


def own_blocks(values):
    order, _ = halving_order(lax.axis_size("dp"))
    return pick_blocks(values, order)


def partner_blocks(values):
    order, _ = halving_order(lax.axis_size("dp"))
    return pick_blocks(values, [index ^ 1 for index in order]).astype(f32)


def pair_product_kernel(spans, blocks_first, *refs):
    groups = (len(refs) - 1 - sum(len(span[2]) for span in spans)) // 4
    out_ref = refs[-1]
    low, high, starts = spans[0]
    total = None
    for block_ref, side_ref in ((refs[0], refs[2]), (refs[1], refs[3])):
        block = block_ref[:, low:high].astype(bf16)
        side = side_ref[...].astype(bf16)
        if blocks_first:
            term = dot(block, side, (0, 0))
        else:
            term = dot(side, block, (0, 0))
        total = term if total is None else total + term
    for start, ref in zip(starts, refs[4:-1]):
        if blocks_first:
            total = total + ref[low - start : high - start, :]
        else:
            total = total + ref[:, low - start : high - start]
    out_ref[...] = total


def pair_product(blocks, sides, low, high, received, blocks_first):
    width = high - low
    side_cols = sides[0].shape[1]
    tokens = sides[0].shape[0]
    whole = blocks[0].shape[1]
    if low % 128 or high % 128 or any(start % 128 for start, _ in received):
        blocks = [block[:, low:high] for block in blocks]
        cut = []
        for start, values in received:
            if blocks_first:
                values = values[low - start : high - start]
            else:
                values = values[:, low - start : high - start]
            cut.append((0, values))
        received, low, high, whole = cut, 0, width, width
    chunk = side_cols // 2 if side_cols % 256 == 0 else side_cols
    shape = (width, side_cols) if blocks_first else (side_cols, width)
    block_spec = pl.BlockSpec((tokens, whole), lambda step: (0, 0))
    side_spec = pl.BlockSpec((tokens, chunk), lambda step: (0, step))
    if blocks_first:
        place = lambda step: (0, step)
        out_spec = pl.BlockSpec((width, chunk), place)
        adds = [pl.BlockSpec((values.shape[0], chunk), place) for _, values in received]
    else:
        place = lambda step: (step, 0)
        out_spec = pl.BlockSpec((chunk, width), place)
        adds = [pl.BlockSpec((chunk, values.shape[1]), place) for _, values in received]
    starts = tuple(start for start, _ in received)
    return pl.pallas_call(
        functools.partial(pair_product_kernel, ((low, high, starts),), blocks_first),
        grid=(side_cols // chunk,),
        in_specs=[block_spec, block_spec, side_spec, side_spec] + adds,
        out_specs=out_spec,
        out_shape=jax.ShapeDtypeStruct(shape, f32),
        compiler_params=params,
        cost_estimate=cost(4 * tokens * width * side_cols, 6 * tokens * side_cols),
        name="pair_product",
    )(*blocks, *sides, *[values for _, values in received])


def halving(blocks, sides, blocks_first):
    order, bits = halving_order(lax.axis_size("dp"))
    width = blocks[0].shape[1] // len(order)
    low, high = 0, len(order)
    received = []
    for bit in bits:
        middle = (low + high) // 2
        sent = pair_product(blocks, sides, low * width, middle * width, received, blocks_first)
        received.append((middle * width, swap(sent, "dp", bit)))
        low = middle
    return pair_product(blocks, sides, low * width, high * width, received, blocks_first)


def conv_values(values, taps, positions):
    total = taps[4:5] + taps[0:1] * values
    for offset in range(1, 4):
        shifted = pltpu.roll(values, offset, 0)
        total = total + taps[offset : offset + 1] * jnp.where(positions >= offset, shifted, 0.0)
    return total


def conv_back(grad, values, taps, positions):
    total = taps[0:1] * grad
    tap_grads = [jnp.sum(grad * values, axis=0, keepdims=True)]
    for offset in range(1, 4):
        masked = jnp.where(positions >= offset, grad, 0.0)
        shifted = pltpu.roll(masked, masked.shape[0] - offset, 0)
        total = total + taps[offset : offset + 1] * shifted
        tap_grads.append(jnp.sum(shifted * values, axis=0, keepdims=True))
    tap_grads.append(jnp.sum(grad, axis=0, keepdims=True))
    return total, tap_grads


def scan_parts(step_in, decay_row, bias_row):
    raw = step_in + bias_row
    step = jnp.maximum(raw, 0.0) + jnp.log(1.0 + jnp.exp(-jnp.abs(raw)))
    rates = -jnp.exp(decay_row) * step
    length = rates.shape[0]
    row = lax.broadcasted_iota(jnp.int32, (length, length), 0)
    col = lax.broadcasted_iota(jnp.int32, (length, length), 1)
    lower = (row >= col).astype(f32)
    upper = (row <= col).astype(f32)
    cumulative = dot(lower, rates, (1, 0), highest)
    cumulative_t = dot(rates, upper, (0, 0), highest)
    return raw, step, rates, cumulative, cumulative_t, row >= col, upper


def scan_forward_kernel(
    zx_ref, bc_ref, dt_ref, taps_x_ref, taps_bc_ref, heads_ref, pos_ref, seg_col_ref, seg_row_ref,
    y_ref, gated_ref, square_ref, xa_ref, ba_ref,
):
    positions = pos_ref[...]
    conv_x = conv_values(zx_ref[1], taps_x_ref[...], positions)
    x_act = conv_x * sigmoid(conv_x)
    conv_bc = conv_values(bc_ref[...], taps_bc_ref[...], positions)
    bc_act = (conv_bc * sigmoid(conv_bc)).astype(bf16)
    state = bc_act.shape[1] // 2
    xa_ref[...] = x_act
    ba_ref[...] = bc_act
    heads = heads_ref[...]
    _, step, _, cumulative, cumulative_t, causal, _ = scan_parts(
        dt_ref[...], heads[0:1], heads[1:2]
    )
    inside = causal & (seg_col_ref[...] == seg_row_ref[...])
    gram = dot(bc_act[:, state:], bc_act[:, :state], (1, 1))
    length = positions.shape[0]
    lane = lax.broadcasted_iota(jnp.int32, (length, 128), 1)
    low_half = lane < 64
    square = jnp.zeros((length, 1), f32)
    for pair in range(x_act.shape[1] // 128):
        cols = slice(pair * 128, pair * 128 + 128)
        first, second = 2 * pair, 2 * pair + 1
        x_pair = x_act[:, cols]
        dt_pair = jnp.where(low_half, step[:, first : first + 1], step[:, second : second + 1])
        scaled = x_pair * dt_pair
        total = jnp.where(
            low_half, heads[2:3, first : first + 1], heads[2:3, second : second + 1]
        ) * x_pair
        for head, keep in ((first, low_half), (second, ~low_half)):
            gap = cumulative[:, head : head + 1] - cumulative_t[head : head + 1, :]
            mixing = gram * jnp.exp(jnp.where(inside, gap, -1e30))
            total = total + dot(
                mixing.astype(bf16), jnp.where(keep, scaled, 0.0).astype(bf16), (1, 0)
            )
        z_pair = zx_ref[0, :, cols]
        gated = total * (z_pair * sigmoid(z_pair))
        y_ref[:, cols] = total
        gated_ref[:, cols] = gated
        square = square + jnp.sum(gated * gated, axis=1, keepdims=True)
    square_ref[...] = square


def scan_forward(zx, bc, dt, taps_x, taps_bc, heads, pos, seg_col, seg_row):
    tokens, inner = zx.shape[1:]
    return pl.pallas_call(
        scan_forward_kernel,
        out_shape=[
            jax.ShapeDtypeStruct((tokens, inner), f32),
            jax.ShapeDtypeStruct((tokens, inner), f32),
            jax.ShapeDtypeStruct((tokens, 1), f32),
            jax.ShapeDtypeStruct((tokens, inner), f32),
            jax.ShapeDtypeStruct(bc.shape, bf16),
        ],
        compiler_params=params,
        cost_estimate=cost(10**9, 4 * 10**6, 10**6),
        name="scan_forward",
    )(zx, bc, dt, taps_x, taps_bc, heads, pos, seg_col, seg_row)


def scan_backward_kernel(
    zx_ref, bc_ref, dt_ref, taps_x_ref, taps_bc_ref, heads_ref, pos_ref, seg_col_ref, seg_row_ref,
    y_ref, xa_ref, ba_ref, up_ref, scale_ref, cross_ref, gain_ref,
    z_cot_ref, x_cot_ref, bc_cot_ref, dt_cot_ref, taps_x_out, taps_bc_out, heads_out, gain_out,
    conv_x_grad,
):
    positions = pos_ref[...]
    length = positions.shape[0]
    bc_act = ba_ref[...]
    state = bc_act.shape[1] // 2
    heads = heads_ref[...]
    raw, step, rates, cumulative, cumulative_t, causal, upper = scan_parts(
        dt_ref[...], heads[0:1], heads[1:2]
    )
    inside = causal & (seg_col_ref[...] == seg_row_ref[...])
    gram = dot(bc_act[:, state:], bc_act[:, :state], (1, 1))
    lane = lax.broadcasted_iota(jnp.int32, (length, 128), 1)
    low_half = lane < 64
    scale = scale_ref[...]
    pull = scale * scale * scale * cross_ref[...]
    gram_grad = jnp.zeros((length, length), f32)
    head_lane = lax.broadcasted_iota(jnp.int32, (length, HEAD_PAD), 1)
    head_row = lax.broadcasted_iota(jnp.int32, (HEAD_PAD, length), 0)
    head_one = lax.broadcasted_iota(jnp.int32, (1, HEAD_PAD), 1)
    step_grad = jnp.zeros((length, HEAD_PAD), f32)
    row_sums = jnp.zeros((length, HEAD_PAD), f32)
    col_sums = jnp.zeros((HEAD_PAD, length), f32)
    skip_grad = jnp.zeros((1, HEAD_PAD), f32)
    for pair in range(y_ref.shape[1] // 128):
        cols = slice(pair * 128, pair * 128 + 128)
        first, second = 2 * pair, 2 * pair + 1
        z_pair = zx_ref[0, :, cols]
        y_pair = y_ref[:, cols]
        gate = sigmoid(z_pair)
        silu = z_pair * gate
        gated = y_pair * silu
        up = up_ref[:, cols]
        gain_out[:, cols] = jnp.sum(up * gated * scale, axis=0, keepdims=True)
        gated_grad = scale * (up * gain_ref[:, cols]) - gated * pull
        z_cot_ref[:, cols] = rounded(gated_grad * y_pair * (gate * (1.0 + z_pair * (1.0 - gate))))
        y_grad = gated_grad * silu
        x_pair = xa_ref[:, cols]
        dt_pair = jnp.where(low_half, step[:, first : first + 1], step[:, second : second + 1])
        skip_pair = jnp.where(
            low_half, heads[2:3, first : first + 1], heads[2:3, second : second + 1]
        )
        scaled = (x_pair * dt_pair).astype(bf16)
        scaled_grad = jnp.zeros((length, 128), f32)
        skip_product = y_grad * x_pair
        for head, keep in ((first, low_half), (second, ~low_half)):
            gap = cumulative[:, head : head + 1] - cumulative_t[head : head + 1, :]
            decay = jnp.exp(jnp.where(inside, gap, -1e30))
            mixing = gram * decay
            y_head = jnp.where(keep, y_grad, 0.0).astype(bf16)
            mixing_grad = dot(y_head, scaled, (1, 1))
            scaled_grad = scaled_grad + dot(mixing.astype(bf16), y_head, (0, 0))
            gram_grad = gram_grad + mixing_grad * decay
            moved = mixing_grad * mixing
            row_sums = row_sums + jnp.where(
                head_lane == head, jnp.sum(moved, axis=1, keepdims=True), 0.0
            )
            col_sums = col_sums + jnp.where(
                head_row == head, jnp.sum(moved, axis=0, keepdims=True), 0.0
            )
        step_product = scaled_grad * x_pair
        for head, keep in ((first, low_half), (second, ~low_half)):
            step_grad = step_grad + jnp.where(
                head_lane == head,
                jnp.sum(jnp.where(keep, step_product, 0.0), axis=1, keepdims=True),
                0.0,
            )
            skip_sum = jnp.sum(
                jnp.sum(jnp.where(keep, skip_product, 0.0), axis=0, keepdims=True),
                axis=1,
                keepdims=True,
            )
            skip_grad = skip_grad + jnp.where(head_one == head, skip_sum, 0.0)
        x_grad = scaled_grad * dt_pair + skip_pair * y_grad
        conv_x = conv_values(zx_ref[1, :, cols], taps_x_ref[:, cols], positions)
        gate = sigmoid(conv_x)
        conv_grad = x_grad * (gate * (1.0 + conv_x * (1.0 - gate)))
        total, tap_grads = conv_back(
            conv_grad, zx_ref[1, :, cols], taps_x_ref[:, cols], positions
        )
        x_cot_ref[:, cols] = rounded(total)
        for index, value in enumerate(tap_grads):
            taps_x_out[index : index + 1, cols] = value
    rate_grad = dot(upper, row_sums, (1, 0), highest) - dot(upper, col_sums, (1, 1), highest)
    step_grad = step_grad - rate_grad * jnp.exp(heads[0:1])
    raw_grad = step_grad * sigmoid(raw)
    dt_cot_ref[...] = rounded(raw_grad)
    heads_out[0:1, :] = jnp.sum(rate_grad * rates, axis=0, keepdims=True)
    heads_out[1:2, :] = jnp.sum(raw_grad, axis=0, keepdims=True)
    heads_out[2:3, :] = skip_grad
    gram_low = gram_grad.astype(bf16)
    b_grad = dot(gram_low, bc_act[:, state:], (0, 0))
    c_grad = dot(gram_low, bc_act[:, :state], (1, 0))
    for part, grad in enumerate((b_grad, c_grad)):
        cols = slice(part * state, part * state + state)
        conv = conv_values(bc_ref[:, cols], taps_bc_ref[:, cols], positions)
        gate = sigmoid(conv)
        conv_grad = grad * (gate * (1.0 + conv * (1.0 - gate)))
        total, tap_grads = conv_back(conv_grad, bc_ref[:, cols], taps_bc_ref[:, cols], positions)
        bc_cot_ref[:, cols] = rounded(total)
        for index, value in enumerate(tap_grads):
            taps_bc_out[index : index + 1, cols] = value


def scan_backward(
    zx, bc, dt, taps_x, taps_bc, heads, pos, seg_col, seg_row, y, xa, ba, up, scale, cross, gain
):
    tokens, inner = zx.shape[1:]
    return pl.pallas_call(
        scan_backward_kernel,
        out_shape=[
            jax.ShapeDtypeStruct((tokens, inner), f32),
            jax.ShapeDtypeStruct((tokens, inner), f32),
            jax.ShapeDtypeStruct(bc.shape, f32),
            jax.ShapeDtypeStruct(dt.shape, f32),
            jax.ShapeDtypeStruct(taps_x.shape, f32),
            jax.ShapeDtypeStruct(taps_bc.shape, f32),
            jax.ShapeDtypeStruct((3, HEAD_PAD), f32),
            jax.ShapeDtypeStruct((1, inner), f32),
        ],
        scratch_shapes=[pltpu.VMEM((8, 128), f32)],
        compiler_params=params,
        cost_estimate=cost(3 * 10**9, 8 * 10**6, 10**6),
        name="scan_backward",
    )(zx, bc, dt, taps_x, taps_bc, heads, pos, seg_col, seg_row, y, xa, ba, up, scale, cross, gain)


def turn(values, cosine, sine, low_quarter):
    width = values.shape[1]
    partner = jnp.where(
        low_quarter, pltpu.roll(values, width - HD // 2, 1), pltpu.roll(values, HD // 2, 1)
    )
    return values * cosine + partner * sine


def masked_scores(q_head, kv, allowed):
    scores = dot(q_head, kv, (1, 1)) * HD ** (-0.5)
    return jnp.where(allowed, scores, -1e30)


def softmax(scores):
    exponent = jnp.exp(scores - jnp.max(scores, axis=1, keepdims=True))
    return exponent * (1.0 / jnp.sum(exponent, axis=1, keepdims=True))


def attention_masks(length, seg_col_ref, seg_row_ref):
    row = lax.broadcasted_iota(jnp.int32, (length, length), 0)
    col = lax.broadcasted_iota(jnp.int32, (length, length), 1)
    allowed = (col <= row) & (seg_col_ref[...] == seg_row_ref[...])
    lane = lax.broadcasted_iota(jnp.int32, (length, 2 * HD), 1)
    return allowed, lane < HD, (lane % HD) < HD // 2


def to_low(values, head):
    return values if head == 0 else pltpu.roll(values, HD, 1)


def to_high(values, head):
    return values if head == 1 else pltpu.roll(values, HD, 1)


def attention_forward_kernel(
    q_ref, kv_ref, cos_ref, sin_ref, seg_col_ref, seg_row_ref, q_out, kv_out, attn_out
):
    length = q_ref.shape[0]
    allowed, low_half, low_quarter = attention_masks(length, seg_col_ref, seg_row_ref)
    cosine, sine = cos_ref[...], sin_ref[...]
    q_rot = rounded(turn(q_ref[...], cosine, sine, low_quarter))
    kv_in = kv_ref[...]
    kv = jnp.where(low_half, turn(kv_in, cosine, sine, low_quarter), kv_in).astype(bf16)
    q_out[...] = q_rot
    kv_out[...] = kv
    parts = []
    for head in range(2):
        q_head = jnp.where(low_half, to_low(q_rot, head), 0.0).astype(bf16)
        probability = softmax(masked_scores(q_head, kv, allowed)).astype(bf16)
        parts.append(dot(probability, kv, (1, 0)))
    attn_out[...] = rounded(jnp.where(low_half, pltpu.roll(parts[0], HD, 1), parts[1]))


def attention_forward(q, kv, cosine, sine, seg_col, seg_row):
    return pl.pallas_call(
        attention_forward_kernel,
        out_shape=[
            jax.ShapeDtypeStruct(q.shape, f32),
            jax.ShapeDtypeStruct(q.shape, bf16),
            jax.ShapeDtypeStruct(q.shape, f32),
        ],
        compiler_params=params,
        cost_estimate=cost(5 * 10**8, 10**6, 10**5),
        name="attention_forward",
    )(q, kv, cosine, sine, seg_col, seg_row)


def attention_backward_kernel(
    q_ref, kv_ref, grad_ref, cos_ref, sin_ref, seg_col_ref, seg_row_ref, q_cot, kv_cot
):
    length = q_ref.shape[0]
    allowed, low_half, low_quarter = attention_masks(length, seg_col_ref, seg_row_ref)
    cosine, sine = cos_ref[...], -sin_ref[...]
    q_rot, kv = q_ref[...], kv_ref[...]
    grad = rounded(grad_ref[...])
    parts = []
    kv_grad = jnp.zeros((length, 2 * HD), f32)
    for head in range(2):
        q_head = jnp.where(low_half, to_low(q_rot, head), 0.0)
        probability = softmax(masked_scores(q_head.astype(bf16), kv, allowed))
        g_head = jnp.where(low_half, 0.0, to_high(grad, head)).astype(bf16)
        prob_grad = dot(g_head, kv, (1, 1))
        inner = jnp.sum(probability * prob_grad, axis=1, keepdims=True)
        score_grad = (probability * (prob_grad - inner)).astype(bf16)
        parts.append(dot(score_grad, kv, (1, 0)) * HD ** (-0.5))
        kv_grad = kv_grad + dot(score_grad, (q_head * HD ** (-0.5)).astype(bf16), (0, 0))
        kv_grad = kv_grad + dot(probability.astype(bf16), g_head, (0, 0))
    q_grad = jnp.where(low_half, parts[0], pltpu.roll(parts[1], HD, 1))
    q_cot[...] = rounded(turn(q_grad, cosine, sine, low_quarter))
    kv_cot[...] = rounded(
        jnp.where(low_half, turn(kv_grad, cosine, sine, low_quarter), kv_grad)
    )


def attention_backward(q, kv, grad, cosine, sine, seg_col, seg_row):
    return pl.pallas_call(
        attention_backward_kernel,
        out_shape=[jax.ShapeDtypeStruct(q.shape, f32), jax.ShapeDtypeStruct(q.shape, f32)],
        compiler_params=params,
        cost_estimate=cost(10**9, 10**6, 10**5),
        name="attention_backward",
    )(q, kv, grad, cosine, sine, seg_col, seg_row)


def rotary_tables(positions):
    half = HD // 2
    frequency = rope_base ** (-jnp.arange(half, dtype=f32) / half)
    angles = positions.astype(f32)[:, None] * frequency[None, :]
    cosine, sine = jnp.cos(angles), jnp.sin(angles)
    return (
        jnp.concatenate([cosine] * 4, axis=1),
        jnp.concatenate([-sine, sine, -sine, sine], axis=1),
    )


def on_device(
    hidden,
    positions,
    out_grad,
    norm_one,
    zx_weight,
    bc_weight,
    dt_weight,
    conv_inner,
    conv_state,
    decay_log,
    dt_bias,
    skip_gain,
    gated_gain,
    out_weight,
    q_weight,
    kv_weight,
    o_weight,
    norm_two,
    gu_weight,
    down_weight,
):
    tokens, model = hidden.shape
    head_count = dt_weight.shape[1]
    inner_cols = conv_inner.shape[1]
    hidden_cols = gu_weight.shape[2]
    query_cols = q_weight.shape[1]
    inner_width = inner_cols * lax.axis_size("tensor")
    segment = jnp.cumsum((positions == 0).astype(jnp.int32), dtype=jnp.int32)
    seg_col, seg_row, pos_col = segment[:, None], segment[None, :], positions[:, None]
    cosine, sine = rotary_tables(positions)
    head_pad = ((0, 0), (0, HEAD_PAD - head_count))
    heads = jnp.pad(jnp.stack([decay_log, dt_bias, skip_gain]), head_pad)
    dt_wide = jnp.pad(dt_weight, head_pad)

    inputs = hidden.astype(f32)
    scale_one = rms_scale(inputs)
    normed_f = inputs * scale_one * norm_one
    normed = normed_f.astype(bf16)
    first_sent = jnp.concatenate(
        [partner_blocks(normed), partner_blocks(out_grad)], axis=1
    )
    first_got = swap(first_sent, "dp", 1)
    half_model = model // 2
    normed_pair = (own_blocks(normed), first_got[:, :half_model])
    out_pair = (own_blocks(out_grad), first_got[:, half_model:])

    proj_zx = jnp.einsum("td,dkc->ktc", normed, zx_weight, preferred_element_type=f32)
    proj_bc = dot(normed, bc_weight, (1, 0))
    proj_dt = dot(normed, dt_wide, (1, 0))
    scan_args = (
        proj_zx, proj_bc, proj_dt, conv_inner, conv_state, heads, pos_col, seg_col, seg_row
    )
    y, gated, square, x_act, bc_act = scan_forward(*scan_args)
    square_sum = sum_tensor_small(square)

    kv_head = lax.axis_index("tensor") * (query_cols // HD) // (QH // KVH)
    kv_slice = lax.dynamic_slice_in_dim(kv_weight, kv_head * HD, HD, 2).reshape(model, 2 * HD)
    query = dot(normed, q_weight, (1, 0))
    key_value = dot(normed, kv_slice, (1, 0))
    q_rot, kv_rot, attn = attention_forward(query, key_value, cosine, sine, seg_col, seg_row)
    attn_b = attn.astype(bf16)

    gate_scale = lax.rsqrt(square_sum / inner_width + epsilon)
    gate_normed = (gated * gate_scale * gated_gain).astype(bf16)
    mixed_own = jnp.concatenate([gate_normed.astype(f32), attn], axis=1)
    mixed_got = swap(mixed_own, "dp", 1)
    gate_pair = (gate_normed, mixed_got[:, :inner_cols])
    attn_pair = (attn, mixed_got[:, inner_cols:])

    def mix_rows(start, size):
        return dot(rows(gate_normed, start, size), out_weight, (1, 0)) + dot(
            rows(attn_b, start, size), o_weight, (1, 0)
        )

    resid = inputs + sum_tensor_rows(mix_rows, tokens)
    scale_two = rms_scale(resid)
    normed_two = (resid * scale_two * norm_two).astype(bf16)
    gate_up = jnp.einsum("td,dkf->ktf", normed_two, gu_weight, preferred_element_type=f32)
    act_grad = dot(out_grad, down_weight, (1, 1))
    sigmoid_gate = sigmoid(gate_up[0])
    gate_act = gate_up[0] * sigmoid_gate
    act_b = (gate_act * gate_up[1]).astype(bf16)
    gate_grad = act_grad * gate_up[1] * sigmoid_gate * (1.0 + gate_up[0] * (1.0 - sigmoid_gate))
    gu_grad_b = jnp.concatenate([gate_grad, act_grad * gate_act], axis=1).astype(bf16)
    normed_two_grad = sum_tensor_rows(
        lambda start, size: jnp.einsum(
            "tkf,dkf->td",
            rows(gu_grad_b, start, size).reshape(size, 2, hidden_cols),
            gu_weight,
            preferred_element_type=f32,
        ),
        tokens,
    )
    feed_sent = jnp.concatenate(
        [partner_blocks(normed_two), act_b.astype(f32), gu_grad_b.astype(f32)], axis=1
    )
    feed_got = swap(feed_sent, "dp", 1)
    normed_two_pair = (own_blocks(normed_two), feed_got[:, :half_model])
    act_pair = (act_b, feed_got[:, half_model : half_model + hidden_cols])
    gu_pair = (gu_grad_b, feed_got[:, half_model + hidden_cols :])
    down_shard = halving(out_pair, act_pair, False)
    gu_shard = halving(normed_two_pair, gu_pair, True).reshape(-1, 2, hidden_cols)
    mlp_total = sum_tensor_rows(
        lambda start, size: dot(rows(act_b, start, size), down_weight, (1, 0)), tokens
    )
    layer_out = (resid + mlp_total).astype(bf16)

    norm_two_grad = jnp.sum(normed_two_grad * resid * scale_two, axis=0)
    weighted_two = normed_two_grad * norm_two
    resid_grad = (
        out_grad.astype(f32)
        + scale_two * weighted_two
        - resid * scale_two**3 * jnp.mean(weighted_two * resid, axis=-1, keepdims=True)
    )
    mix_grad_b = resid_grad.astype(bf16)
    gate_normed_grad = dot(mix_grad_b, out_weight, (1, 1))
    cross = jnp.sum(gate_normed_grad * gated_gain * gated, axis=1, keepdims=True)
    cross_sum = sum_tensor_small(cross) / inner_width
    attn_grad = dot(mix_grad_b, o_weight, (1, 1))
    q_cot, kv_cot = attention_backward(q_rot, kv_rot, attn_grad, cosine, sine, seg_col, seg_row)
    mix_pair = (own_blocks(mix_grad_b), swap(partner_blocks(mix_grad_b), "dp", 1))
    out_shard = halving(mix_pair, gate_pair, False)
    o_shard = halving(mix_pair, attn_pair, False)

    z_cot, x_cot, bc_cot, dt_cot, taps_x_grad, taps_bc_grad, heads_grad, gain_grad = scan_backward(
        *scan_args, y, x_act, bc_act, gate_normed_grad, gate_scale, cross_sum, gated_gain[None, :]
    )
    zx_cot = jnp.stack([z_cot, x_cot], axis=1).astype(bf16)
    normed_grad = (
        jnp.einsum("tkc,dkc->td", zx_cot, zx_weight, preferred_element_type=f32)
        + dot(bc_cot.astype(bf16), bc_weight, (1, 1))
        + dot(dt_cot.astype(bf16), dt_wide, (1, 1))
        + dot(q_cot.astype(bf16), q_weight, (1, 1))
        + dot(kv_cot.astype(bf16), kv_slice, (1, 1))
    )
    kv_wide = lax.dynamic_update_slice_in_dim(
        jnp.zeros((tokens, 2, KVH * HD), f32), kv_cot.reshape(tokens, 2, HD), kv_head * HD, 2
    )
    shared = share_columns(jnp.concatenate([bc_cot, kv_wide.reshape(tokens, -1)], axis=1))
    shared_cols = shared.shape[1]
    dt_tail = jnp.pad(dt_cot, ((0, 0), (0, 128 - HEAD_PAD)))
    tail_own = jnp.concatenate([z_cot, x_cot, q_cot, shared, dt_tail], axis=1)
    tail = halving(normed_pair, (tail_own, swap(tail_own, "dp", 1)), True)
    edges = [0, 2 * inner_cols]
    for size in (query_cols, shared_cols, 128):
        edges.append(edges[-1] + size)
    zx_shard, q_shard, shared_shard, dt_shard = [
        tail[:, low:high] for low, high in zip(edges[:-1], edges[1:])
    ]
    zx_shard = zx_shard.reshape(-1, 2, inner_cols)
    dt_shard = dt_shard[:, :head_count]
    shared_parts = gather_columns(shared_shard)
    bc_shard = jnp.concatenate(shared_parts[:2], axis=1)
    kv_shard = jnp.stack(shared_parts[2:], axis=1)

    input_normed_grad = sum_tensor_rows(
        lambda start, size: rows(normed_grad, start, size), tokens
    )
    norm_one_grad = jnp.sum(input_normed_grad * inputs * scale_one, axis=0)
    weighted_one = input_normed_grad * norm_one
    input_grad = (
        resid_grad
        + scale_one * weighted_one
        - inputs * scale_one**3 * jnp.mean(weighted_one * inputs, axis=-1, keepdims=True)
    )
    state_part = sum_tensor_small(taps_bc_grad)
    pieces = (
        norm_one_grad,
        norm_two_grad,
        taps_x_grad.reshape(-1),
        state_part.reshape(-1),
        gain_grad.reshape(-1),
        heads_grad.reshape(-1),
    )
    packed = jnp.concatenate(pieces)
    padding = -packed.shape[0] % 1024
    packed = sum_dp(jnp.pad(packed, (0, padding)).reshape(-1, 128)).reshape(-1)
    sums, start = [], 0
    for piece in pieces:
        sums.append(packed[start : start + piece.shape[0]])
        start += piece.shape[0]
    head_sums = sums[5].reshape(3, HEAD_PAD)[:, :head_count]
    return (
        layer_out,
        input_grad.astype(bf16),
        sums[0],
        zx_shard,
        bc_shard,
        dt_shard,
        sums[2].reshape(-1, inner_cols),
        sums[3].reshape(conv_state.shape),
        head_sums[0],
        head_sums[1],
        head_sums[2],
        sums[4],
        out_shard,
        q_shard,
        kv_shard,
        o_shard,
        sums[1],
        gu_shard,
        down_shard,
    )


def solution(mesh):
    placed = (
        P("dp", None),
        P("dp"),
        P("dp", None),
        P(),
        P(None, None, "tensor"),
        P(),
        P(None, "tensor"),
        P(None, "tensor"),
        P(),
        P("tensor"),
        P("tensor"),
        P("tensor"),
        P("tensor"),
        P("tensor", None),
        P(None, "tensor"),
        P(),
        P("tensor", None),
        P(),
        P(None, None, "tensor"),
        P("tensor", None),
    )
    return jax.shard_map(
        on_device,
        mesh=mesh,
        in_specs=placed,
        out_specs=(
            P("dp", None),
            P("dp", None),
            P(),
            P("dp", None, "tensor"),
            P("dp", None),
            P("dp", "tensor"),
            P(None, "tensor"),
            P(),
            P("tensor"),
            P("tensor"),
            P("tensor"),
            P("tensor"),
            P("tensor", "dp"),
            P("dp", "tensor"),
            P("dp", None, None),
            P("tensor", "dp"),
            P(),
            P("dp", None, "tensor"),
            P("tensor", "dp"),
        ),
        check_vma=False,
    )
```

```python
import functools

import jax
import jax.numpy as jnp
from jax import lax
from jax.experimental import pallas as pl
from jax.experimental.pallas import tpu as pltpu
from jax.sharding import PartitionSpec as P

QH = 8
KVH = 2
HD = 64
HEAD_PAD = 128
STATE_ROWS = 18
STATE_PAD = 24
SMALL_ROWS = 16
COST = 1000

epsilon = 1e-05
rope_base = 10000.0
highest = lax.Precision.HIGHEST
bf16 = jnp.bfloat16
f32 = jnp.float32
params = pltpu.CompilerParams(vmem_limit_bytes=16 * 1024 * 1024)


def dot(left, right, dims, precision=None):
    return lax.dot_general(
        left,
        right,
        ((dims[:1], dims[1:]), ((), ())),
        precision=precision,
        preferred_element_type=f32,
    )


def rms_scale(values):
    return lax.rsqrt(jnp.mean(values * values, axis=-1, keepdims=True) + epsilon)


def sigmoid(values):
    return 1.0 / (1.0 + jnp.exp(-values))


def rounded(values):
    return values.astype(bf16).astype(f32)


def cost(flops, read, exps=0):
    return pl.CostEstimate(flops=COST, bytes_accessed=COST, transcendentals=0)


def swap(values, axis, mask):
    pairs = [(index, index ^ mask) for index in range(lax.axis_size(axis))]
    return lax.ppermute(values, axis, pairs)


def spread_tensor(values):
    return [values] + [swap(values, "tensor", mask) for mask in (1, 2, 3)]


def add_spread(parts):
    return (parts[0] + parts[1]) + (parts[2] + parts[3])


def add_kernel(left_ref, right_ref, *rest):
    rest[-1][...] = left_ref[...] + right_ref[...]


def tensor_halves(mine, ahead=()):
    vmem = pl.BlockSpec(memory_space=pltpu.VMEM)
    mine = pl.pallas_call(
        add_kernel,
        in_specs=[vmem] * 2 + [pl.BlockSpec(memory_space=pl.ANY)] * len(ahead),
        out_shape=jax.ShapeDtypeStruct(mine.shape, f32),
        compiler_params=params,
        cost_estimate=cost(10**6, 10**6),
        name="add_halves",
    )(mine, swap(mine, "tensor", 2), *ahead)
    return mine, swap(mine, "tensor", 1)


def swap_shared(values, mask):
    first = swap(values, "dp", mask)
    return first, swap(first, "tensor", 1)


def rows(values, start, size):
    return lax.dynamic_slice_in_dim(values, start, size, 0)


def half_rows(core, size):
    return pl.ds(pl.multiple_of(core * size, size), size)


def halving_order(size, pair):
    order, bits, bit = [0], [], 1
    while bit < size:
        if bit != pair:
            bits.append(bit)
        bit *= 2
    for bit in reversed(bits):
        order = [index ^ bit for index in order] + order
    return order, bits


def pick_blocks(values, offsets):
    width = values.shape[1] // lax.axis_size("dp")
    me = lax.axis_index("dp")
    return jnp.concatenate(
        [
            lax.dynamic_slice_in_dim(values, (me ^ offset) * width, width, 1)
            for offset in offsets
        ],
        axis=1,
    )


def arrange_kernel(order, pair, width, me_ref, *refs):
    count = len(refs) // 2
    me = me_ref[0]
    half = refs[-1].shape[0]
    span = half_rows(me_ref[1], half)
    partner_ref = refs[-1]
    for index in range(count):
        value_ref, own_ref = refs[index], refs[count + index]
        base = index * len(order) * width
        for place, offset in enumerate(order):
            cols = pl.ds(pl.multiple_of((me ^ offset) * width, 128), width)
            own_ref[:, place * width : (place + 1) * width] = value_ref[:, cols].astype(bf16)
            cols = pl.ds(pl.multiple_of((me ^ offset ^ pair) * width, 128), width)
            start = base + place * width
            partner_ref[:, start : start + width] = value_ref[span, cols].astype(f32)


def arrange(pair, *arrays):
    size = lax.axis_size("dp")
    order, _ = halving_order(size, pair)
    tokens, model = arrays[0].shape
    width = model // size
    half = len(order) * width
    if width % 128:
        partner = [index ^ pair for index in order]
        start = lax.axis_index("tensor") % 2 * (tokens // 2)
        sent = [
            rows(pick_blocks(values, partner), start, tokens // 2).astype(f32) for values in arrays
        ]
        return [pick_blocks(values, order) for values in arrays] + [
            jnp.concatenate(sent, axis=1)
        ]
    vmem = pl.BlockSpec(memory_space=pltpu.VMEM)
    me = jnp.stack([lax.axis_index("dp"), lax.axis_index("tensor") % 2]).astype(jnp.int32)
    return pl.pallas_call(
        functools.partial(arrange_kernel, order, pair, width),
        in_specs=[pl.BlockSpec(memory_space=pltpu.SMEM)] + [vmem] * len(arrays),
        out_shape=[jax.ShapeDtypeStruct((tokens, half), bf16) for _ in arrays]
        + [jax.ShapeDtypeStruct((tokens // 2, half * len(arrays)), f32)],
        compiler_params=params,
        cost_estimate=cost(10**6, 8 * tokens * model),
        name="arrange",
    )(me, *arrays)


def pair_product_kernel(low, high, starts, blocks_first, core_ref, *refs):
    own_ref, got_ref, other_ref, side_ref, side_got_ref = refs[:5]
    out_ref, joined_ref = refs[-2:]
    half = got_ref.shape[0]
    tokens = 2 * half
    core = core_ref[0]
    joined_ref[half_rows(core, half), :] = got_ref[:, low:high].astype(bf16)
    joined_ref[half_rows(1 - core, half), :] = other_ref[:, low:high].astype(bf16)
    side_cols = side_ref.shape[1]
    chunk = 384 if side_cols % 384 == 0 else 512 if side_cols % 512 == 0 else side_cols
    added = refs[5 : 5 + len(starts)]
    for at in range(0, side_cols, chunk):
        cols = slice(at, at + chunk)
        total = None
        for block, ref in ((own_ref[:, low:high], side_ref), (joined_ref[...], side_got_ref)):
            side = ref[:tokens, cols].astype(bf16)
            if blocks_first:
                term = dot(block, side, (0, 0))
            else:
                term = dot(side, block, (0, 0))
            total = term if total is None else total + term
        for start, ref in zip(starts, added):
            if blocks_first:
                total = total + ref[low - start : high - start, cols]
            else:
                total = total + ref[cols, low - start : high - start]
        if blocks_first:
            out_ref[: high - low, cols] = total
        else:
            out_ref[cols, :] = total
    if side_ref.shape[0] > tokens:
        extra = side_ref[tokens:, :] + side_got_ref[tokens:, :]
        for ref in added:
            extra = extra + ref[ref.shape[0] - extra.shape[0] :, :]
        out_ref[high - low :, :] = extra


def pair_product(blocks, sides, low, high, received, blocks_first, ahead):
    width = high - low
    rows_in, side_cols = sides[0].shape
    tokens = blocks[0].shape[0]
    extra = rows_in - tokens
    core = (lax.axis_index("tensor") % 2).astype(jnp.int32).reshape(1)
    if low % 128 or high % 128 or any(start % 128 for start, _ in received):
        blocks = [block[:, low:high] for block in blocks]
        cut = []
        for start, values in received:
            if blocks_first:
                tail = values[values.shape[0] - extra :]
                values = jnp.concatenate([values[low - start : high - start], tail], axis=0)
            else:
                values = values[:, low - start : high - start]
            cut.append((0, values))
        received, low, high = cut, 0, width
    shape = (width + extra, side_cols) if blocks_first else (side_cols, width)
    vmem = pl.BlockSpec(memory_space=pltpu.VMEM)
    starts = tuple(start for start, _ in received)
    values = (*blocks, *sides, *[value for _, value in received])
    return pl.pallas_call(
        functools.partial(pair_product_kernel, low, high, starts, blocks_first),
        in_specs=[pl.BlockSpec(memory_space=pltpu.SMEM)]
        + [vmem] * len(values)
        + [pl.BlockSpec(memory_space=pl.ANY)] * len(ahead),
        out_shape=jax.ShapeDtypeStruct(shape, f32),
        scratch_shapes=[pltpu.VMEM((tokens, width), bf16)],
        compiler_params=params,
        cost_estimate=cost(4 * tokens * width * side_cols, 6 * tokens * side_cols),
        name="pair_product",
    )(core, *values, *ahead)


def halving(blocks, sides, blocks_first, pair=1):
    order, bits = halving_order(lax.axis_size("dp"), pair)
    width = blocks[0].shape[1] // len(order)
    low, high = 0, len(order)
    received = []
    ahead = yield None
    for bit in bits + [0]:
        middle = (low + high) // 2 if bit else high
        value = pair_product(
            blocks, sides, low * width, middle * width, received, blocks_first, ahead or ()
        )
        got = value
        if bit:
            got = swap(value, "dp", bit)
            received.append((middle * width, got))
        low = middle
        ahead = yield value, got


def as_row(values):
    ones = jnp.ones((8, values.shape[1]), f32)
    return dot(ones, values, (1, 1), highest)[0:1]


def as_column(row):
    length = row.shape[1]
    down = lax.broadcasted_iota(jnp.int32, (length, length), 0)
    across = lax.broadcasted_iota(jnp.int32, (length, length), 1)
    return jnp.sum(jnp.where(down == across, row, 0.0), axis=1, keepdims=True)


def sum_column(refs):
    return as_column((refs[0][...] + refs[1][...]) + (refs[2][...] + refs[3][...]))


def conv_values(values, taps, positions):
    total = taps[4:5] + taps[0:1] * values
    for offset in range(1, 4):
        shifted = pltpu.roll(values, offset, 0)
        total = total + taps[offset : offset + 1] * jnp.where(positions >= offset, shifted, 0.0)
    return total


def conv_back(grad, values, taps, positions):
    total = taps[0:1] * grad
    tap_grads = [jnp.sum(grad * values, axis=0, keepdims=True)]
    for offset in range(1, 4):
        masked = jnp.where(positions >= offset, grad, 0.0)
        shifted = pltpu.roll(masked, masked.shape[0] - offset, 0)
        total = total + taps[offset : offset + 1] * shifted
        tap_grads.append(jnp.sum(shifted * values, axis=0, keepdims=True))
    tap_grads.append(jnp.sum(grad, axis=0, keepdims=True))
    return total, tap_grads


def scan_parts(step_in, decay_row, bias_row):
    raw = step_in + bias_row
    step = jnp.maximum(raw, 0.0) + jnp.log(1.0 + jnp.exp(-jnp.abs(raw)))
    rates = -jnp.exp(decay_row) * step
    length = rates.shape[0]
    row = lax.broadcasted_iota(jnp.int32, (length, length), 0)
    col = lax.broadcasted_iota(jnp.int32, (length, length), 1)
    lower = (row >= col).astype(f32)
    upper = (row <= col).astype(f32)
    cumulative = dot(lower, rates, (1, 0), highest)
    cumulative_t = dot(rates, upper, (0, 0), highest)
    return raw, step, rates, cumulative, cumulative_t, row >= col, upper


def scan_forward_kernel(
    zx_ref, bc_ref, dt_ref, taps_x_ref, taps_bc_ref, heads_ref, pos_ref, seg_col_ref, seg_row_ref,
    y_ref, gated_ref, square_ref, xa_ref, ba_ref,
):
    positions = pos_ref[...]
    conv_x = conv_values(zx_ref[1], taps_x_ref[...], positions)
    x_act = conv_x * sigmoid(conv_x)
    conv_bc = conv_values(bc_ref[...], taps_bc_ref[...], positions)
    bc_act = (conv_bc * sigmoid(conv_bc)).astype(bf16)
    state = bc_act.shape[1] // 2
    xa_ref[...] = x_act
    ba_ref[...] = bc_act
    heads = heads_ref[...]
    _, step, _, cumulative, cumulative_t, causal, _ = scan_parts(
        dt_ref[...], heads[0:1], heads[1:2]
    )
    inside = causal & (seg_col_ref[...] == seg_row_ref[...])
    gram = dot(bc_act[:, state:], bc_act[:, :state], (1, 1))
    length = positions.shape[0]
    lane = lax.broadcasted_iota(jnp.int32, (length, 128), 1)
    low_half = lane < 64
    square = jnp.zeros((length, 128), f32)
    for pair in range(x_act.shape[1] // 128):
        cols = slice(pair * 128, pair * 128 + 128)
        first, second = 2 * pair, 2 * pair + 1
        x_pair = x_act[:, cols]
        dt_pair = jnp.where(low_half, step[:, first : first + 1], step[:, second : second + 1])
        scaled = x_pair * dt_pair
        total = jnp.where(
            low_half, heads[2:3, first : first + 1], heads[2:3, second : second + 1]
        ) * x_pair
        for head, keep in ((first, low_half), (second, ~low_half)):
            gap = cumulative[:, head : head + 1] - cumulative_t[head : head + 1, :]
            mixing = gram * jnp.exp(jnp.where(inside, gap, -1e30))
            total = total + dot(
                mixing.astype(bf16), jnp.where(keep, scaled, 0.0).astype(bf16), (1, 0)
            )
        z_pair = zx_ref[0, :, cols]
        gated = total * (z_pair * sigmoid(z_pair))
        y_ref[:, cols] = total
        gated_ref[:, cols] = gated
        square = square + gated * gated
    square_ref[...] = as_row(square)


def scan_forward(zx, bc, dt, taps_x, taps_bc, heads, pos, seg_col, seg_row):
    tokens, inner = zx.shape[1:]
    return pl.pallas_call(
        scan_forward_kernel,
        out_shape=[
            jax.ShapeDtypeStruct((tokens, inner), f32),
            jax.ShapeDtypeStruct((tokens, inner), f32),
            jax.ShapeDtypeStruct((1, tokens), f32),
            jax.ShapeDtypeStruct((tokens, inner), f32),
            jax.ShapeDtypeStruct(bc.shape, bf16),
        ],
        compiler_params=params,
        cost_estimate=cost(10**9, 4 * 10**6, 10**6),
        name="scan_forward",
    )(zx, bc, dt, taps_x, taps_bc, heads, pos, seg_col, seg_row)


def scan_backward_kernel(
    zx_ref, bc_ref, dt_ref, taps_x_ref, taps_bc_ref, heads_ref, pos_ref, seg_col_ref, seg_row_ref,
    y_ref, xa_ref, ba_ref, up_ref, scale_ref, gain_ref, cross_a, cross_b, cross_c, cross_d, *rest
):
    (
        z_cot_ref, x_cot_ref, bc_cot_ref, dt_cot_ref, taps_x_out, taps_bc_out, heads_out, gain_out
    ) = rest[-8:]
    inner_width = y_ref.shape[1] * 4
    positions = pos_ref[...]
    length = positions.shape[0]
    bc_act = ba_ref[...]
    state = bc_act.shape[1] // 2
    heads = heads_ref[...]
    raw, step, rates, cumulative, cumulative_t, causal, upper = scan_parts(
        dt_ref[...], heads[0:1], heads[1:2]
    )
    inside = causal & (seg_col_ref[...] == seg_row_ref[...])
    gram = dot(bc_act[:, state:], bc_act[:, :state], (1, 1))
    lane = lax.broadcasted_iota(jnp.int32, (length, 128), 1)
    low_half = lane < 64
    scale = scale_ref[...]
    cross = sum_column((cross_a, cross_b, cross_c, cross_d)) / inner_width
    pull = scale * scale * scale * cross
    gram_grad = jnp.zeros((length, length), f32)
    head_lane = lax.broadcasted_iota(jnp.int32, (length, HEAD_PAD), 1)
    head_row = lax.broadcasted_iota(jnp.int32, (HEAD_PAD, length), 0)
    head_one = lax.broadcasted_iota(jnp.int32, (1, HEAD_PAD), 1)
    step_grad = jnp.zeros((length, HEAD_PAD), f32)
    row_sums = jnp.zeros((length, HEAD_PAD), f32)
    col_sums = jnp.zeros((HEAD_PAD, length), f32)
    skip_grad = jnp.zeros((1, HEAD_PAD), f32)
    for pair in range(y_ref.shape[1] // 128):
        cols = slice(pair * 128, pair * 128 + 128)
        first, second = 2 * pair, 2 * pair + 1
        z_pair = zx_ref[0, :, cols]
        y_pair = y_ref[:, cols]
        gate = sigmoid(z_pair)
        silu = z_pair * gate
        gated = y_pair * silu
        up = up_ref[:, cols]
        gain_out[:, cols] = jnp.sum(up * gated * scale, axis=0, keepdims=True)
        gated_grad = scale * (up * gain_ref[:, cols]) - gated * pull
        z_cot_ref[:, cols] = rounded(gated_grad * y_pair * (gate * (1.0 + z_pair * (1.0 - gate))))
        y_grad = gated_grad * silu
        x_pair = xa_ref[:, cols]
        dt_pair = jnp.where(low_half, step[:, first : first + 1], step[:, second : second + 1])
        skip_pair = jnp.where(
            low_half, heads[2:3, first : first + 1], heads[2:3, second : second + 1]
        )
        scaled = (x_pair * dt_pair).astype(bf16)
        scaled_grad = jnp.zeros((length, 128), f32)
        skip_product = y_grad * x_pair
        for head, keep in ((first, low_half), (second, ~low_half)):
            gap = cumulative[:, head : head + 1] - cumulative_t[head : head + 1, :]
            decay = jnp.exp(jnp.where(inside, gap, -1e30))
            mixing = gram * decay
            y_head = jnp.where(keep, y_grad, 0.0).astype(bf16)
            mixing_grad = dot(y_head, scaled, (1, 1))
            scaled_grad = scaled_grad + dot(mixing.astype(bf16), y_head, (0, 0))
            gram_grad = gram_grad + mixing_grad * decay
            moved = mixing_grad * mixing
            row_sums = row_sums + jnp.where(
                head_lane == head, jnp.sum(moved, axis=1, keepdims=True), 0.0
            )
            col_sums = col_sums + jnp.where(
                head_row == head, jnp.sum(moved, axis=0, keepdims=True), 0.0
            )
        step_product = scaled_grad * x_pair
        for head, keep in ((first, low_half), (second, ~low_half)):
            step_grad = step_grad + jnp.where(
                head_lane == head,
                jnp.sum(jnp.where(keep, step_product, 0.0), axis=1, keepdims=True),
                0.0,
            )
            skip_sum = jnp.sum(
                jnp.sum(jnp.where(keep, skip_product, 0.0), axis=0, keepdims=True),
                axis=1,
                keepdims=True,
            )
            skip_grad = skip_grad + jnp.where(head_one == head, skip_sum, 0.0)
        x_grad = scaled_grad * dt_pair + skip_pair * y_grad
        conv_x = conv_values(zx_ref[1, :, cols], taps_x_ref[:, cols], positions)
        gate = sigmoid(conv_x)
        conv_grad = x_grad * (gate * (1.0 + conv_x * (1.0 - gate)))
        total, tap_grads = conv_back(
            conv_grad, zx_ref[1, :, cols], taps_x_ref[:, cols], positions
        )
        x_cot_ref[:, cols] = rounded(total)
        for index, value in enumerate(tap_grads):
            taps_x_out[index : index + 1, cols] = value
    rate_grad = dot(upper, row_sums, (1, 0), highest) - dot(upper, col_sums, (1, 1), highest)
    step_grad = step_grad - rate_grad * jnp.exp(heads[0:1])
    raw_grad = step_grad * sigmoid(raw)
    dt_cot_ref[...] = rounded(raw_grad)
    heads_out[0:1, :] = jnp.sum(rate_grad * rates, axis=0, keepdims=True)
    heads_out[1:2, :] = jnp.sum(raw_grad, axis=0, keepdims=True)
    heads_out[2:3, :] = skip_grad
    gram_low = gram_grad.astype(bf16)
    b_grad = dot(gram_low, bc_act[:, state:], (0, 0))
    c_grad = dot(gram_low, bc_act[:, :state], (1, 0))
    for part, grad in enumerate((b_grad, c_grad)):
        cols = slice(part * state, part * state + state)
        conv = conv_values(bc_ref[:, cols], taps_bc_ref[:, cols], positions)
        gate = sigmoid(conv)
        conv_grad = grad * (gate * (1.0 + conv * (1.0 - gate)))
        total, tap_grads = conv_back(conv_grad, bc_ref[:, cols], taps_bc_ref[:, cols], positions)
        bc_cot_ref[:, cols] = rounded(total)
        for index, value in enumerate(tap_grads):
            taps_bc_out[index : index + 1, cols] = value


def scan_backward(
    zx, bc, dt, taps_x, taps_bc, heads, pos, seg_col, seg_row, y, xa, ba, up, scale, gain, cross,
    ahead,
):
    tokens, inner = zx.shape[1:]
    values = (zx, bc, dt, taps_x, taps_bc, heads, pos, seg_col, seg_row, y, xa, ba, up, scale, gain)
    values = values + tuple(cross)
    return pl.pallas_call(
        scan_backward_kernel,
        in_specs=[pl.BlockSpec(memory_space=pltpu.VMEM)] * len(values)
        + [pl.BlockSpec(memory_space=pl.ANY)] * len(ahead),
        out_shape=[
            jax.ShapeDtypeStruct((tokens, inner), f32),
            jax.ShapeDtypeStruct((tokens, inner), f32),
            jax.ShapeDtypeStruct(bc.shape, f32),
            jax.ShapeDtypeStruct(dt.shape, f32),
            jax.ShapeDtypeStruct(taps_x.shape, f32),
            jax.ShapeDtypeStruct(taps_bc.shape, f32),
            jax.ShapeDtypeStruct((3, HEAD_PAD), f32),
            jax.ShapeDtypeStruct((1, inner), f32),
        ],
        compiler_params=params,
        cost_estimate=cost(3 * 10**9, 8 * 10**6, 10**6),
        name="scan_backward",
    )(*values, *ahead)


def turn(values, cosine, sine, low_quarter):
    width = values.shape[1]
    partner = jnp.where(
        low_quarter, pltpu.roll(values, width - HD // 2, 1), pltpu.roll(values, HD // 2, 1)
    )
    return values * cosine + partner * sine


def masked_scores(q_head, kv, allowed):
    scores = dot(q_head, kv, (1, 1)) * HD ** (-0.5)
    return jnp.where(allowed, scores, -1e30)


def softmax(scores):
    exponent = jnp.exp(scores - jnp.max(scores, axis=1, keepdims=True))
    return exponent * (1.0 / jnp.sum(exponent, axis=1, keepdims=True))


def attention_masks(length, seg_col_ref, seg_row_ref):
    row = lax.broadcasted_iota(jnp.int32, (length, length), 0)
    col = lax.broadcasted_iota(jnp.int32, (length, length), 1)
    allowed = (col <= row) & (seg_col_ref[...] == seg_row_ref[...])
    lane = lax.broadcasted_iota(jnp.int32, (length, 2 * HD), 1)
    return allowed, lane < HD, (lane % HD) < HD // 2


def to_low(values, head):
    return values if head == 0 else pltpu.roll(values, HD, 1)


def to_high(values, head):
    return values if head == 1 else pltpu.roll(values, HD, 1)


def attention_forward_kernel(
    head_ref, q_ref, kv_ref, cos_ref, sin_ref, seg_col_ref, seg_row_ref, q_out, kv_out, attn_out
):
    length = q_ref.shape[0]
    allowed, low_half, low_quarter = attention_masks(length, seg_col_ref, seg_row_ref)
    cosine, sine = cos_ref[...], sin_ref[...]
    q_rot = rounded(turn(q_ref[...], cosine, sine, low_quarter))
    first = head_ref[0] == 0
    keys = jnp.where(first, kv_ref[0], pltpu.roll(kv_ref[0], HD, 1))
    kv_in = jnp.where(low_half, keys, jnp.where(first, pltpu.roll(kv_ref[1], HD, 1), kv_ref[1]))
    kv = jnp.where(low_half, turn(kv_in, cosine, sine, low_quarter), kv_in).astype(bf16)
    q_out[...] = q_rot
    kv_out[...] = kv
    parts = []
    for head in range(2):
        q_head = jnp.where(low_half, to_low(q_rot, head), 0.0).astype(bf16)
        probability = softmax(masked_scores(q_head, kv, allowed)).astype(bf16)
        parts.append(dot(probability, kv, (1, 0)))
    attn_out[...] = rounded(jnp.where(low_half, pltpu.roll(parts[0], HD, 1), parts[1]))


def attention_forward(kv_head, q, kv, cosine, sine, seg_col, seg_row):
    return pl.pallas_call(
        attention_forward_kernel,
        in_specs=[pl.BlockSpec(memory_space=pltpu.SMEM)]
        + [pl.BlockSpec(memory_space=pltpu.VMEM)] * 6,
        out_shape=[
            jax.ShapeDtypeStruct(q.shape, f32),
            jax.ShapeDtypeStruct(q.shape, bf16),
            jax.ShapeDtypeStruct(q.shape, f32),
        ],
        compiler_params=params,
        cost_estimate=cost(5 * 10**8, 10**6, 10**5),
        name="attention_forward",
    )(kv_head, q, kv, cosine, sine, seg_col, seg_row)


def attention_backward_kernel(
    head_ref, q_ref, kv_ref, grad_ref, cos_ref, sin_ref, seg_col_ref, seg_row_ref, *rest
):
    q_cot, kv_cot = rest[-2:]
    length = q_ref.shape[0]
    allowed, low_half, low_quarter = attention_masks(length, seg_col_ref, seg_row_ref)
    cosine, sine = cos_ref[...], -sin_ref[...]
    q_rot, kv = q_ref[...], kv_ref[...]
    grad = rounded(grad_ref[...])
    parts = []
    kv_grad = jnp.zeros((length, 2 * HD), f32)
    for head in range(2):
        q_head = jnp.where(low_half, to_low(q_rot, head), 0.0)
        probability = softmax(masked_scores(q_head.astype(bf16), kv, allowed))
        g_head = jnp.where(low_half, 0.0, to_high(grad, head)).astype(bf16)
        prob_grad = dot(g_head, kv, (1, 1))
        inner = jnp.sum(probability * prob_grad, axis=1, keepdims=True)
        score_grad = (probability * (prob_grad - inner)).astype(bf16)
        parts.append(dot(score_grad, kv, (1, 0)) * HD ** (-0.5))
        kv_grad = kv_grad + dot(score_grad, (q_head * HD ** (-0.5)).astype(bf16), (0, 0))
        kv_grad = kv_grad + dot(probability.astype(bf16), g_head, (0, 0))
    q_grad = jnp.where(low_half, parts[0], pltpu.roll(parts[1], HD, 1))
    q_cot[...] = rounded(turn(q_grad, cosine, sine, low_quarter))
    kv_grad = rounded(jnp.where(low_half, turn(kv_grad, cosine, sine, low_quarter), kv_grad))
    turned = pltpu.roll(kv_grad, HD, 1)
    first = head_ref[0] == 0
    kept = low_half == first
    kv_cot[:, : 2 * HD] = jnp.where(kept, jnp.where(first, kv_grad, turned), 0.0)
    kv_cot[:, 2 * HD :] = jnp.where(kept, jnp.where(first, turned, kv_grad), 0.0)


def attention_backward(kv_head, q, kv, grad, cosine, sine, seg_col, seg_row, ahead):
    wide = (q.shape[0], KVH * 2 * HD)
    return pl.pallas_call(
        attention_backward_kernel,
        in_specs=[pl.BlockSpec(memory_space=pltpu.SMEM)]
        + [pl.BlockSpec(memory_space=pltpu.VMEM)] * 7
        + [pl.BlockSpec(memory_space=pl.ANY)] * len(ahead),
        out_shape=[jax.ShapeDtypeStruct(q.shape, f32), jax.ShapeDtypeStruct(wide, f32)],
        compiler_params=params,
        cost_estimate=cost(10**9, 10**6, 10**5),
        name="attention_backward",
    )(kv_head, q, kv, grad, cosine, sine, seg_col, seg_row, *ahead)


def mix_kernel(
    core_ref, gated_ref, gain_ref, attn_ref, out_w_ref, o_w_ref, sq_a, sq_b, sq_c, sq_d, *rest
):
    mixed_ref, scale_ref, other_ref = rest[-3:]
    inner = gated_ref.shape[1]
    half = gated_ref.shape[0] // 2
    scale = lax.rsqrt(sum_column((sq_a, sq_b, sq_c, sq_d)) / (4 * inner) + epsilon)
    scale_ref[...] = scale
    mixed_ref[:, :inner] = rounded(gated_ref[...] * scale * gain_ref[...])
    mixed_ref[:, inner:] = attn_ref[...]
    other_ref[...] = mix_product(mixed_ref, out_w_ref, o_w_ref, half_rows(1 - core_ref[0], half))


def mix_product(mixed_ref, out_w_ref, o_w_ref, span):
    inner = out_w_ref.shape[0]
    part = mixed_ref[span, :].astype(bf16)
    return dot(part[:, :inner], out_w_ref[...], (1, 0)) + dot(part[:, inner:], o_w_ref[...], (1, 0))


def mix_mine_kernel(core_ref, mixed_ref, out_w_ref, o_w_ref, got_ref, mine_ref):
    half = got_ref.shape[0]
    span = half_rows(core_ref[0], half)
    mine_ref[...] = mix_product(mixed_ref, out_w_ref, o_w_ref, span) + got_ref[...]


def feed_product(cot_ref, gu_ref, span):
    hidden = gu_ref.shape[2]
    part = cot_ref[span, :].astype(bf16)
    return dot(part[:, :hidden], gu_ref[0], (1, 1)) + dot(part[:, hidden:], gu_ref[1], (1, 1))


def feed_kernel(core_ref, mine_ref, got_ref, in_ref, gain_ref, act_grad_ref, gu_ref, *rest):
    resid_ref, scale_ref, normed_ref, act_ref, cot_ref, other_ref = rest[-6:]
    core = core_ref[0]
    half = mine_ref.shape[0]
    for which, ref in ((core, mine_ref), (1 - core, got_ref)):
        span = half_rows(which, half)
        resid_ref[span, :] = in_ref[span, :].astype(f32) + ref[...]
    resid = resid_ref[...]
    scale = rms_scale(resid)
    scale_ref[...] = scale
    normed_ref[...] = (resid * scale * gain_ref[...]).astype(bf16)
    normed = normed_ref[...]
    hidden = gu_ref.shape[2]
    for start in range(0, hidden, 256):
        cols = slice(start, start + 256)
        gate = dot(normed, gu_ref[0, :, cols], (1, 0))
        up = dot(normed, gu_ref[1, :, cols], (1, 0))
        slope = sigmoid(gate)
        silu = gate * slope
        act_ref[:, cols] = rounded(silu * up)
        act_grad = act_grad_ref[:, cols]
        cot_ref[:, cols] = rounded(act_grad * up * slope * (1.0 + gate * (1.0 - slope)))
        cot_ref[:, hidden + start : hidden + start + 256] = rounded(act_grad * silu)
    other_ref[...] = feed_product(cot_ref, gu_ref, half_rows(1 - core, half))


def feed_mine_kernel(core_ref, cot_ref, gu_ref, got_ref, *rest):
    span = half_rows(core_ref[0], got_ref.shape[0])
    rest[-1][...] = feed_product(cot_ref, gu_ref, span) + got_ref[...]


def mix_back_kernel(
    core_ref, mine_ref, got_ref, resid_ref, scale_ref, gain_ref, out_grad_ref, out_w_ref, o_w_ref,
    gated_ref, gated_gain_ref, *rest,
):
    grad_ref, mix_ref, gain_grad_ref, up_ref, attn_grad_ref, cross_ref = rest[-6:]
    core = core_ref[0]
    half = mine_ref.shape[0]
    for which, ref in ((core, mine_ref), (1 - core, got_ref)):
        grad_ref[half_rows(which, half), :] = ref[...]
    normed_grad = grad_ref[...]
    resid = resid_ref[...]
    scale = scale_ref[...]
    gain_grad_ref[...] = jnp.sum(normed_grad * resid * scale, axis=0, keepdims=True)
    weighted = normed_grad * gain_ref[...]
    mean = jnp.mean(weighted * resid, axis=1, keepdims=True)
    resid_grad = (
        out_grad_ref[...].astype(f32) + scale * weighted - resid * (scale * scale * scale * mean)
    )
    grad_ref[...] = resid_grad
    mix = resid_grad.astype(bf16)
    mix_ref[...] = mix
    up = dot(mix, out_w_ref[...], (1, 1))
    up_ref[...] = up
    attn_grad_ref[...] = dot(mix, o_w_ref[...], (1, 1))
    cross_ref[...] = as_row(up * gated_gain_ref[...] * gated_ref[...])


def call_dense(kernel, name, shapes, core, values, ahead=(), scratch=()):
    flops = 2 * sum(value.size for value in values) * 256
    places = [pltpu.SMEM if value.dtype == jnp.int32 else pltpu.VMEM for value in values]
    return pl.pallas_call(
        kernel,
        in_specs=[pl.BlockSpec(memory_space=pltpu.SMEM)]
        + [pl.BlockSpec(memory_space=place) for place in places]
        + [pl.BlockSpec(memory_space=pl.ANY)] * len(ahead),
        out_shape=[jax.ShapeDtypeStruct(shape, kind) for shape, kind in shapes],
        scratch_shapes=[pltpu.VMEM(shape, f32) for shape in scratch],
        compiler_params=params,
        cost_estimate=cost(flops, 4 * 10**6, 10**5),
        name=name,
    )(core, *values, *ahead)


def chunks(values):
    return [
        (value, row, start)
        for value in values
        for row in range(value.shape[0])
        for start in range(0, value.shape[1], 128)
    ]


def pick(index, blocks):
    total = blocks[0]
    for place in range(1, len(blocks)):
        total = jnp.where(index == place, blocks[place], total)
    return total


def shared_blocks(bc_ref, kv_ref):
    return [ref[:, at : at + 128] for ref in (bc_ref, kv_ref) for at in (0, 128)]


def post_kernel(
    core_ref, me_ref, grad_ref, in_ref, taps_ref, bc_ref, kv_ref, mine_ref, other_ref, near_ref,
    state_ref,
):
    half = mine_ref.shape[0]
    tokens = 2 * half
    mine_ref[...] = grad_ref[half_rows(core_ref[0], half), :]
    other_ref[...] = grad_ref[half_rows(1 - core_ref[0], half), :]
    inputs = in_ref[...].astype(f32)
    gain = jnp.sum(grad_ref[...] * inputs * rms_scale(inputs), axis=0, keepdims=True)
    state_ref[...] = jnp.zeros_like(state_ref)
    for at, (value, row, start) in enumerate(chunks((gain, taps_ref[...]))):
        state_ref[at : at + 1, :] = value[row : row + 1, start : start + 128]
    blocks = shared_blocks(bc_ref, kv_ref)
    near_ref[:tokens, :] = pick(me_ref[0] ^ 1, blocks)
    near_ref[tokens : 2 * tokens, :] = pick(me_ref[0] ^ 3, blocks)
    near_ref[2 * tokens :, :] = state_ref[...]


def share_kernel(core_ref, me_ref, near_ref, bc_ref, kv_ref, state_ref, far_ref):
    tokens = bc_ref.shape[0]
    blocks = shared_blocks(bc_ref, kv_ref)
    far_ref[:tokens, :] = pick(me_ref[0] ^ 2, blocks) + near_ref[tokens : 2 * tokens, :]
    far_ref[tokens:, :] = state_ref[...] + near_ref[2 * tokens :, :]


def few_kernel(
    core_ref, me_ref, near_ref, far_own_ref, far_ref, bc_ref, kv_ref, q_ref, dt_ref, gain_two_ref,
    taps_ref, gain_ref, heads_ref, *rest
):
    few_ref = rest[-1]
    tokens = bc_ref.shape[0]
    blocks = shared_blocks(bc_ref, kv_ref)
    few_ref[:tokens, :128] = q_ref[...]
    few_ref[:tokens, 128:256] = (
        pick(me_ref[0], blocks) + near_ref[:tokens, :] + far_ref[:tokens, :]
    )
    few_ref[:tokens, 256:] = dt_ref[...]
    state = far_own_ref[tokens:, :] + far_ref[tokens:, :]
    used = STATE_ROWS
    few_ref[tokens:, :] = jnp.zeros((few_ref.shape[0] - tokens, few_ref.shape[1]), f32)
    values = (state[:used], gain_two_ref[...], taps_ref[...], gain_ref[...], heads_ref[...])
    for at, (value, row, start) in enumerate(chunks(values)):
        place = tokens + at // 3
        cols = slice(at % 3 * 128, at % 3 * 128 + 128)
        few_ref[place : place + 1, cols] = value[row : row + 1, start : start + 128]


def unpack_kernel(core_ref, few_ref, own_ref, *refs):
    rows_out = own_ref.shape[0]
    own_ref[...] = few_ref[:rows_out, 128:256]
    for at, (ref, row, start) in enumerate(chunks(refs)):
        place = rows_out + at // 3
        cols = slice(at % 3 * 128, at % 3 * 128 + 128)
        ref[row : row + 1, start : start + 128] = few_ref[place : place + 1, cols]


def assemble_kernel(core_ref, me_ref, own_ref, near_ref, far_ref, far_near_ref, bc_ref, *kv_refs):
    blocks = (own_ref[...], near_ref[...], far_ref[...], far_near_ref[...])
    for place in range(4):
        value = pick(me_ref[0] ^ place, blocks)
        if place < 2:
            bc_ref[:, place * 128 : place * 128 + 128] = value
        else:
            kv_refs[place - 2][...] = value


def input_grad_kernel(core_ref, mine_ref, got_ref, grad_ref, in_ref, gain_ref, out_ref, full_ref):
    half = mine_ref.shape[0]
    full_ref[half_rows(core_ref[0], half), :] = mine_ref[...]
    full_ref[half_rows(1 - core_ref[0], half), :] = got_ref[...]
    inputs = in_ref[...].astype(f32)
    scale = rms_scale(inputs)
    weighted = full_ref[...] * gain_ref[...]
    mean = jnp.mean(weighted * inputs, axis=1, keepdims=True)
    total = grad_ref[...] + scale * weighted - inputs * (scale * scale * scale * mean)
    out_ref[...] = total.astype(bf16)


def layer_out_kernel(core_ref, mine_ref, got_ref, resid_ref, out_ref, full_ref):
    half = mine_ref.shape[0]
    full_ref[half_rows(core_ref[0], half), :] = mine_ref[...]
    full_ref[half_rows(1 - core_ref[0], half), :] = got_ref[...]
    out_ref[...] = (resid_ref[...] + full_ref[...]).astype(bf16)


def rotary_tables(positions):
    half = HD // 2
    frequency = rope_base ** (-jnp.arange(half, dtype=f32) / half)
    angles = positions.astype(f32)[:, None] * frequency[None, :]
    cosine, sine = jnp.cos(angles), jnp.sin(angles)
    return (
        jnp.concatenate([cosine] * 4, axis=1),
        jnp.concatenate([-sine, sine, -sine, sine], axis=1),
    )


def on_device(
    hidden,
    positions,
    out_grad,
    norm_one,
    zx_weight,
    bc_weight,
    dt_weight,
    conv_inner,
    conv_state,
    decay_log,
    dt_bias,
    skip_gain,
    gated_gain,
    out_weight,
    q_weight,
    kv_weight,
    o_weight,
    norm_two,
    gu_weight,
    down_weight,
):
    tokens, model = hidden.shape
    head_count = dt_weight.shape[1]
    inner_cols = conv_inner.shape[1]
    hidden_cols = gu_weight.shape[2]
    query_cols = q_weight.shape[1]
    segment = jnp.cumsum((positions == 0).astype(jnp.int32), dtype=jnp.int32)
    seg_col, seg_row, pos_col = segment[:, None], segment[None, :], positions[:, None]
    cosine, sine = rotary_tables(positions)
    head_pad = ((0, 0), (0, HEAD_PAD - head_count))
    heads = jnp.pad(jnp.stack([decay_log, dt_bias, skip_gain]), head_pad)
    dt_wide = jnp.pad(dt_weight, head_pad)

    core = lax.axis_index("tensor").astype(jnp.int32) % 2
    core_arg = core.reshape(1)
    kv_head = (lax.axis_index("tensor") * (query_cols // HD) // (QH // KVH)).astype(jnp.int32)
    kv_head = kv_head.reshape(1)
    half = tokens // 2
    half_model = model // 2
    wide = (tokens, model)
    half_wide = (half, model)

    inputs = hidden.astype(f32)
    scale_one = rms_scale(inputs)
    normed = (inputs * scale_one * norm_one).astype(bf16)
    own_normed, normed_sent = arrange(1, normed)
    normed_pair = (own_normed, *swap_shared(normed_sent, 1))
    own_out, out_sent = arrange(2, out_grad)
    out_pair = (own_out, *swap_shared(out_sent, 2))

    proj_zx = jnp.einsum("td,dkc->ktc", normed, zx_weight, preferred_element_type=f32)
    proj_bc = dot(normed, bc_weight, (1, 0))
    proj_dt = dot(normed, dt_wide, (1, 0))
    scan_args = (
        proj_zx, proj_bc, proj_dt, conv_inner, conv_state, heads, pos_col, seg_col, seg_row
    )
    y, gated, square, x_act, bc_act = scan_forward(*scan_args)
    squares = spread_tensor(square)

    query = dot(normed, q_weight, (1, 0))
    key_value = jnp.einsum("td,dkc->ktc", normed, kv_weight, preferred_element_type=f32)
    q_rot, kv_rot, attn = attention_forward(
        kv_head, query, key_value, cosine, sine, seg_col, seg_row
    )
    act_grad = dot(out_grad, down_weight, (1, 1))
    gu_split = gu_weight.transpose(1, 0, 2)

    gain_row = gated_gain[None, :]
    mixed, gate_scale, other = call_dense(
        mix_kernel,
        "mix",
        [((tokens, inner_cols + query_cols), f32), ((tokens, 1), f32), (half_wide, f32)],
        core_arg,
        (gated, gain_row, attn, out_weight, o_weight, *squares),
        (normed_pair[1],),
    )
    mixed_got = swap(mixed, "dp", 1)
    mixed_pair = (mixed, mixed_got)
    (mine,) = call_dense(
        mix_mine_kernel,
        "mix_mine",
        [(half_wide, f32)],
        core_arg,
        (mixed, out_weight, o_weight, swap(other, "tensor", 1)),
    )
    resid, scale_two, normed_two, act, gu_cot, other = call_dense(
        feed_kernel,
        "feed",
        [
            (wide, f32),
            ((tokens, 1), f32),
            (wide, bf16),
            ((tokens, hidden_cols), f32),
            ((tokens, 2 * hidden_cols), f32),
            (half_wide, f32),
        ],
        core_arg,
        (
            *tensor_halves(mine, (out_pair[1], mixed_got, act_grad, gu_split)),
            hidden,
            norm_two[None, :],
            act_grad,
            gu_split,
        ),
    )
    (mine,) = call_dense(
        feed_mine_kernel,
        "feed_mine",
        [(half_wide, f32)],
        core_arg,
        (gu_cot, gu_split, swap(other, "tensor", 1)),
    )
    own_two, sent_two = arrange(1, normed_two)
    two_got = swap_shared(sent_two, 1)
    normed_two_pair = (own_two, *two_got)
    act_got = swap(act, "dp", 2)
    gu_got = swap(gu_cot, "dp", 1)
    down_stages = halving(out_pair, (act, act_got), False, 2)
    gu_stages = halving(normed_two_pair, (gu_cot, gu_got), True)
    for stages in (down_stages, gu_stages):
        next(stages)
    resid_grad, mix_grad, norm_two_grad, up, attn_grad, cross = call_dense(
        mix_back_kernel,
        "mix_back",
        [
            (wide, f32),
            (wide, bf16),
            ((1, model), f32),
            ((tokens, inner_cols), f32),
            ((tokens, query_cols), f32),
            ((1, tokens), f32),
        ],
        core_arg,
        (
            *tensor_halves(mine, (act_got, *two_got)),
            resid,
            scale_two,
            norm_two[None, :],
            out_grad,
            out_weight,
            o_weight,
            gated,
            gain_row,
        ),
    )
    crosses = spread_tensor(cross)
    last, down_got = down_stages.send((up,))
    q_cot, kv_cot = attention_backward(
        kv_head, q_rot, kv_rot, attn_grad, cosine, sine, seg_col, seg_row, (last,)
    )
    own_mix, sent_mix = arrange(1, mix_grad)
    mix_pair = (own_mix, *swap_shared(sent_mix, 1))

    mix_stages = halving(mix_pair, mixed_pair, False)
    next(mix_stages)
    act_b = act.astype(bf16)
    mlp_other = dot(rows(act_b, (1 - core) * half, half), down_weight, (1, 0))
    mlp_mine = dot(rows(act_b, core * half, half), down_weight, (1, 0)) + swap(
        mlp_other, "tensor", 1
    )

    z_cot, x_cot, bc_cot, dt_cot, taps_x_grad, taps_bc_grad, heads_grad, gain_grad = scan_backward(
        *scan_args, y, x_act, bc_act, up, gate_scale, gain_row, crosses, (q_cot,)
    )

    zx_cot = jnp.stack([z_cot, x_cot], axis=1).astype(bf16)
    normed_grad = (
        jnp.einsum("tkc,dkc->td", zx_cot, zx_weight, preferred_element_type=f32)
        + dot(bc_cot.astype(bf16), bc_weight, (1, 1))
        + dot(dt_cot.astype(bf16), dt_wide, (1, 1))
        + dot(q_cot.astype(bf16), q_weight, (1, 1))
        + jnp.einsum(
            "tkc,dkc->td",
            kv_cot.astype(bf16).reshape(tokens, 2, KVH * HD),
            kv_weight,
            preferred_element_type=f32,
        )
    )
    me_arg = lax.axis_index("tensor").astype(jnp.int32).reshape(1)
    normed_mine, normed_other, near, state_part = call_dense(
        post_kernel,
        "post",
        [
            (half_wide, f32),
            (half_wide, f32),
            ((2 * tokens + STATE_PAD, 128), f32),
            ((STATE_PAD, 128), f32),
        ],
        core_arg,
        (me_arg, normed_grad, hidden, taps_bc_grad, bc_cot, kv_cot),
    )
    zx_own = jnp.concatenate([z_cot, x_cot], axis=1)
    zx_got = swap(zx_own, "dp", 1)
    zx_stages = halving(normed_pair, (zx_own, zx_got), True)
    near = swap(near, "tensor", 1)
    (far_own,) = call_dense(
        share_kernel,
        "share",
        [((tokens + STATE_PAD, 128), f32)],
        core_arg,
        (me_arg, near, bc_cot, kv_cot, state_part),
    )
    far = swap(far_own, "tensor", 2)
    (few,) = call_dense(
        few_kernel,
        "few",
        [((tokens + SMALL_ROWS, 384), f32)],
        core_arg,
        (
            me_arg, near, far_own, far, bc_cot, kv_cot, q_cot, dt_cot, norm_two_grad, taps_x_grad,
            gain_grad, heads_grad,
        ),
    )
    few_got = swap(few, "dp", 1)
    few_stages = halving(normed_pair, (few, few_got), True)
    next(zx_stages)
    next(few_stages)
    normed_mine = normed_mine + swap(normed_other, "tensor", 1)

    gots = {"down": [down_got]}
    totals = {}
    stage_list = {
        "down": down_stages,
        "gu": gu_stages,
        "mix": mix_stages,
        "zx": zx_stages,
        "few": few_stages,
    }

    def advance(name, *ahead):
        value, got = stage_list[name].send(ahead)
        gots.setdefault(name, []).append(got)
        totals[name] = value
        return value

    last = advance("gu", x_cot)
    last = advance("mix", last, zx_got)
    last = advance("gu", last, few)
    last = advance("zx", last, gots["mix"][0])
    normed_mine, normed_other = tensor_halves(normed_mine, (last,))
    last = advance("few", normed_mine)
    last = advance("mix", last)
    last = advance("down", last, gots["gu"][1])
    last = advance("zx", last)
    last = advance("gu", last)
    last = advance("few", last)
    last = advance("mix", last)
    last = advance("down", last)
    last = advance("few", last)
    last = advance("zx", last)
    (input_grad,) = call_dense(
        input_grad_kernel,
        "input_grad",
        [(wide, bf16)],
        core_arg,
        (normed_mine, normed_other, resid_grad, hidden, norm_one[None, :]),
        scratch=(wide,),
    )
    (layer_out,) = call_dense(
        layer_out_kernel,
        "layer_out",
        [(wide, bf16)],
        core_arg,
        (*tensor_halves(mlp_mine), resid),
        scratch=(wide,),
    )
    for name, stages in stage_list.items():
        for value, _ in stages:
            totals[name] = value
    down_shard, mixed_shard = totals["down"], totals["mix"]
    out_shard, o_shard = mixed_shard[:inner_cols], mixed_shard[inner_cols:]
    gu_shard = totals["gu"].reshape(-1, 2, hidden_cols)
    zx_shard = totals["zx"].reshape(-1, 2, inner_cols)
    few_shard = totals["few"]
    shard_rows = model // lax.axis_size("dp")
    q_shard = few_shard[:shard_rows, :query_cols]
    dt_shard = few_shard[:shard_rows, 256 : 256 + head_count]
    own, norm_one_grad, state_grad, norm_two_grad, inner_grad, gain_grad, heads_grad = call_dense(
        unpack_kernel,
        "unpack",
        [
            ((shard_rows, 128), f32),
            ((1, model), f32),
            (conv_state.shape, f32),
            ((1, model), f32),
            (conv_inner.shape, f32),
            ((1, inner_cols), f32),
            ((3, HEAD_PAD), f32),
        ],
        core_arg,
        (few_shard,),
    )
    head_sums = heads_grad[:, :head_count]
    near = swap(own, "tensor", 1)
    bc_shard, *kv_parts = call_dense(
        assemble_kernel,
        "assemble",
        [((shard_rows, 256), f32), ((shard_rows, 128), f32), ((shard_rows, 128), f32)],
        core_arg,
        (me_arg, own, near, swap(own, "tensor", 2), swap(own, "tensor", 3)),
    )
    kv_shard = jnp.stack(kv_parts, axis=1)
    return (
        layer_out,
        input_grad,
        norm_one_grad.reshape(-1),
        zx_shard,
        bc_shard,
        dt_shard,
        inner_grad,
        state_grad,
        head_sums[0],
        head_sums[1],
        head_sums[2],
        gain_grad.reshape(-1),
        out_shard,
        q_shard,
        kv_shard,
        o_shard,
        norm_two_grad.reshape(-1),
        gu_shard,
        down_shard,
    )


def solution(mesh):
    placed = (
        P("dp", None),
        P("dp"),
        P("dp", None),
        P(),
        P(None, None, "tensor"),
        P(),
        P(None, "tensor"),
        P(None, "tensor"),
        P(),
        P("tensor"),
        P("tensor"),
        P("tensor"),
        P("tensor"),
        P("tensor", None),
        P(None, "tensor"),
        P(),
        P("tensor", None),
        P(),
        P(None, None, "tensor"),
        P("tensor", None),
    )
    return jax.shard_map(
        on_device,
        mesh=mesh,
        in_specs=placed,
        out_specs=(
            P("dp", None),
            P("dp", None),
            P(),
            P("dp", None, "tensor"),
            P("dp", None),
            P("dp", "tensor"),
            P(None, "tensor"),
            P(),
            P("tensor"),
            P("tensor"),
            P("tensor"),
            P("tensor"),
            P("tensor", "dp"),
            P("dp", "tensor"),
            P("dp", None, None),
            P("tensor", "dp"),
            P(),
            P("dp", None, "tensor"),
            P("tensor", "dp"),
        ),
        check_vma=False,
    )
```

```python
import functools

import jax
import jax.numpy as jnp
from jax import lax
from jax.experimental import pallas as pl
from jax.experimental.pallas import tpu as pltpu
from jax.sharding import PartitionSpec as P

QH = 8
KVH = 2
HD = 64
HEAD_PAD = 128
STATE_ROWS = 18
STATE_PAD = 24
SMALL_ROWS = 16
COST = 3 * 10**9

epsilon = 1e-05
rope_base = 10000.0
highest = lax.Precision.HIGHEST
bf16 = jnp.bfloat16
f32 = jnp.float32
params = pltpu.CompilerParams(vmem_limit_bytes=40 * 1024 * 1024)


def dot(left, right, dims, precision=None):
    return lax.dot_general(
        left,
        right,
        ((dims[:1], dims[1:]), ((), ())),
        precision=precision,
        preferred_element_type=f32,
    )


def rms_scale(values):
    return lax.rsqrt(jnp.mean(values * values, axis=-1, keepdims=True) + epsilon)


def sigmoid(values):
    return 1.0 / (1.0 + jnp.exp(-values))


def rounded(values):
    return values.astype(bf16).astype(f32)


def cost(flops, read, exps=0):
    return pl.CostEstimate(flops=COST, bytes_accessed=10**6, transcendentals=0)


def call(kernel, name, out_shapes, values, ahead=(), scratch=(), flops=10**6):
    def place(value):
        if value.dtype == jnp.int32 and value.size == 1:
            return pl.BlockSpec(memory_space=pltpu.SMEM)
        return whole(value)

    def whole(value):
        zeros = (0,) * len(value.shape)
        return pl.BlockSpec(value.shape, lambda step: zeros)

    shapes = [jax.ShapeDtypeStruct(shape, kind) for shape, kind in out_shapes]
    return pl.pallas_call(
        kernel,
        grid=(1,),
        in_specs=[place(value) for value in values]
        + [pl.BlockSpec(memory_space=pl.ANY)] * len(ahead),
        out_specs=[whole(shape) for shape in shapes],
        out_shape=shapes,
        scratch_shapes=[pltpu.VMEM(shape, kind) for shape, kind in scratch],
        compiler_params=params,
        cost_estimate=cost(flops, flops),
        name=name,
    )(*values, *ahead)


def swap(values, axis, mask):
    pairs = [(index, index ^ mask) for index in range(lax.axis_size(axis))]
    return lax.ppermute(values, axis, pairs)


def spread_tensor(values):
    return [values] + [swap(values, "tensor", mask) for mask in (1, 2, 3)]


def add_spread(parts):
    return (parts[0] + parts[1]) + (parts[2] + parts[3])


def add_kernel(left_ref, right_ref, *rest):
    rest[-1][...] = left_ref[...] + right_ref[...]


def tensor_halves(mine, ahead=()):
    values = (mine, swap(mine, "tensor", 2))
    (mine,) = call(add_kernel, "add_halves", [(mine.shape, f32)], values, ahead)
    return mine, swap(mine, "tensor", 1)


def swap_shared(values, mask):
    first = swap(values, "dp", mask)
    return first, swap(first, "tensor", 1)


def rows(values, start, size):
    return lax.dynamic_slice_in_dim(values, start, size, 0)


def half_rows(core, size):
    return pl.ds(pl.multiple_of(core * size, size), size)


def halving_order(size, pair):
    order, bits, bit = [0], [], 1
    while bit < size:
        if bit != pair:
            bits.append(bit)
        bit *= 2
    for bit in reversed(bits):
        order = [index ^ bit for index in order] + order
    return order, bits


def pick_blocks(values, offsets):
    width = values.shape[1] // lax.axis_size("dp")
    me = lax.axis_index("dp")
    return jnp.concatenate(
        [
            lax.dynamic_slice_in_dim(values, (me ^ offset) * width, width, 1)
            for offset in offsets
        ],
        axis=1,
    )


def arrange_kernel(order, pair, width, me_ref, *refs):
    count = len(refs) // 2
    me = me_ref[0]
    half = refs[-1].shape[0]
    span = half_rows(me_ref[1], half)
    partner_ref = refs[-1]
    for index in range(count):
        value_ref, own_ref = refs[index], refs[count + index]
        base = index * len(order) * width
        for place, offset in enumerate(order):
            cols = pl.ds(pl.multiple_of((me ^ offset) * width, 128), width)
            own_ref[:, place * width : (place + 1) * width] = value_ref[:, cols].astype(bf16)
            cols = pl.ds(pl.multiple_of((me ^ offset ^ pair) * width, 128), width)
            start = base + place * width
            partner_ref[:, start : start + width] = value_ref[span, cols].astype(f32)


def arrange(pair, *arrays):
    size = lax.axis_size("dp")
    order, _ = halving_order(size, pair)
    tokens, model = arrays[0].shape
    width = model // size
    half = len(order) * width
    if width % 128:
        partner = [index ^ pair for index in order]
        start = lax.axis_index("tensor") % 2 * (tokens // 2)
        sent = [
            rows(pick_blocks(values, partner), start, tokens // 2).astype(f32) for values in arrays
        ]
        return [pick_blocks(values, order) for values in arrays] + [
            jnp.concatenate(sent, axis=1)
        ]
    vmem = pl.BlockSpec(memory_space=pltpu.VMEM)
    me = jnp.stack([lax.axis_index("dp"), lax.axis_index("tensor") % 2]).astype(jnp.int32)
    return pl.pallas_call(
        functools.partial(arrange_kernel, order, pair, width),
        in_specs=[pl.BlockSpec(memory_space=pltpu.SMEM)] + [vmem] * len(arrays),
        out_shape=[jax.ShapeDtypeStruct((tokens, half), bf16) for _ in arrays]
        + [jax.ShapeDtypeStruct((tokens // 2, half * len(arrays)), f32)],
        compiler_params=params,
        cost_estimate=cost(10**6, 8 * tokens * model),
        name="arrange",
    )(me, *arrays)


def pair_product_kernel(low, high, starts, blocks_first, core_ref, *refs):
    own_ref, got_ref, other_ref, side_ref, side_got_ref = refs[:5]
    out_ref, joined_ref = refs[-2:]
    half = got_ref.shape[0]
    tokens = 2 * half
    core = core_ref[0]
    joined_ref[half_rows(core, half), :] = got_ref[:, low:high].astype(bf16)
    joined_ref[half_rows(1 - core, half), :] = other_ref[:, low:high].astype(bf16)
    side_cols = side_ref.shape[1]
    chunk = 384 if side_cols % 384 == 0 else 512 if side_cols % 512 == 0 else side_cols
    added = refs[5 : 5 + len(starts)]
    for at in range(0, side_cols, chunk):
        cols = slice(at, at + chunk)
        total = None
        for block, ref in ((own_ref[:, low:high], side_ref), (joined_ref[...], side_got_ref)):
            side = ref[:tokens, cols].astype(bf16)
            if blocks_first:
                term = dot(block, side, (0, 0))
            else:
                term = dot(side, block, (0, 0))
            total = term if total is None else total + term
        for start, ref in zip(starts, added):
            if blocks_first:
                total = total + ref[low - start : high - start, cols]
            else:
                total = total + ref[cols, low - start : high - start]
        if blocks_first:
            out_ref[: high - low, cols] = total
        else:
            out_ref[cols, :] = total
    if side_ref.shape[0] > tokens:
        extra = side_ref[tokens:, :] + side_got_ref[tokens:, :]
        for ref in added:
            extra = extra + ref[ref.shape[0] - extra.shape[0] :, :]
        out_ref[high - low :, :] = extra


def pair_product(blocks, sides, low, high, received, blocks_first, ahead):
    width = high - low
    rows_in, side_cols = sides[0].shape
    tokens = blocks[0].shape[0]
    extra = rows_in - tokens
    core = (lax.axis_index("tensor") % 2).astype(jnp.int32).reshape(1)
    if low % 128 or high % 128 or any(start % 128 for start, _ in received):
        blocks = [block[:, low:high] for block in blocks]
        cut = []
        for start, values in received:
            if blocks_first:
                tail = values[values.shape[0] - extra :]
                values = jnp.concatenate([values[low - start : high - start], tail], axis=0)
            else:
                values = values[:, low - start : high - start]
            cut.append((0, values))
        received, low, high = cut, 0, width
    shape = (width + extra, side_cols) if blocks_first else (side_cols, width)
    starts = tuple(start for start, _ in received)
    (total,) = call(
        functools.partial(pair_product_kernel, low, high, starts, blocks_first),
        "pair_product",
        [(shape, f32)],
        (core, *blocks, *sides, *[value for _, value in received]),
        ahead,
        [((tokens, width), bf16)],
    )
    return total


def halving(blocks, sides, blocks_first, pair=1):
    order, bits = halving_order(lax.axis_size("dp"), pair)
    width = blocks[0].shape[1] // len(order)
    low, high = 0, len(order)
    received = []
    ahead = yield None
    for bit in bits + [0]:
        middle = (low + high) // 2 if bit else high
        value = pair_product(
            blocks, sides, low * width, middle * width, received, blocks_first, ahead or ()
        )
        got = value
        if bit:
            got = swap(value, "dp", bit)
            received.append((middle * width, got))
        low = middle
        ahead = yield value, got


def as_row(values):
    ones = jnp.ones((8, values.shape[1]), f32)
    return dot(ones, values, (1, 1), highest)[0:1]


def as_column(row):
    length = row.shape[1]
    down = lax.broadcasted_iota(jnp.int32, (length, length), 0)
    across = lax.broadcasted_iota(jnp.int32, (length, length), 1)
    return jnp.sum(jnp.where(down == across, row, 0.0), axis=1, keepdims=True)


def sum_column(refs):
    return as_column((refs[0][...] + refs[1][...]) + (refs[2][...] + refs[3][...]))


def conv_values(values, taps, positions):
    total = taps[4:5] + taps[0:1] * values
    for offset in range(1, 4):
        shifted = pltpu.roll(values, offset, 0)
        total = total + taps[offset : offset + 1] * jnp.where(positions >= offset, shifted, 0.0)
    return total


def conv_back(grad, values, taps, positions):
    total = taps[0:1] * grad
    tap_grads = [jnp.sum(grad * values, axis=0, keepdims=True)]
    for offset in range(1, 4):
        masked = jnp.where(positions >= offset, grad, 0.0)
        shifted = pltpu.roll(masked, masked.shape[0] - offset, 0)
        total = total + taps[offset : offset + 1] * shifted
        tap_grads.append(jnp.sum(shifted * values, axis=0, keepdims=True))
    tap_grads.append(jnp.sum(grad, axis=0, keepdims=True))
    return total, tap_grads


def scan_parts(step_in, decay_row, bias_row):
    raw = step_in + bias_row
    step = jnp.maximum(raw, 0.0) + jnp.log(1.0 + jnp.exp(-jnp.abs(raw)))
    rates = -jnp.exp(decay_row) * step
    length = rates.shape[0]
    row = lax.broadcasted_iota(jnp.int32, (length, length), 0)
    col = lax.broadcasted_iota(jnp.int32, (length, length), 1)
    lower = (row >= col).astype(f32)
    upper = (row <= col).astype(f32)
    cumulative = dot(lower, rates, (1, 0), highest)
    cumulative_t = dot(rates, upper, (0, 0), highest)
    return raw, step, rates, cumulative, cumulative_t, row >= col, upper


def scan_forward_kernel(
    zx_ref, bc_ref, dt_ref, taps_x_ref, taps_bc_ref, heads_ref, pos_ref, seg_col_ref, seg_row_ref,
    y_ref, gated_ref, square_ref, xa_ref, ba_ref,
):
    positions = pos_ref[...]
    conv_x = conv_values(zx_ref[1], taps_x_ref[...], positions)
    x_act = conv_x * sigmoid(conv_x)
    conv_bc = conv_values(bc_ref[...], taps_bc_ref[...], positions)
    bc_act = (conv_bc * sigmoid(conv_bc)).astype(bf16)
    state = bc_act.shape[1] // 2
    xa_ref[...] = x_act
    ba_ref[...] = bc_act
    heads = heads_ref[...]
    _, step, _, cumulative, cumulative_t, causal, _ = scan_parts(
        dt_ref[...], heads[0:1], heads[1:2]
    )
    inside = causal & (seg_col_ref[...] == seg_row_ref[...])
    gram = dot(bc_act[:, state:], bc_act[:, :state], (1, 1))
    length = positions.shape[0]
    lane = lax.broadcasted_iota(jnp.int32, (length, 128), 1)
    low_half = lane < 64
    square = jnp.zeros((length, 128), f32)
    for pair in range(x_act.shape[1] // 128):
        cols = slice(pair * 128, pair * 128 + 128)
        first, second = 2 * pair, 2 * pair + 1
        x_pair = x_act[:, cols]
        dt_pair = jnp.where(low_half, step[:, first : first + 1], step[:, second : second + 1])
        scaled = x_pair * dt_pair
        total = jnp.where(
            low_half, heads[2:3, first : first + 1], heads[2:3, second : second + 1]
        ) * x_pair
        for head, keep in ((first, low_half), (second, ~low_half)):
            gap = cumulative[:, head : head + 1] - cumulative_t[head : head + 1, :]
            mixing = gram * jnp.exp(jnp.where(inside, gap, -1e30))
            total = total + dot(
                mixing.astype(bf16), jnp.where(keep, scaled, 0.0).astype(bf16), (1, 0)
            )
        z_pair = zx_ref[0, :, cols]
        gated = total * (z_pair * sigmoid(z_pair))
        y_ref[:, cols] = total
        gated_ref[:, cols] = gated
        square = square + gated * gated
    square_ref[...] = as_row(square)


def scan_forward(*values):
    tokens, inner = values[0].shape[1:]
    wide = (tokens, inner)
    shapes = [(wide, f32), (wide, f32), ((1, tokens), f32), (wide, f32), (values[1].shape, bf16)]
    return call(scan_forward_kernel, "scan_forward", shapes, values)


def scan_backward_kernel(
    zx_ref, bc_ref, dt_ref, taps_x_ref, taps_bc_ref, heads_ref, pos_ref, seg_col_ref, seg_row_ref,
    y_ref, xa_ref, ba_ref, up_ref, scale_ref, gain_ref, cross_a, cross_b, cross_c, cross_d, *rest
):
    (
        z_cot_ref, x_cot_ref, bc_cot_ref, dt_cot_ref, taps_x_out, taps_bc_out, heads_out, gain_out
    ) = rest[-8:]
    inner_width = y_ref.shape[1] * 4
    positions = pos_ref[...]
    length = positions.shape[0]
    bc_act = ba_ref[...]
    state = bc_act.shape[1] // 2
    heads = heads_ref[...]
    raw, step, rates, cumulative, cumulative_t, causal, upper = scan_parts(
        dt_ref[...], heads[0:1], heads[1:2]
    )
    inside = causal & (seg_col_ref[...] == seg_row_ref[...])
    gram = dot(bc_act[:, state:], bc_act[:, :state], (1, 1))
    lane = lax.broadcasted_iota(jnp.int32, (length, 128), 1)
    low_half = lane < 64
    scale = scale_ref[...]
    cross = sum_column((cross_a, cross_b, cross_c, cross_d)) / inner_width
    pull = scale * scale * scale * cross
    gram_grad = jnp.zeros((length, length), f32)
    head_lane = lax.broadcasted_iota(jnp.int32, (length, HEAD_PAD), 1)
    head_row = lax.broadcasted_iota(jnp.int32, (HEAD_PAD, length), 0)
    head_one = lax.broadcasted_iota(jnp.int32, (1, HEAD_PAD), 1)
    step_grad = jnp.zeros((length, HEAD_PAD), f32)
    row_sums = jnp.zeros((length, HEAD_PAD), f32)
    col_sums = jnp.zeros((HEAD_PAD, length), f32)
    skip_grad = jnp.zeros((1, HEAD_PAD), f32)
    for pair in range(y_ref.shape[1] // 128):
        cols = slice(pair * 128, pair * 128 + 128)
        first, second = 2 * pair, 2 * pair + 1
        z_pair = zx_ref[0, :, cols]
        y_pair = y_ref[:, cols]
        gate = sigmoid(z_pair)
        silu = z_pair * gate
        gated = y_pair * silu
        up = up_ref[:, cols]
        gain_out[:, cols] = jnp.sum(up * gated * scale, axis=0, keepdims=True)
        gated_grad = scale * (up * gain_ref[:, cols]) - gated * pull
        z_cot_ref[:, cols] = rounded(gated_grad * y_pair * (gate * (1.0 + z_pair * (1.0 - gate))))
        y_grad = gated_grad * silu
        x_pair = xa_ref[:, cols]
        dt_pair = jnp.where(low_half, step[:, first : first + 1], step[:, second : second + 1])
        skip_pair = jnp.where(
            low_half, heads[2:3, first : first + 1], heads[2:3, second : second + 1]
        )
        scaled = (x_pair * dt_pair).astype(bf16)
        scaled_grad = jnp.zeros((length, 128), f32)
        skip_product = y_grad * x_pair
        for head, keep in ((first, low_half), (second, ~low_half)):
            gap = cumulative[:, head : head + 1] - cumulative_t[head : head + 1, :]
            decay = jnp.exp(jnp.where(inside, gap, -1e30))
            mixing = gram * decay
            y_head = jnp.where(keep, y_grad, 0.0).astype(bf16)
            mixing_grad = dot(y_head, scaled, (1, 1))
            scaled_grad = scaled_grad + dot(mixing.astype(bf16), y_head, (0, 0))
            gram_grad = gram_grad + mixing_grad * decay
            moved = mixing_grad * mixing
            row_sums = row_sums + jnp.where(
                head_lane == head, jnp.sum(moved, axis=1, keepdims=True), 0.0
            )
            col_sums = col_sums + jnp.where(
                head_row == head, jnp.sum(moved, axis=0, keepdims=True), 0.0
            )
        step_product = scaled_grad * x_pair
        for head, keep in ((first, low_half), (second, ~low_half)):
            step_grad = step_grad + jnp.where(
                head_lane == head,
                jnp.sum(jnp.where(keep, step_product, 0.0), axis=1, keepdims=True),
                0.0,
            )
            skip_sum = jnp.sum(
                jnp.sum(jnp.where(keep, skip_product, 0.0), axis=0, keepdims=True),
                axis=1,
                keepdims=True,
            )
            skip_grad = skip_grad + jnp.where(head_one == head, skip_sum, 0.0)
        x_grad = scaled_grad * dt_pair + skip_pair * y_grad
        conv_x = conv_values(zx_ref[1, :, cols], taps_x_ref[:, cols], positions)
        gate = sigmoid(conv_x)
        conv_grad = x_grad * (gate * (1.0 + conv_x * (1.0 - gate)))
        total, tap_grads = conv_back(
            conv_grad, zx_ref[1, :, cols], taps_x_ref[:, cols], positions
        )
        x_cot_ref[:, cols] = rounded(total)
        for index, value in enumerate(tap_grads):
            taps_x_out[index : index + 1, cols] = value
    rate_grad = dot(upper, row_sums, (1, 0), highest) - dot(upper, col_sums, (1, 1), highest)
    step_grad = step_grad - rate_grad * jnp.exp(heads[0:1])
    raw_grad = step_grad * sigmoid(raw)
    dt_cot_ref[...] = rounded(raw_grad)
    heads_out[0:1, :] = jnp.sum(rate_grad * rates, axis=0, keepdims=True)
    heads_out[1:2, :] = jnp.sum(raw_grad, axis=0, keepdims=True)
    heads_out[2:3, :] = skip_grad
    gram_low = gram_grad.astype(bf16)
    b_grad = dot(gram_low, bc_act[:, state:], (0, 0))
    c_grad = dot(gram_low, bc_act[:, :state], (1, 0))
    for part, grad in enumerate((b_grad, c_grad)):
        cols = slice(part * state, part * state + state)
        conv = conv_values(bc_ref[:, cols], taps_bc_ref[:, cols], positions)
        gate = sigmoid(conv)
        conv_grad = grad * (gate * (1.0 + conv * (1.0 - gate)))
        total, tap_grads = conv_back(conv_grad, bc_ref[:, cols], taps_bc_ref[:, cols], positions)
        bc_cot_ref[:, cols] = rounded(total)
        for index, value in enumerate(tap_grads):
            taps_bc_out[index : index + 1, cols] = value


def scan_backward(*values, ahead=()):
    zx, bc, dt, taps_x, taps_bc = values[:5]
    tokens, inner = zx.shape[1:]
    shapes = [
        (tokens, inner),
        (tokens, inner),
        bc.shape,
        dt.shape,
        taps_x.shape,
        taps_bc.shape,
        (3, HEAD_PAD),
        (1, inner),
    ]
    shapes = [(shape, f32) for shape in shapes]
    return call(scan_backward_kernel, "scan_backward", shapes, values, ahead)


def turn(values, cosine, sine, low_quarter):
    width = values.shape[1]
    partner = jnp.where(
        low_quarter, pltpu.roll(values, width - HD // 2, 1), pltpu.roll(values, HD // 2, 1)
    )
    return values * cosine + partner * sine


def masked_scores(q_head, kv, allowed):
    scores = dot(q_head, kv, (1, 1)) * HD ** (-0.5)
    return jnp.where(allowed, scores, -1e30)


def softmax(scores):
    exponent = jnp.exp(scores - jnp.max(scores, axis=1, keepdims=True))
    return exponent * (1.0 / jnp.sum(exponent, axis=1, keepdims=True))


def attention_masks(length, seg_col_ref, seg_row_ref):
    row = lax.broadcasted_iota(jnp.int32, (length, length), 0)
    col = lax.broadcasted_iota(jnp.int32, (length, length), 1)
    allowed = (col <= row) & (seg_col_ref[...] == seg_row_ref[...])
    lane = lax.broadcasted_iota(jnp.int32, (length, 2 * HD), 1)
    return allowed, lane < HD, (lane % HD) < HD // 2


def to_low(values, head):
    return values if head == 0 else pltpu.roll(values, HD, 1)


def to_high(values, head):
    return values if head == 1 else pltpu.roll(values, HD, 1)


def attention_forward_kernel(
    head_ref, q_ref, kv_ref, cos_ref, sin_ref, seg_col_ref, seg_row_ref, q_out, kv_out, attn_out
):
    length = q_ref.shape[0]
    allowed, low_half, low_quarter = attention_masks(length, seg_col_ref, seg_row_ref)
    cosine, sine = cos_ref[...], sin_ref[...]
    q_rot = rounded(turn(q_ref[...], cosine, sine, low_quarter))
    first = head_ref[0] == 0
    keys = jnp.where(first, kv_ref[0], pltpu.roll(kv_ref[0], HD, 1))
    kv_in = jnp.where(low_half, keys, jnp.where(first, pltpu.roll(kv_ref[1], HD, 1), kv_ref[1]))
    kv = jnp.where(low_half, turn(kv_in, cosine, sine, low_quarter), kv_in).astype(bf16)
    q_out[...] = q_rot
    kv_out[...] = kv
    parts = []
    for head in range(2):
        q_head = jnp.where(low_half, to_low(q_rot, head), 0.0).astype(bf16)
        probability = softmax(masked_scores(q_head, kv, allowed)).astype(bf16)
        parts.append(dot(probability, kv, (1, 0)))
    attn_out[...] = rounded(jnp.where(low_half, pltpu.roll(parts[0], HD, 1), parts[1]))


def attention_forward(*values):
    shape = values[1].shape
    shapes = [(shape, f32), (shape, bf16), (shape, f32)]
    return call(attention_forward_kernel, "attention_forward", shapes, values)


def attention_backward_kernel(
    head_ref, q_ref, kv_ref, grad_ref, cos_ref, sin_ref, seg_col_ref, seg_row_ref, *rest
):
    q_cot, kv_cot = rest[-2:]
    length = q_ref.shape[0]
    allowed, low_half, low_quarter = attention_masks(length, seg_col_ref, seg_row_ref)
    cosine, sine = cos_ref[...], -sin_ref[...]
    q_rot, kv = q_ref[...], kv_ref[...]
    grad = rounded(grad_ref[...])
    parts = []
    kv_grad = jnp.zeros((length, 2 * HD), f32)
    for head in range(2):
        q_head = jnp.where(low_half, to_low(q_rot, head), 0.0)
        probability = softmax(masked_scores(q_head.astype(bf16), kv, allowed))
        g_head = jnp.where(low_half, 0.0, to_high(grad, head)).astype(bf16)
        prob_grad = dot(g_head, kv, (1, 1))
        inner = jnp.sum(probability * prob_grad, axis=1, keepdims=True)
        score_grad = (probability * (prob_grad - inner)).astype(bf16)
        parts.append(dot(score_grad, kv, (1, 0)) * HD ** (-0.5))
        kv_grad = kv_grad + dot(score_grad, (q_head * HD ** (-0.5)).astype(bf16), (0, 0))
        kv_grad = kv_grad + dot(probability.astype(bf16), g_head, (0, 0))
    q_grad = jnp.where(low_half, parts[0], pltpu.roll(parts[1], HD, 1))
    q_cot[...] = rounded(turn(q_grad, cosine, sine, low_quarter))
    kv_grad = rounded(jnp.where(low_half, turn(kv_grad, cosine, sine, low_quarter), kv_grad))
    turned = pltpu.roll(kv_grad, HD, 1)
    first = head_ref[0] == 0
    kept = low_half == first
    kv_cot[:, : 2 * HD] = jnp.where(kept, jnp.where(first, kv_grad, turned), 0.0)
    kv_cot[:, 2 * HD :] = jnp.where(kept, jnp.where(first, turned, kv_grad), 0.0)


def attention_backward(*values, ahead=()):
    shape = values[1].shape
    shapes = [(shape, f32), ((shape[0], KVH * 2 * HD), f32)]
    return call(attention_backward_kernel, "attention_backward", shapes, values, ahead)


def mix_kernel(
    core_ref, gated_ref, gain_ref, attn_ref, out_w_ref, o_w_ref, sq_a, sq_b, sq_c, sq_d, *rest
):
    mixed_ref, scale_ref, other_ref = rest[-3:]
    inner = gated_ref.shape[1]
    half = gated_ref.shape[0] // 2
    scale = lax.rsqrt(sum_column((sq_a, sq_b, sq_c, sq_d)) / (4 * inner) + epsilon)
    scale_ref[...] = scale
    mixed_ref[:, :inner] = rounded(gated_ref[...] * scale * gain_ref[...])
    mixed_ref[:, inner:] = attn_ref[...]
    other_ref[...] = mix_product(mixed_ref, out_w_ref, o_w_ref, half_rows(1 - core_ref[0], half))


def mix_product(mixed_ref, out_w_ref, o_w_ref, span):
    inner = out_w_ref.shape[0]
    part = mixed_ref[span, :].astype(bf16)
    return dot(part[:, :inner], out_w_ref[...], (1, 0)) + dot(part[:, inner:], o_w_ref[...], (1, 0))


def mix_mine_kernel(core_ref, mixed_ref, out_w_ref, o_w_ref, got_ref, mine_ref):
    half = got_ref.shape[0]
    span = half_rows(core_ref[0], half)
    mine_ref[...] = mix_product(mixed_ref, out_w_ref, o_w_ref, span) + got_ref[...]


def feed_product(gate_cot_ref, up_cot_ref, gu_ref, span):
    gate_part = gate_cot_ref[span, :].astype(bf16)
    up_part = up_cot_ref[span, :].astype(bf16)
    return dot(gate_part, gu_ref[0], (1, 1)) + dot(up_part, gu_ref[1], (1, 1))


def feed_kernel(core_ref, mine_ref, got_ref, in_ref, gain_ref, act_grad_ref, gu_ref, *rest):
    resid_ref, scale_ref, normed_ref, act_ref, gate_cot_ref, up_cot_ref, other_ref = rest[-7:]
    core = core_ref[0]
    half = mine_ref.shape[0]
    for which, ref in ((core, mine_ref), (1 - core, got_ref)):
        span = half_rows(which, half)
        resid_ref[span, :] = in_ref[span, :].astype(f32) + ref[...]
    resid = resid_ref[...]
    scale = rms_scale(resid)
    scale_ref[...] = scale
    normed_ref[...] = (resid * scale * gain_ref[...]).astype(bf16)
    normed = normed_ref[...]
    hidden = gu_ref.shape[2]
    for start in range(0, hidden, 256):
        cols = slice(start, start + 256)
        gate = dot(normed, gu_ref[0, :, cols], (1, 0))
        up = dot(normed, gu_ref[1, :, cols], (1, 0))
        slope = sigmoid(gate)
        silu = gate * slope
        act_ref[:, cols] = rounded(silu * up)
        act_grad = act_grad_ref[:, cols]
        gate_cot_ref[:, cols] = rounded(act_grad * up * slope * (1.0 + gate * (1.0 - slope)))
        up_cot_ref[:, cols] = rounded(act_grad * silu)
    other_ref[...] = feed_product(gate_cot_ref, up_cot_ref, gu_ref, half_rows(1 - core, half))


def feed_mine_kernel(core_ref, gate_cot_ref, up_cot_ref, gu_ref, got_ref, *rest):
    span = half_rows(core_ref[0], got_ref.shape[0])
    rest[-1][...] = feed_product(gate_cot_ref, up_cot_ref, gu_ref, span) + got_ref[...]


def mix_back_kernel(
    core_ref, mine_ref, got_ref, resid_ref, scale_ref, gain_ref, out_grad_ref, out_w_ref, o_w_ref,
    gated_ref, gated_gain_ref, *rest,
):
    grad_ref, mix_ref, gain_grad_ref, up_ref, attn_grad_ref, cross_ref = rest[-6:]
    core = core_ref[0]
    half = mine_ref.shape[0]
    for which, ref in ((core, mine_ref), (1 - core, got_ref)):
        grad_ref[half_rows(which, half), :] = ref[...]
    normed_grad = grad_ref[...]
    resid = resid_ref[...]
    scale = scale_ref[...]
    gain_grad_ref[...] = jnp.sum(normed_grad * resid * scale, axis=0, keepdims=True)
    weighted = normed_grad * gain_ref[...]
    mean = jnp.mean(weighted * resid, axis=1, keepdims=True)
    resid_grad = (
        out_grad_ref[...].astype(f32) + scale * weighted - resid * (scale * scale * scale * mean)
    )
    grad_ref[...] = resid_grad
    mix = resid_grad.astype(bf16)
    mix_ref[...] = mix
    up = dot(mix, out_w_ref[...], (1, 1))
    up_ref[...] = up
    attn_grad_ref[...] = dot(mix, o_w_ref[...], (1, 1))
    cross_ref[...] = as_row(up * gated_gain_ref[...] * gated_ref[...])


def call_dense(kernel, name, shapes, core, values, ahead=(), scratch=()):
    scratch = [(shape, f32) for shape in scratch]
    return call(kernel, name, shapes, (core, *values), ahead, scratch)


def chunks(values):
    return [
        (value, row, start)
        for value in values
        for row in range(value.shape[0])
        for start in range(0, value.shape[1], 128)
    ]


def pick(index, blocks):
    total = blocks[0]
    for place in range(1, len(blocks)):
        total = jnp.where(index == place, blocks[place], total)
    return total


def shared_blocks(bc_ref, kv_ref):
    return [ref[:, at : at + 128] for ref in (bc_ref, kv_ref) for at in (0, 128)]


def post_kernel(core_ref, me_ref, grad_ref, in_ref, taps_ref, bc_ref, kv_ref, *rest):
    mine_ref, other_ref, near_ref, state_ref = rest[-4:]
    half = mine_ref.shape[0]
    tokens = 2 * half
    mine_ref[...] = grad_ref[half_rows(core_ref[0], half), :]
    other_ref[...] = grad_ref[half_rows(1 - core_ref[0], half), :]
    inputs = in_ref[...].astype(f32)
    gain = jnp.sum(grad_ref[...] * inputs * rms_scale(inputs), axis=0, keepdims=True)
    state_ref[...] = jnp.zeros_like(state_ref)
    for at, (value, row, start) in enumerate(chunks((gain, taps_ref[...]))):
        state_ref[at : at + 1, :] = value[row : row + 1, start : start + 128]
    blocks = shared_blocks(bc_ref, kv_ref)
    near_ref[:tokens, :] = pick(me_ref[0] ^ 1, blocks)
    near_ref[tokens : 2 * tokens, :] = pick(me_ref[0] ^ 3, blocks)
    near_ref[2 * tokens :, :] = state_ref[...]


def share_kernel(core_ref, me_ref, near_ref, bc_ref, kv_ref, state_ref, far_ref):
    tokens = bc_ref.shape[0]
    blocks = shared_blocks(bc_ref, kv_ref)
    far_ref[:tokens, :] = pick(me_ref[0] ^ 2, blocks) + near_ref[tokens : 2 * tokens, :]
    far_ref[tokens:, :] = state_ref[...] + near_ref[2 * tokens :, :]


def few_kernel(
    core_ref, me_ref, near_ref, far_own_ref, far_ref, bc_ref, kv_ref, q_ref, dt_ref, gain_two_ref,
    taps_ref, gain_ref, heads_ref, *rest
):
    few_ref = rest[-1]
    tokens = bc_ref.shape[0]
    blocks = shared_blocks(bc_ref, kv_ref)
    few_ref[:tokens, :128] = q_ref[...]
    few_ref[:tokens, 128:256] = (
        pick(me_ref[0], blocks) + near_ref[:tokens, :] + far_ref[:tokens, :]
    )
    few_ref[:tokens, 256:] = dt_ref[...]
    state = far_own_ref[tokens:, :] + far_ref[tokens:, :]
    used = STATE_ROWS
    few_ref[tokens:, :] = jnp.zeros((few_ref.shape[0] - tokens, few_ref.shape[1]), f32)
    values = (state[:used], gain_two_ref[...], taps_ref[...], gain_ref[...], heads_ref[...])
    for at, (value, row, start) in enumerate(chunks(values)):
        place = tokens + at // 3
        cols = slice(at % 3 * 128, at % 3 * 128 + 128)
        few_ref[place : place + 1, cols] = value[row : row + 1, start : start + 128]


def unpack_kernel(core_ref, few_ref, own_ref, *refs):
    rows_out = own_ref.shape[0]
    own_ref[...] = few_ref[:rows_out, 128:256]
    for at, (ref, row, start) in enumerate(chunks(refs)):
        place = rows_out + at // 3
        cols = slice(at % 3 * 128, at % 3 * 128 + 128)
        ref[row : row + 1, start : start + 128] = few_ref[place : place + 1, cols]


def assemble_kernel(core_ref, me_ref, own_ref, near_ref, far_ref, far_near_ref, bc_ref, *kv_refs):
    blocks = (own_ref[...], near_ref[...], far_ref[...], far_near_ref[...])
    for place in range(4):
        value = pick(me_ref[0] ^ place, blocks)
        if place < 2:
            bc_ref[:, place * 128 : place * 128 + 128] = value
        else:
            kv_refs[place - 2][...] = value


def input_grad_kernel(core_ref, mine_ref, got_ref, grad_ref, in_ref, gain_ref, out_ref, full_ref):
    half = mine_ref.shape[0]
    full_ref[half_rows(core_ref[0], half), :] = mine_ref[...]
    full_ref[half_rows(1 - core_ref[0], half), :] = got_ref[...]
    inputs = in_ref[...].astype(f32)
    scale = rms_scale(inputs)
    weighted = full_ref[...] * gain_ref[...]
    mean = jnp.mean(weighted * inputs, axis=1, keepdims=True)
    total = grad_ref[...] + scale * weighted - inputs * (scale * scale * scale * mean)
    out_ref[...] = total.astype(bf16)


def layer_out_kernel(core_ref, mine_ref, got_ref, resid_ref, out_ref, full_ref):
    half = mine_ref.shape[0]
    full_ref[half_rows(core_ref[0], half), :] = mine_ref[...]
    full_ref[half_rows(1 - core_ref[0], half), :] = got_ref[...]
    out_ref[...] = (resid_ref[...] + full_ref[...]).astype(bf16)


def rotary_tables(positions):
    half = HD // 2
    frequency = rope_base ** (-jnp.arange(half, dtype=f32) / half)
    angles = positions.astype(f32)[:, None] * frequency[None, :]
    cosine, sine = jnp.cos(angles), jnp.sin(angles)
    return (
        jnp.concatenate([cosine] * 4, axis=1),
        jnp.concatenate([-sine, sine, -sine, sine], axis=1),
    )


def on_device(
    hidden,
    positions,
    out_grad,
    norm_one,
    zx_weight,
    bc_weight,
    dt_weight,
    conv_inner,
    conv_state,
    decay_log,
    dt_bias,
    skip_gain,
    gated_gain,
    out_weight,
    q_weight,
    kv_weight,
    o_weight,
    norm_two,
    gu_weight,
    down_weight,
):
    tokens, model = hidden.shape
    head_count = dt_weight.shape[1]
    inner_cols = conv_inner.shape[1]
    hidden_cols = gu_weight.shape[2]
    query_cols = q_weight.shape[1]
    segment = jnp.cumsum((positions == 0).astype(jnp.int32), dtype=jnp.int32)
    seg_col, seg_row, pos_col = segment[:, None], segment[None, :], positions[:, None]
    cosine, sine = rotary_tables(positions)
    head_pad = ((0, 0), (0, HEAD_PAD - head_count))
    heads = jnp.pad(jnp.stack([decay_log, dt_bias, skip_gain]), head_pad)
    dt_wide = jnp.pad(dt_weight, head_pad)

    core = lax.axis_index("tensor").astype(jnp.int32) % 2
    core_arg = core.reshape(1)
    kv_head = (lax.axis_index("tensor") * (query_cols // HD) // (QH // KVH)).astype(jnp.int32)
    kv_head = kv_head.reshape(1)
    half = tokens // 2
    half_model = model // 2
    wide = (tokens, model)
    half_wide = (half, model)

    inputs = hidden.astype(f32)
    scale_one = rms_scale(inputs)
    normed = (inputs * scale_one * norm_one).astype(bf16)
    own_normed, normed_sent = arrange(1, normed)
    normed_pair = (own_normed, *swap_shared(normed_sent, 1))
    own_out, out_sent = arrange(2, out_grad)
    out_pair = (own_out, *swap_shared(out_sent, 2))

    proj_zx = jnp.einsum("td,dkc->ktc", normed, zx_weight, preferred_element_type=f32)
    proj_bc = dot(normed, bc_weight, (1, 0))
    proj_dt = dot(normed, dt_wide, (1, 0))
    scan_args = (
        proj_zx, proj_bc, proj_dt, conv_inner, conv_state, heads, pos_col, seg_col, seg_row
    )
    y, gated, square, x_act, bc_act = scan_forward(*scan_args)
    squares = spread_tensor(square)

    query = dot(normed, q_weight, (1, 0))
    key_value = jnp.einsum("td,dkc->ktc", normed, kv_weight, preferred_element_type=f32)
    q_rot, kv_rot, attn = attention_forward(
        kv_head, query, key_value, cosine, sine, seg_col, seg_row
    )
    act_grad = dot(out_grad, down_weight, (1, 1))
    gu_split = gu_weight.transpose(1, 0, 2)

    gain_row = gated_gain[None, :]
    mixed, gate_scale, other = call_dense(
        mix_kernel,
        "mix",
        [((tokens, inner_cols + query_cols), f32), ((tokens, 1), f32), (half_wide, f32)],
        core_arg,
        (gated, gain_row, attn, out_weight, o_weight, *squares),
        (normed_pair[1],),
    )
    mixed_got = swap(mixed, "dp", 1)
    mixed_pair = (mixed, mixed_got)
    (mine,) = call_dense(
        mix_mine_kernel,
        "mix_mine",
        [(half_wide, f32)],
        core_arg,
        (mixed, out_weight, o_weight, swap(other, "tensor", 1)),
    )
    resid, scale_two, normed_two, act, gate_cot, up_cot, other = call_dense(
        feed_kernel,
        "feed",
        [
            (wide, f32),
            ((tokens, 1), f32),
            (wide, bf16),
            ((tokens, hidden_cols), f32),
            ((tokens, hidden_cols), f32),
            ((tokens, hidden_cols), f32),
            (half_wide, f32),
        ],
        core_arg,
        (
            *tensor_halves(mine, (out_pair[1], mixed_got, act_grad, gu_split)),
            hidden,
            norm_two[None, :],
            act_grad,
            gu_split,
        ),
    )
    (mine,) = call_dense(
        feed_mine_kernel,
        "feed_mine",
        [(half_wide, f32)],
        core_arg,
        (gate_cot, up_cot, gu_split, swap(other, "tensor", 1)),
    )
    act_got = swap(act, "dp", 2)
    own_up, sent_up = arrange(1, normed_two)
    two_up = swap_shared(sent_up, 1)
    own_gate, sent_gate = arrange(2, normed_two)
    two_gate = swap_shared(sent_gate, 2)
    up_got = swap(up_cot, "dp", 1)
    gate_got = swap(gate_cot, "dp", 2)
    down_stages = halving(out_pair, (act, act_got), False, 2)
    gate_stages = halving((own_gate, *two_gate), (gate_cot, gate_got), True, 2)
    up_stages = halving((own_up, *two_up), (up_cot, up_got), True)
    for stages in (down_stages, gate_stages, up_stages):
        next(stages)
    halves = tensor_halves(mine, (act_got, *two_up, *two_gate, up_got))
    up_first, up_one = up_stages.send((halves[0],))
    resid_grad, mix_grad, norm_two_grad, up, attn_grad, cross = call_dense(
        mix_back_kernel,
        "mix_back",
        [
            (wide, f32),
            (wide, bf16),
            ((1, model), f32),
            ((tokens, inner_cols), f32),
            ((tokens, query_cols), f32),
            ((1, tokens), f32),
        ],
        core_arg,
        (
            *halves,
            resid,
            scale_two,
            norm_two[None, :],
            out_grad,
            out_weight,
            o_weight,
            gated,
            gain_row,
        ),
        (up_first,),
    )
    own_mix, sent_mix = arrange(1, mix_grad)
    mix_pair = (own_mix, *swap_shared(sent_mix, 1))
    crosses = spread_tensor(cross)
    last, gate_one = gate_stages.send((up,))
    q_cot, kv_cot = attention_backward(
        kv_head, q_rot, kv_rot, attn_grad, cosine, sine, seg_col, seg_row, ahead=(last, own_mix)
    )

    mix_stages = halving(mix_pair, mixed_pair, False)
    next(mix_stages)
    act_b = act.astype(bf16)
    mlp_other = dot(rows(act_b, (1 - core) * half, half), down_weight, (1, 0))
    mlp_mine = dot(rows(act_b, core * half, half), down_weight, (1, 0)) + swap(
        mlp_other, "tensor", 1
    )

    z_cot, x_cot, bc_cot, dt_cot, taps_x_grad, taps_bc_grad, heads_grad, gain_grad = scan_backward(
        *scan_args, y, x_act, bc_act, up, gate_scale, gain_row, *crosses, ahead=(q_cot,)
    )

    zx_cot = jnp.stack([z_cot, x_cot], axis=1).astype(bf16)
    normed_grad = (
        jnp.einsum("tkc,dkc->td", zx_cot, zx_weight, preferred_element_type=f32)
        + dot(bc_cot.astype(bf16), bc_weight, (1, 1))
        + dot(dt_cot.astype(bf16), dt_wide, (1, 1))
        + dot(q_cot.astype(bf16), q_weight, (1, 1))
        + jnp.einsum(
            "tkc,dkc->td",
            kv_cot.astype(bf16).reshape(tokens, 2, KVH * HD),
            kv_weight,
            preferred_element_type=f32,
        )
    )
    me_arg = lax.axis_index("tensor").astype(jnp.int32).reshape(1)
    normed_mine, normed_other, near, state_part = call_dense(
        post_kernel,
        "post",
        [
            (half_wide, f32),
            (half_wide, f32),
            ((2 * tokens + STATE_PAD, 128), f32),
            ((STATE_PAD, 128), f32),
        ],
        core_arg,
        (me_arg, normed_grad, hidden, taps_bc_grad, bc_cot, kv_cot),
        (mix_pair[1],),
    )
    zx_own = jnp.concatenate([z_cot, x_cot], axis=1)
    zx_got = swap(zx_own, "dp", 1)
    zx_stages = halving(normed_pair, (zx_own, zx_got), True)
    near = swap(near, "tensor", 1)
    (far_own,) = call_dense(
        share_kernel,
        "share",
        [((tokens + STATE_PAD, 128), f32)],
        core_arg,
        (me_arg, near, bc_cot, kv_cot, state_part),
    )
    far = swap(far_own, "tensor", 2)
    (few,) = call_dense(
        few_kernel,
        "few",
        [((tokens + SMALL_ROWS, 384), f32)],
        core_arg,
        (
            me_arg, near, far_own, far, bc_cot, kv_cot, q_cot, dt_cot, norm_two_grad, taps_x_grad,
            gain_grad, heads_grad,
        ),
    )
    few_got = swap(few, "dp", 1)
    few_stages = halving(normed_pair, (few, few_got), True)
    next(zx_stages)
    next(few_stages)
    normed_mine = normed_mine + swap(normed_other, "tensor", 1)

    gots = {"up": [up_one], "gate": [gate_one]}
    totals = {}
    stage_list = {
        "down": down_stages,
        "gate": gate_stages,
        "up": up_stages,
        "mix": mix_stages,
        "zx": zx_stages,
        "few": few_stages,
    }

    def advance(name, *ahead):
        value, got = stage_list[name].send(ahead)
        gots.setdefault(name, []).append(got)
        totals[name] = value
        return value

    last = advance("up", x_cot)
    last = advance("mix", last, far_own)
    last = advance("gate", last, zx_got)
    last = advance("zx", last)
    last = advance("mix", last, few)
    last = advance("few", last)
    last = advance("down", last)
    last = advance("up", last)
    last = advance("gate", last)
    last = advance("zx", last)
    last = advance("few", last)
    normed_mine, normed_other = tensor_halves(normed_mine, (last,))
    last = normed_mine
    last = advance("down", last)
    last = advance("mix", last)
    last = advance("zx", last)
    last = advance("few", last)
    last = advance("down", last)
    (input_grad,) = call_dense(
        input_grad_kernel,
        "input_grad",
        [(wide, bf16)],
        core_arg,
        (normed_mine, normed_other, resid_grad, hidden, norm_one[None, :]),
        scratch=(wide,),
    )
    (layer_out,) = call_dense(
        layer_out_kernel,
        "layer_out",
        [(wide, bf16)],
        core_arg,
        (*tensor_halves(mlp_mine, (x_cot,)), resid),
        scratch=(wide,),
    )
    for name, stages in stage_list.items():
        for value, _ in stages:
            totals[name] = value
    down_shard, mixed_shard = totals["down"], totals["mix"]
    out_shard, o_shard = mixed_shard[:inner_cols], mixed_shard[inner_cols:]
    gu_shard = jnp.stack([totals["gate"], totals["up"]], axis=1)
    zx_shard = totals["zx"].reshape(-1, 2, inner_cols)
    few_shard = totals["few"]
    shard_rows = model // lax.axis_size("dp")
    q_shard = few_shard[:shard_rows, :query_cols]
    dt_shard = few_shard[:shard_rows, 256 : 256 + head_count]
    own, norm_one_grad, state_grad, norm_two_grad, inner_grad, gain_grad, heads_grad = call_dense(
        unpack_kernel,
        "unpack",
        [
            ((shard_rows, 128), f32),
            ((1, model), f32),
            (conv_state.shape, f32),
            ((1, model), f32),
            (conv_inner.shape, f32),
            ((1, inner_cols), f32),
            ((3, HEAD_PAD), f32),
        ],
        core_arg,
        (few_shard,),
    )
    head_sums = heads_grad[:, :head_count]
    near = swap(own, "tensor", 1)
    bc_shard, *kv_parts = call_dense(
        assemble_kernel,
        "assemble",
        [((shard_rows, 256), f32), ((shard_rows, 128), f32), ((shard_rows, 128), f32)],
        core_arg,
        (me_arg, own, near, swap(own, "tensor", 2), swap(own, "tensor", 3)),
    )
    kv_shard = jnp.stack(kv_parts, axis=1)
    return (
        layer_out,
        input_grad,
        norm_one_grad.reshape(-1),
        zx_shard,
        bc_shard,
        dt_shard,
        inner_grad,
        state_grad,
        head_sums[0],
        head_sums[1],
        head_sums[2],
        gain_grad.reshape(-1),
        out_shard,
        q_shard,
        kv_shard,
        o_shard,
        norm_two_grad.reshape(-1),
        gu_shard,
        down_shard,
    )


def solution(mesh):
    placed = (
        P("dp", None),
        P("dp"),
        P("dp", None),
        P(),
        P(None, None, "tensor"),
        P(),
        P(None, "tensor"),
        P(None, "tensor"),
        P(),
        P("tensor"),
        P("tensor"),
        P("tensor"),
        P("tensor"),
        P("tensor", None),
        P(None, "tensor"),
        P(),
        P("tensor", None),
        P(),
        P(None, None, "tensor"),
        P("tensor", None),
    )
    return jax.shard_map(
        on_device,
        mesh=mesh,
        in_specs=placed,
        out_specs=(
            P("dp", None),
            P("dp", None),
            P(),
            P("dp", None, "tensor"),
            P("dp", None),
            P("dp", "tensor"),
            P(None, "tensor"),
            P(),
            P("tensor"),
            P("tensor"),
            P("tensor"),
            P("tensor"),
            P("tensor", "dp"),
            P("dp", "tensor"),
            P("dp", None, None),
            P("tensor", "dp"),
            P(),
            P("dp", None, "tensor"),
            P("tensor", "dp"),
        ),
        check_vma=False,
    )
```

```python
import functools

import jax
import jax.numpy as jnp
from jax import lax
from jax.experimental import pallas as pl
from jax.experimental.pallas import tpu as pltpu
from jax.sharding import PartitionSpec as P

QH = 8
KVH = 2
HD = 64
HEAD_PAD = 128
STATE_ROWS = 18
STATE_PAD = 24
SMALL_ROWS = 48
COST = 3 * 10**9

epsilon = 1e-05
rope_base = 10000.0
highest = lax.Precision.HIGHEST
bf16 = jnp.bfloat16
f32 = jnp.float32
params = pltpu.CompilerParams(vmem_limit_bytes=40 * 1024 * 1024)


def dot(left, right, dims, precision=None):
    return lax.dot_general(
        left,
        right,
        ((dims[:1], dims[1:]), ((), ())),
        precision=precision,
        preferred_element_type=f32,
    )


def rms_scale(values):
    return lax.rsqrt(jnp.mean(values * values, axis=-1, keepdims=True) + epsilon)


def sigmoid(values):
    return 1.0 / (1.0 + jnp.exp(-values))


def rounded(values):
    return values.astype(bf16).astype(f32)


def cost(flops, read, exps=0):
    return pl.CostEstimate(flops=COST, bytes_accessed=10**6, transcendentals=0)


def call(kernel, name, out_shapes, values, ahead=(), scratch=(), flops=10**6):
    def place(value):
        if value.dtype == jnp.int32 and value.size == 1:
            return pl.BlockSpec(memory_space=pltpu.SMEM)
        return whole(value)

    def whole(value):
        zeros = (0,) * len(value.shape)
        return pl.BlockSpec(value.shape, lambda step: zeros)

    shapes = [jax.ShapeDtypeStruct(shape, kind) for shape, kind in out_shapes]
    return pl.pallas_call(
        kernel,
        grid=(1,),
        in_specs=[place(value) for value in values]
        + [pl.BlockSpec(memory_space=pl.ANY)] * len(ahead),
        out_specs=[whole(shape) for shape in shapes],
        out_shape=shapes,
        scratch_shapes=[pltpu.VMEM(shape, kind) for shape, kind in scratch],
        compiler_params=params,
        cost_estimate=cost(flops, flops),
        name=name,
    )(*values, *ahead)


def swap(values, axis, mask):
    pairs = [(index, index ^ mask) for index in range(lax.axis_size(axis))]
    return lax.ppermute(values, axis, pairs)


def spread_tensor(values):
    return [values] + [swap(values, "tensor", mask) for mask in (1, 2, 3)]


def add_spread(parts):
    return (parts[0] + parts[1]) + (parts[2] + parts[3])


def add_kernel(left_ref, right_ref, *rest):
    rest[-1][...] = left_ref[...] + right_ref[...]


def tensor_halves(mine, ahead=()):
    values = (mine, swap(mine, "tensor", 2))
    (mine,) = call(add_kernel, "add_halves", [(mine.shape, f32)], values, ahead)
    return mine, swap(mine, "tensor", 1)


def swap_shared(values, mask):
    first = swap(values, "dp", mask)
    return first, swap(first, "tensor", 1)


def rows(values, start, size):
    return lax.dynamic_slice_in_dim(values, start, size, 0)


def half_rows(core, size):
    return pl.ds(pl.multiple_of(core * size, size), size)


def halving_order(size, pair):
    order, bits, bit = [0], [], 1
    while bit < size:
        if bit != pair:
            bits.append(bit)
        bit *= 2
    for bit in reversed(bits):
        order = [index ^ bit for index in order] + order
    return order, bits


def pick_blocks(values, offsets):
    width = values.shape[1] // lax.axis_size("dp")
    me = lax.axis_index("dp")
    return jnp.concatenate(
        [
            lax.dynamic_slice_in_dim(values, (me ^ offset) * width, width, 1)
            for offset in offsets
        ],
        axis=1,
    )


def arrange_kernel(order, pair, width, me_ref, *refs):
    count = len(refs) // 2
    me = me_ref[0]
    half = refs[-1].shape[0]
    span = half_rows(me_ref[1], half)
    partner_ref = refs[-1]
    for index in range(count):
        value_ref, own_ref = refs[index], refs[count + index]
        base = index * len(order) * width
        for place, offset in enumerate(order):
            cols = pl.ds(pl.multiple_of((me ^ offset) * width, 128), width)
            own_ref[:, place * width : (place + 1) * width] = value_ref[:, cols].astype(bf16)
            cols = pl.ds(pl.multiple_of((me ^ offset ^ pair) * width, 128), width)
            start = base + place * width
            partner_ref[:, start : start + width] = value_ref[span, cols].astype(f32)


def arrange(pair, *arrays):
    size = lax.axis_size("dp")
    order, _ = halving_order(size, pair)
    tokens, model = arrays[0].shape
    width = model // size
    half = len(order) * width
    if width % 128:
        partner = [index ^ pair for index in order]
        start = lax.axis_index("tensor") % 2 * (tokens // 2)
        sent = [
            rows(pick_blocks(values, partner), start, tokens // 2).astype(f32) for values in arrays
        ]
        return [pick_blocks(values, order) for values in arrays] + [
            jnp.concatenate(sent, axis=1)
        ]
    vmem = pl.BlockSpec(memory_space=pltpu.VMEM)
    me = jnp.stack([lax.axis_index("dp"), lax.axis_index("tensor") % 2]).astype(jnp.int32)
    return pl.pallas_call(
        functools.partial(arrange_kernel, order, pair, width),
        in_specs=[pl.BlockSpec(memory_space=pltpu.SMEM)] + [vmem] * len(arrays),
        out_shape=[jax.ShapeDtypeStruct((tokens, half), bf16) for _ in arrays]
        + [jax.ShapeDtypeStruct((tokens // 2, half * len(arrays)), f32)],
        compiler_params=params,
        cost_estimate=cost(10**6, 8 * tokens * model),
        name="arrange",
    )(me, *arrays)


def pair_product_kernel(low, high, starts, blocks_first, core_ref, *refs):
    own_ref, got_ref, other_ref, side_ref, side_got_ref = refs[:5]
    out_ref, joined_ref = refs[-2:]
    half = got_ref.shape[0]
    tokens = 2 * half
    core = core_ref[0]
    joined_ref[half_rows(core, half), :] = got_ref[:, low:high].astype(bf16)
    joined_ref[half_rows(1 - core, half), :] = other_ref[:, low:high].astype(bf16)
    side_cols = side_ref.shape[1]
    chunk = 384 if side_cols % 384 == 0 else 512 if side_cols % 512 == 0 else side_cols
    added = refs[5 : 5 + len(starts)]
    for at in range(0, side_cols, chunk):
        cols = slice(at, at + chunk)
        total = None
        for block, ref in ((own_ref[:, low:high], side_ref), (joined_ref[...], side_got_ref)):
            side = ref[:tokens, cols].astype(bf16)
            if blocks_first:
                term = dot(block, side, (0, 0))
            else:
                term = dot(side, block, (0, 0))
            total = term if total is None else total + term
        for start, ref in zip(starts, added):
            if blocks_first:
                total = total + ref[low - start : high - start, cols]
            else:
                total = total + ref[cols, low - start : high - start]
        if blocks_first:
            out_ref[: high - low, cols] = total
        else:
            out_ref[cols, :] = total
    if side_ref.shape[0] > tokens:
        extra = side_ref[tokens:, :] + side_got_ref[tokens:, :]
        for ref in added:
            extra = extra + ref[ref.shape[0] - extra.shape[0] :, :]
        out_ref[high - low :, :] = extra


def pair_product(blocks, sides, low, high, received, blocks_first, ahead):
    width = high - low
    rows_in, side_cols = sides[0].shape
    tokens = blocks[0].shape[0]
    extra = rows_in - tokens
    core = (lax.axis_index("tensor") % 2).astype(jnp.int32).reshape(1)
    if low % 128 or high % 128 or any(start % 128 for start, _ in received):
        blocks = [block[:, low:high] for block in blocks]
        cut = []
        for start, values in received:
            if blocks_first:
                tail = values[values.shape[0] - extra :]
                values = jnp.concatenate([values[low - start : high - start], tail], axis=0)
            else:
                values = values[:, low - start : high - start]
            cut.append((0, values))
        received, low, high = cut, 0, width
    shape = (width + extra, side_cols) if blocks_first else (side_cols, width)
    starts = tuple(start for start, _ in received)
    (total,) = call(
        functools.partial(pair_product_kernel, low, high, starts, blocks_first),
        "pair_product",
        [(shape, f32)],
        (core, *blocks, *sides, *[value for _, value in received]),
        ahead,
        [((tokens, width), bf16)],
    )
    return total


def halving(blocks, sides, blocks_first, pair=1):
    order, bits = halving_order(lax.axis_size("dp"), pair)
    width = blocks[0].shape[1] // len(order)
    low, high = 0, len(order)
    received = []
    ahead = yield None
    for bit in bits + [0]:
        middle = (low + high) // 2 if bit else high
        value = pair_product(
            blocks, sides, low * width, middle * width, received, blocks_first, ahead or ()
        )
        got = value
        if bit:
            got = swap(value, "dp", bit)
            received.append((middle * width, got))
        low = middle
        ahead = yield value, got


def as_row(values):
    ones = jnp.ones((8, values.shape[1]), f32)
    return dot(ones, values, (1, 1), highest)[0:1]


def as_column(row):
    length = row.shape[1]
    down = lax.broadcasted_iota(jnp.int32, (length, length), 0)
    across = lax.broadcasted_iota(jnp.int32, (length, length), 1)
    return jnp.sum(jnp.where(down == across, row, 0.0), axis=1, keepdims=True)


def sum_column(refs):
    return as_column((refs[0][...] + refs[1][...]) + (refs[2][...] + refs[3][...]))


def conv_values(values, taps, positions):
    total = taps[4:5] + taps[0:1] * values
    for offset in range(1, 4):
        shifted = pltpu.roll(values, offset, 0)
        total = total + taps[offset : offset + 1] * jnp.where(positions >= offset, shifted, 0.0)
    return total


def conv_back(grad, values, taps, positions):
    total = taps[0:1] * grad
    tap_grads = [jnp.sum(grad * values, axis=0, keepdims=True)]
    for offset in range(1, 4):
        masked = jnp.where(positions >= offset, grad, 0.0)
        shifted = pltpu.roll(masked, masked.shape[0] - offset, 0)
        total = total + taps[offset : offset + 1] * shifted
        tap_grads.append(jnp.sum(shifted * values, axis=0, keepdims=True))
    tap_grads.append(jnp.sum(grad, axis=0, keepdims=True))
    return total, tap_grads


def scan_parts(step_in, decay_row, bias_row):
    raw = step_in + bias_row
    step = jnp.maximum(raw, 0.0) + jnp.log(1.0 + jnp.exp(-jnp.abs(raw)))
    rates = -jnp.exp(decay_row) * step
    length = rates.shape[0]
    row = lax.broadcasted_iota(jnp.int32, (length, length), 0)
    col = lax.broadcasted_iota(jnp.int32, (length, length), 1)
    lower = (row >= col).astype(f32)
    upper = (row <= col).astype(f32)
    cumulative = dot(lower, rates, (1, 0), highest)
    cumulative_t = dot(rates, upper, (0, 0), highest)
    return raw, step, rates, cumulative, cumulative_t, row >= col, upper


def scan_forward_kernel(
    zx_ref, bc_ref, dt_ref, taps_x_ref, taps_bc_ref, heads_ref, pos_ref, seg_col_ref, seg_row_ref,
    y_ref, gated_ref, square_ref, xa_ref, ba_ref,
):
    positions = pos_ref[...]
    conv_x = conv_values(zx_ref[1], taps_x_ref[...], positions)
    x_act = conv_x * sigmoid(conv_x)
    conv_bc = conv_values(bc_ref[...], taps_bc_ref[...], positions)
    bc_act = (conv_bc * sigmoid(conv_bc)).astype(bf16)
    state = bc_act.shape[1] // 2
    xa_ref[...] = x_act
    ba_ref[...] = bc_act
    heads = heads_ref[...]
    _, step, _, cumulative, cumulative_t, causal, _ = scan_parts(
        dt_ref[...], heads[0:1], heads[1:2]
    )
    inside = causal & (seg_col_ref[...] == seg_row_ref[...])
    gram = dot(bc_act[:, state:], bc_act[:, :state], (1, 1))
    length = positions.shape[0]
    lane = lax.broadcasted_iota(jnp.int32, (length, 128), 1)
    low_half = lane < 64
    square = jnp.zeros((length, 128), f32)
    for pair in range(x_act.shape[1] // 128):
        cols = slice(pair * 128, pair * 128 + 128)
        first, second = 2 * pair, 2 * pair + 1
        x_pair = x_act[:, cols]
        dt_pair = jnp.where(low_half, step[:, first : first + 1], step[:, second : second + 1])
        scaled = x_pair * dt_pair
        total = jnp.where(
            low_half, heads[2:3, first : first + 1], heads[2:3, second : second + 1]
        ) * x_pair
        for head, keep in ((first, low_half), (second, ~low_half)):
            gap = cumulative[:, head : head + 1] - cumulative_t[head : head + 1, :]
            mixing = gram * jnp.exp(jnp.where(inside, gap, -1e30))
            total = total + dot(
                mixing.astype(bf16), jnp.where(keep, scaled, 0.0).astype(bf16), (1, 0)
            )
        z_pair = zx_ref[0, :, cols]
        gated = total * (z_pair * sigmoid(z_pair))
        y_ref[:, cols] = total
        gated_ref[:, cols] = gated
        square = square + gated * gated
    square_ref[...] = as_row(square)


def scan_forward(*values):
    tokens, inner = values[0].shape[1:]
    wide = (tokens, inner)
    shapes = [(wide, f32), (wide, f32), ((1, tokens), f32), (wide, f32), (values[1].shape, bf16)]
    return call(scan_forward_kernel, "scan_forward", shapes, values)


def scan_backward_kernel(
    zx_ref, bc_ref, dt_ref, taps_x_ref, taps_bc_ref, heads_ref, pos_ref, seg_col_ref, seg_row_ref,
    y_ref, xa_ref, ba_ref, up_ref, scale_ref, gain_ref, cross_a, cross_b, cross_c, cross_d, *rest
):
    (
        z_cot_ref, x_cot_ref, bc_cot_ref, dt_cot_ref, taps_x_out, taps_bc_out, heads_out, gain_out
    ) = rest[-8:]
    inner_width = y_ref.shape[1] * 4
    positions = pos_ref[...]
    length = positions.shape[0]
    bc_act = ba_ref[...]
    state = bc_act.shape[1] // 2
    heads = heads_ref[...]
    raw, step, rates, cumulative, cumulative_t, causal, upper = scan_parts(
        dt_ref[...], heads[0:1], heads[1:2]
    )
    inside = causal & (seg_col_ref[...] == seg_row_ref[...])
    gram = dot(bc_act[:, state:], bc_act[:, :state], (1, 1))
    lane = lax.broadcasted_iota(jnp.int32, (length, 128), 1)
    low_half = lane < 64
    scale = scale_ref[...]
    cross = sum_column((cross_a, cross_b, cross_c, cross_d)) / inner_width
    pull = scale * scale * scale * cross
    gram_grad = jnp.zeros((length, length), f32)
    head_lane = lax.broadcasted_iota(jnp.int32, (length, HEAD_PAD), 1)
    head_row = lax.broadcasted_iota(jnp.int32, (HEAD_PAD, length), 0)
    head_one = lax.broadcasted_iota(jnp.int32, (1, HEAD_PAD), 1)
    step_grad = jnp.zeros((length, HEAD_PAD), f32)
    row_sums = jnp.zeros((length, HEAD_PAD), f32)
    col_sums = jnp.zeros((HEAD_PAD, length), f32)
    skip_grad = jnp.zeros((1, HEAD_PAD), f32)
    for pair in range(y_ref.shape[1] // 128):
        cols = slice(pair * 128, pair * 128 + 128)
        first, second = 2 * pair, 2 * pair + 1
        z_pair = zx_ref[0, :, cols]
        y_pair = y_ref[:, cols]
        gate = sigmoid(z_pair)
        silu = z_pair * gate
        gated = y_pair * silu
        up = up_ref[:, cols]
        gain_out[:, cols] = jnp.sum(up * gated * scale, axis=0, keepdims=True)
        gated_grad = scale * (up * gain_ref[:, cols]) - gated * pull
        z_cot_ref[:, cols] = rounded(gated_grad * y_pair * (gate * (1.0 + z_pair * (1.0 - gate))))
        y_grad = gated_grad * silu
        x_pair = xa_ref[:, cols]
        dt_pair = jnp.where(low_half, step[:, first : first + 1], step[:, second : second + 1])
        skip_pair = jnp.where(
            low_half, heads[2:3, first : first + 1], heads[2:3, second : second + 1]
        )
        scaled = (x_pair * dt_pair).astype(bf16)
        scaled_grad = jnp.zeros((length, 128), f32)
        skip_product = y_grad * x_pair
        for head, keep in ((first, low_half), (second, ~low_half)):
            gap = cumulative[:, head : head + 1] - cumulative_t[head : head + 1, :]
            decay = jnp.exp(jnp.where(inside, gap, -1e30))
            mixing = gram * decay
            y_head = jnp.where(keep, y_grad, 0.0).astype(bf16)
            mixing_grad = dot(y_head, scaled, (1, 1))
            scaled_grad = scaled_grad + dot(mixing.astype(bf16), y_head, (0, 0))
            gram_grad = gram_grad + mixing_grad * decay
            moved = mixing_grad * mixing
            row_sums = row_sums + jnp.where(
                head_lane == head, jnp.sum(moved, axis=1, keepdims=True), 0.0
            )
            col_sums = col_sums + jnp.where(
                head_row == head, jnp.sum(moved, axis=0, keepdims=True), 0.0
            )
        step_product = scaled_grad * x_pair
        for head, keep in ((first, low_half), (second, ~low_half)):
            step_grad = step_grad + jnp.where(
                head_lane == head,
                jnp.sum(jnp.where(keep, step_product, 0.0), axis=1, keepdims=True),
                0.0,
            )
            skip_sum = jnp.sum(
                jnp.sum(jnp.where(keep, skip_product, 0.0), axis=0, keepdims=True),
                axis=1,
                keepdims=True,
            )
            skip_grad = skip_grad + jnp.where(head_one == head, skip_sum, 0.0)
        x_grad = scaled_grad * dt_pair + skip_pair * y_grad
        conv_x = conv_values(zx_ref[1, :, cols], taps_x_ref[:, cols], positions)
        gate = sigmoid(conv_x)
        conv_grad = x_grad * (gate * (1.0 + conv_x * (1.0 - gate)))
        total, tap_grads = conv_back(
            conv_grad, zx_ref[1, :, cols], taps_x_ref[:, cols], positions
        )
        x_cot_ref[:, cols] = rounded(total)
        for index, value in enumerate(tap_grads):
            taps_x_out[index : index + 1, cols] = value
    rate_grad = dot(upper, row_sums, (1, 0), highest) - dot(upper, col_sums, (1, 1), highest)
    step_grad = step_grad - rate_grad * jnp.exp(heads[0:1])
    raw_grad = step_grad * sigmoid(raw)
    dt_cot_ref[...] = rounded(raw_grad)
    heads_out[0:1, :] = jnp.sum(rate_grad * rates, axis=0, keepdims=True)
    heads_out[1:2, :] = jnp.sum(raw_grad, axis=0, keepdims=True)
    heads_out[2:3, :] = skip_grad
    gram_low = gram_grad.astype(bf16)
    b_grad = dot(gram_low, bc_act[:, state:], (0, 0))
    c_grad = dot(gram_low, bc_act[:, :state], (1, 0))
    for part, grad in enumerate((b_grad, c_grad)):
        cols = slice(part * state, part * state + state)
        conv = conv_values(bc_ref[:, cols], taps_bc_ref[:, cols], positions)
        gate = sigmoid(conv)
        conv_grad = grad * (gate * (1.0 + conv * (1.0 - gate)))
        total, tap_grads = conv_back(conv_grad, bc_ref[:, cols], taps_bc_ref[:, cols], positions)
        bc_cot_ref[:, cols] = rounded(total)
        for index, value in enumerate(tap_grads):
            taps_bc_out[index : index + 1, cols] = value


def scan_backward(*values, ahead=()):
    zx, bc, dt, taps_x, taps_bc = values[:5]
    tokens, inner = zx.shape[1:]
    shapes = [
        (tokens, inner),
        (tokens, inner),
        bc.shape,
        dt.shape,
        taps_x.shape,
        taps_bc.shape,
        (3, HEAD_PAD),
        (1, inner),
    ]
    shapes = [(shape, f32) for shape in shapes]
    return call(scan_backward_kernel, "scan_backward", shapes, values, ahead)


def turn(values, cosine, sine, low_quarter):
    width = values.shape[1]
    partner = jnp.where(
        low_quarter, pltpu.roll(values, width - HD // 2, 1), pltpu.roll(values, HD // 2, 1)
    )
    return values * cosine + partner * sine


def masked_scores(q_head, kv, allowed):
    scores = dot(q_head, kv, (1, 1)) * HD ** (-0.5)
    return jnp.where(allowed, scores, -1e30)


def softmax(scores):
    exponent = jnp.exp(scores - jnp.max(scores, axis=1, keepdims=True))
    return exponent * (1.0 / jnp.sum(exponent, axis=1, keepdims=True))


def attention_masks(length, seg_col_ref, seg_row_ref):
    row = lax.broadcasted_iota(jnp.int32, (length, length), 0)
    col = lax.broadcasted_iota(jnp.int32, (length, length), 1)
    allowed = (col <= row) & (seg_col_ref[...] == seg_row_ref[...])
    lane = lax.broadcasted_iota(jnp.int32, (length, 2 * HD), 1)
    return allowed, lane < HD, (lane % HD) < HD // 2


def to_low(values, head):
    return values if head == 0 else pltpu.roll(values, HD, 1)


def to_high(values, head):
    return values if head == 1 else pltpu.roll(values, HD, 1)


def attention_forward_kernel(
    head_ref, q_ref, kv_ref, cos_ref, sin_ref, seg_col_ref, seg_row_ref, q_out, kv_out, attn_out
):
    length = q_ref.shape[0]
    allowed, low_half, low_quarter = attention_masks(length, seg_col_ref, seg_row_ref)
    cosine, sine = cos_ref[...], sin_ref[...]
    q_rot = rounded(turn(q_ref[...], cosine, sine, low_quarter))
    first = head_ref[0] == 0
    keys = jnp.where(first, kv_ref[0], pltpu.roll(kv_ref[0], HD, 1))
    kv_in = jnp.where(low_half, keys, jnp.where(first, pltpu.roll(kv_ref[1], HD, 1), kv_ref[1]))
    kv = jnp.where(low_half, turn(kv_in, cosine, sine, low_quarter), kv_in).astype(bf16)
    q_out[...] = q_rot
    kv_out[...] = kv
    parts = []
    for head in range(2):
        q_head = jnp.where(low_half, to_low(q_rot, head), 0.0).astype(bf16)
        probability = softmax(masked_scores(q_head, kv, allowed)).astype(bf16)
        parts.append(dot(probability, kv, (1, 0)))
    attn_out[...] = rounded(jnp.where(low_half, pltpu.roll(parts[0], HD, 1), parts[1]))


def attention_forward(*values):
    shape = values[1].shape
    shapes = [(shape, f32), (shape, bf16), (shape, f32)]
    return call(attention_forward_kernel, "attention_forward", shapes, values)


def attention_backward_kernel(
    head_ref, q_ref, kv_ref, grad_ref, cos_ref, sin_ref, seg_col_ref, seg_row_ref, *rest
):
    q_cot, kv_cot = rest[-2:]
    length = q_ref.shape[0]
    allowed, low_half, low_quarter = attention_masks(length, seg_col_ref, seg_row_ref)
    cosine, sine = cos_ref[...], -sin_ref[...]
    q_rot, kv = q_ref[...], kv_ref[...]
    grad = rounded(grad_ref[...])
    parts = []
    kv_grad = jnp.zeros((length, 2 * HD), f32)
    for head in range(2):
        q_head = jnp.where(low_half, to_low(q_rot, head), 0.0)
        probability = softmax(masked_scores(q_head.astype(bf16), kv, allowed))
        g_head = jnp.where(low_half, 0.0, to_high(grad, head)).astype(bf16)
        prob_grad = dot(g_head, kv, (1, 1))
        inner = jnp.sum(probability * prob_grad, axis=1, keepdims=True)
        score_grad = (probability * (prob_grad - inner)).astype(bf16)
        parts.append(dot(score_grad, kv, (1, 0)) * HD ** (-0.5))
        kv_grad = kv_grad + dot(score_grad, (q_head * HD ** (-0.5)).astype(bf16), (0, 0))
        kv_grad = kv_grad + dot(probability.astype(bf16), g_head, (0, 0))
    q_grad = jnp.where(low_half, parts[0], pltpu.roll(parts[1], HD, 1))
    q_cot[...] = rounded(turn(q_grad, cosine, sine, low_quarter))
    kv_grad = rounded(jnp.where(low_half, turn(kv_grad, cosine, sine, low_quarter), kv_grad))
    turned = pltpu.roll(kv_grad, HD, 1)
    first = head_ref[0] == 0
    kept = low_half == first
    kv_cot[:, : 2 * HD] = jnp.where(kept, jnp.where(first, kv_grad, turned), 0.0)
    kv_cot[:, 2 * HD :] = jnp.where(kept, jnp.where(first, turned, kv_grad), 0.0)


def attention_backward(*values, ahead=()):
    shape = values[1].shape
    shapes = [(shape, f32), ((shape[0], KVH * 2 * HD), f32)]
    return call(attention_backward_kernel, "attention_backward", shapes, values, ahead)


def mix_kernel(
    core_ref, gated_ref, gain_ref, attn_ref, out_w_ref, o_w_ref, sq_a, sq_b, sq_c, sq_d, *rest
):
    mixed_ref, scale_ref, other_ref = rest[-3:]
    inner = gated_ref.shape[1]
    half = gated_ref.shape[0] // 2
    scale = lax.rsqrt(sum_column((sq_a, sq_b, sq_c, sq_d)) / (4 * inner) + epsilon)
    scale_ref[...] = scale
    mixed_ref[:, :inner] = rounded(gated_ref[...] * scale * gain_ref[...])
    mixed_ref[:, inner:] = attn_ref[...]
    other_ref[...] = mix_product(mixed_ref, out_w_ref, o_w_ref, half_rows(1 - core_ref[0], half))


def mix_product(mixed_ref, out_w_ref, o_w_ref, span):
    inner = out_w_ref.shape[0]
    part = mixed_ref[span, :].astype(bf16)
    return dot(part[:, :inner], out_w_ref[...], (1, 0)) + dot(part[:, inner:], o_w_ref[...], (1, 0))


def mix_mine_kernel(core_ref, mixed_ref, out_w_ref, o_w_ref, got_ref, mine_ref):
    half = got_ref.shape[0]
    span = half_rows(core_ref[0], half)
    mine_ref[...] = mix_product(mixed_ref, out_w_ref, o_w_ref, span) + got_ref[...]


def feed_product(gate_cot_ref, up_cot_ref, gu_ref, span):
    gate_part = gate_cot_ref[span, :].astype(bf16)
    up_part = up_cot_ref[span, :].astype(bf16)
    return dot(gate_part, gu_ref[0], (1, 1)) + dot(up_part, gu_ref[1], (1, 1))


def feed_kernel(core_ref, mine_ref, got_ref, in_ref, gain_ref, act_grad_ref, gu_ref, *rest):
    resid_ref, scale_ref, normed_ref, act_ref, gate_cot_ref, up_cot_ref, other_ref = rest[-7:]
    core = core_ref[0]
    half = mine_ref.shape[0]
    for which, ref in ((core, mine_ref), (1 - core, got_ref)):
        span = half_rows(which, half)
        resid_ref[span, :] = in_ref[span, :].astype(f32) + ref[...]
    resid = resid_ref[...]
    scale = rms_scale(resid)
    scale_ref[...] = scale
    normed_ref[...] = (resid * scale * gain_ref[...]).astype(bf16)
    normed = normed_ref[...]
    hidden = gu_ref.shape[2]
    for start in range(0, hidden, 256):
        cols = slice(start, start + 256)
        gate = dot(normed, gu_ref[0, :, cols], (1, 0))
        up = dot(normed, gu_ref[1, :, cols], (1, 0))
        slope = sigmoid(gate)
        silu = gate * slope
        act_ref[:, cols] = rounded(silu * up)
        act_grad = act_grad_ref[:, cols]
        gate_cot_ref[:, cols] = rounded(act_grad * up * slope * (1.0 + gate * (1.0 - slope)))
        up_cot_ref[:, cols] = rounded(act_grad * silu)
    other_ref[...] = feed_product(gate_cot_ref, up_cot_ref, gu_ref, half_rows(1 - core, half))


def feed_mine_kernel(core_ref, gate_cot_ref, up_cot_ref, gu_ref, got_ref, *rest):
    span = half_rows(core_ref[0], got_ref.shape[0])
    rest[-1][...] = feed_product(gate_cot_ref, up_cot_ref, gu_ref, span) + got_ref[...]


def mix_back_kernel(
    core_ref, mine_ref, got_ref, resid_ref, scale_ref, gain_ref, out_grad_ref, out_w_ref, o_w_ref,
    gated_ref, gated_gain_ref, *rest,
):
    grad_ref, mix_ref, gain_grad_ref, up_ref, attn_grad_ref, cross_ref = rest[-6:]
    core = core_ref[0]
    half = mine_ref.shape[0]
    for which, ref in ((core, mine_ref), (1 - core, got_ref)):
        grad_ref[half_rows(which, half), :] = ref[...]
    normed_grad = grad_ref[...]
    resid = resid_ref[...]
    scale = scale_ref[...]
    gain_grad_ref[...] = jnp.sum(normed_grad * resid * scale, axis=0, keepdims=True)
    weighted = normed_grad * gain_ref[...]
    mean = jnp.mean(weighted * resid, axis=1, keepdims=True)
    resid_grad = (
        out_grad_ref[...].astype(f32) + scale * weighted - resid * (scale * scale * scale * mean)
    )
    grad_ref[...] = resid_grad
    mix = resid_grad.astype(bf16)
    mix_ref[...] = mix
    up = dot(mix, out_w_ref[...], (1, 1))
    up_ref[...] = up
    attn_grad_ref[...] = dot(mix, o_w_ref[...], (1, 1))
    cross_ref[...] = as_row(up * gated_gain_ref[...] * gated_ref[...])


def call_dense(kernel, name, shapes, core, values, ahead=(), scratch=()):
    scratch = [(shape, f32) for shape in scratch]
    return call(kernel, name, shapes, (core, *values), ahead, scratch)


def chunks(values):
    return [
        (value, row, start)
        for value in values
        for row in range(value.shape[0])
        for start in range(0, value.shape[1], 128)
    ]


def pick(index, blocks):
    total = blocks[0]
    for place in range(1, len(blocks)):
        total = jnp.where(index == place, blocks[place], total)
    return total


def shared_blocks(bc_ref, kv_ref):
    return [ref[:, at : at + 128] for ref in (bc_ref, kv_ref) for at in (0, 128)]


def post_kernel(core_ref, me_ref, grad_ref, in_ref, taps_ref, bc_ref, kv_ref, *rest):
    mine_ref, other_ref, near_ref, state_ref = rest[-4:]
    half = mine_ref.shape[0]
    tokens = 2 * half
    mine_ref[...] = grad_ref[half_rows(core_ref[0], half), :]
    other_ref[...] = grad_ref[half_rows(1 - core_ref[0], half), :]
    inputs = in_ref[...].astype(f32)
    gain = jnp.sum(grad_ref[...] * inputs * rms_scale(inputs), axis=0, keepdims=True)
    state_ref[...] = jnp.zeros_like(state_ref)
    for at, (value, row, start) in enumerate(chunks((gain, taps_ref[...]))):
        state_ref[at : at + 1, :] = value[row : row + 1, start : start + 128]
    blocks = shared_blocks(bc_ref, kv_ref)
    near_ref[:tokens, :] = pick(me_ref[0] ^ 1, blocks)
    near_ref[tokens : 2 * tokens, :] = pick(me_ref[0] ^ 3, blocks)
    near_ref[2 * tokens :, :] = state_ref[...]


def share_kernel(core_ref, me_ref, near_ref, bc_ref, kv_ref, state_ref, far_ref):
    tokens = bc_ref.shape[0]
    blocks = shared_blocks(bc_ref, kv_ref)
    far_ref[:tokens, :] = pick(me_ref[0] ^ 2, blocks) + near_ref[tokens : 2 * tokens, :]
    far_ref[tokens:, :] = state_ref[...] + near_ref[2 * tokens :, :]


def few_kernel(
    core_ref, me_ref, near_ref, far_own_ref, far_ref, bc_ref, kv_ref, gain_two_ref, taps_ref,
    gain_ref, heads_ref, *rest
):
    few_ref = rest[-1]
    tokens = bc_ref.shape[0]
    blocks = shared_blocks(bc_ref, kv_ref)
    few_ref[:tokens, :] = pick(me_ref[0], blocks) + near_ref[:tokens, :] + far_ref[:tokens, :]
    state = far_own_ref[tokens:, :] + far_ref[tokens:, :]
    used = STATE_ROWS
    few_ref[tokens:, :] = jnp.zeros((few_ref.shape[0] - tokens, few_ref.shape[1]), f32)
    values = (state[:used], gain_two_ref[...], taps_ref[...], gain_ref[...], heads_ref[...])
    for at, (value, row, start) in enumerate(chunks(values)):
        place = tokens + at
        few_ref[place : place + 1, :] = value[row : row + 1, start : start + 128]


def unpack_kernel(core_ref, few_ref, own_ref, *refs):
    rows_out = own_ref.shape[0]
    own_ref[...] = few_ref[:rows_out, :]
    for at, (ref, row, start) in enumerate(chunks(refs)):
        place = rows_out + at
        ref[row : row + 1, start : start + 128] = few_ref[place : place + 1, :]


def assemble_kernel(core_ref, me_ref, own_ref, near_ref, far_ref, far_near_ref, bc_ref, *kv_refs):
    blocks = (own_ref[...], near_ref[...], far_ref[...], far_near_ref[...])
    for place in range(4):
        value = pick(me_ref[0] ^ place, blocks)
        if place < 2:
            bc_ref[:, place * 128 : place * 128 + 128] = value
        else:
            kv_refs[place - 2][...] = value


def input_grad_kernel(core_ref, mine_ref, got_ref, grad_ref, in_ref, gain_ref, out_ref, full_ref):
    half = mine_ref.shape[0]
    full_ref[half_rows(core_ref[0], half), :] = mine_ref[...]
    full_ref[half_rows(1 - core_ref[0], half), :] = got_ref[...]
    inputs = in_ref[...].astype(f32)
    scale = rms_scale(inputs)
    weighted = full_ref[...] * gain_ref[...]
    mean = jnp.mean(weighted * inputs, axis=1, keepdims=True)
    total = grad_ref[...] + scale * weighted - inputs * (scale * scale * scale * mean)
    out_ref[...] = total.astype(bf16)


def layer_out_kernel(core_ref, mine_ref, got_ref, resid_ref, out_ref, full_ref):
    half = mine_ref.shape[0]
    full_ref[half_rows(core_ref[0], half), :] = mine_ref[...]
    full_ref[half_rows(1 - core_ref[0], half), :] = got_ref[...]
    out_ref[...] = (resid_ref[...] + full_ref[...]).astype(bf16)


def rotary_tables(positions):
    half = HD // 2
    frequency = rope_base ** (-jnp.arange(half, dtype=f32) / half)
    angles = positions.astype(f32)[:, None] * frequency[None, :]
    cosine, sine = jnp.cos(angles), jnp.sin(angles)
    return (
        jnp.concatenate([cosine] * 4, axis=1),
        jnp.concatenate([-sine, sine, -sine, sine], axis=1),
    )


def on_device(
    hidden,
    positions,
    out_grad,
    norm_one,
    zx_weight,
    bc_weight,
    dt_weight,
    conv_inner,
    conv_state,
    decay_log,
    dt_bias,
    skip_gain,
    gated_gain,
    out_weight,
    q_weight,
    kv_weight,
    o_weight,
    norm_two,
    gu_weight,
    down_weight,
):
    tokens, model = hidden.shape
    head_count = dt_weight.shape[1]
    inner_cols = conv_inner.shape[1]
    hidden_cols = gu_weight.shape[2]
    query_cols = q_weight.shape[1]
    segment = jnp.cumsum((positions == 0).astype(jnp.int32), dtype=jnp.int32)
    seg_col, seg_row, pos_col = segment[:, None], segment[None, :], positions[:, None]
    cosine, sine = rotary_tables(positions)
    head_pad = ((0, 0), (0, HEAD_PAD - head_count))
    heads = jnp.pad(jnp.stack([decay_log, dt_bias, skip_gain]), head_pad)
    dt_wide = jnp.pad(dt_weight, head_pad)

    core = lax.axis_index("tensor").astype(jnp.int32) % 2
    core_arg = core.reshape(1)
    kv_head = (lax.axis_index("tensor") * (query_cols // HD) // (QH // KVH)).astype(jnp.int32)
    kv_head = kv_head.reshape(1)
    half = tokens // 2
    half_model = model // 2
    wide = (tokens, model)
    half_wide = (half, model)

    inputs = hidden.astype(f32)
    scale_one = rms_scale(inputs)
    normed = (inputs * scale_one * norm_one).astype(bf16)
    own_normed, normed_sent = arrange(1, normed)
    normed_pair = (own_normed, *swap_shared(normed_sent, 1))
    own_out, out_sent = arrange(2, out_grad)
    out_pair = (own_out, *swap_shared(out_sent, 2))

    proj_zx = jnp.einsum("td,dkc->ktc", normed, zx_weight, preferred_element_type=f32)
    proj_bc = dot(normed, bc_weight, (1, 0))
    proj_dt = dot(normed, dt_wide, (1, 0))
    scan_args = (
        proj_zx, proj_bc, proj_dt, conv_inner, conv_state, heads, pos_col, seg_col, seg_row
    )
    y, gated, square, x_act, bc_act = scan_forward(*scan_args)
    squares = spread_tensor(square)

    query = dot(normed, q_weight, (1, 0))
    key_value = jnp.einsum("td,dkc->ktc", normed, kv_weight, preferred_element_type=f32)
    q_rot, kv_rot, attn = attention_forward(
        kv_head, query, key_value, cosine, sine, seg_col, seg_row
    )
    act_grad = dot(out_grad, down_weight, (1, 1))
    gu_split = gu_weight.transpose(1, 0, 2)

    gain_row = gated_gain[None, :]
    mixed, gate_scale, other = call_dense(
        mix_kernel,
        "mix",
        [((tokens, inner_cols + query_cols), f32), ((tokens, 1), f32), (half_wide, f32)],
        core_arg,
        (gated, gain_row, attn, out_weight, o_weight, *squares),
        (normed_pair[1],),
    )
    mixed_got = swap(mixed, "dp", 1)
    mixed_pair = (mixed, mixed_got)
    (mine,) = call_dense(
        mix_mine_kernel,
        "mix_mine",
        [(half_wide, f32)],
        core_arg,
        (mixed, out_weight, o_weight, swap(other, "tensor", 1)),
    )
    resid, scale_two, normed_two, act, gate_cot, up_cot, other = call_dense(
        feed_kernel,
        "feed",
        [
            (wide, f32),
            ((tokens, 1), f32),
            (wide, bf16),
            ((tokens, hidden_cols), f32),
            ((tokens, hidden_cols), f32),
            ((tokens, hidden_cols), f32),
            (half_wide, f32),
        ],
        core_arg,
        (
            *tensor_halves(mine, (out_pair[1], mixed_got, act_grad, gu_split)),
            hidden,
            norm_two[None, :],
            act_grad,
            gu_split,
        ),
    )
    (mine,) = call_dense(
        feed_mine_kernel,
        "feed_mine",
        [(half_wide, f32)],
        core_arg,
        (gate_cot, up_cot, gu_split, swap(other, "tensor", 1)),
    )
    act_got = swap(act, "dp", 2)
    own_up, sent_up = arrange(1, normed_two)
    two_up = swap_shared(sent_up, 1)
    own_gate, sent_gate = arrange(2, normed_two)
    two_gate = swap_shared(sent_gate, 2)
    up_got = swap(up_cot, "dp", 1)
    gate_got = swap(gate_cot, "dp", 2)
    down_stages = halving(out_pair, (act, act_got), False, 2)
    gate_stages = halving((own_gate, *two_gate), (gate_cot, gate_got), True, 2)
    up_stages = halving((own_up, *two_up), (up_cot, up_got), True)
    for stages in (down_stages, gate_stages, up_stages):
        next(stages)
    halves = tensor_halves(mine, (act_got, *two_up, *two_gate, up_got))
    up_first, up_one = up_stages.send((halves[0],))
    resid_grad, mix_grad, norm_two_grad, up, attn_grad, cross = call_dense(
        mix_back_kernel,
        "mix_back",
        [
            (wide, f32),
            (wide, bf16),
            ((1, model), f32),
            ((tokens, inner_cols), f32),
            ((tokens, query_cols), f32),
            ((1, tokens), f32),
        ],
        core_arg,
        (
            *halves,
            resid,
            scale_two,
            norm_two[None, :],
            out_grad,
            out_weight,
            o_weight,
            gated,
            gain_row,
        ),
        (up_first,),
    )
    own_mix, sent_mix = arrange(1, mix_grad)
    mix_pair = (own_mix, *swap_shared(sent_mix, 1))
    crosses = spread_tensor(cross)
    last, gate_one = gate_stages.send((up,))
    q_cot, kv_cot = attention_backward(
        kv_head, q_rot, kv_rot, attn_grad, cosine, sine, seg_col, seg_row, ahead=(last, own_mix)
    )

    mix_stages = halving(mix_pair, mixed_pair, False)
    next(mix_stages)
    act_b = act.astype(bf16)
    mlp_other = dot(rows(act_b, (1 - core) * half, half), down_weight, (1, 0))
    mlp_mine = dot(rows(act_b, core * half, half), down_weight, (1, 0)) + swap(
        mlp_other, "tensor", 1
    )

    z_cot, x_cot, bc_cot, dt_cot, taps_x_grad, taps_bc_grad, heads_grad, gain_grad = scan_backward(
        *scan_args, y, x_act, bc_act, up, gate_scale, gain_row, *crosses, ahead=(q_cot,)
    )

    zx_cot = jnp.stack([z_cot, x_cot], axis=1).astype(bf16)
    normed_grad = (
        jnp.einsum("tkc,dkc->td", zx_cot, zx_weight, preferred_element_type=f32)
        + dot(bc_cot.astype(bf16), bc_weight, (1, 1))
        + dot(dt_cot.astype(bf16), dt_wide, (1, 1))
        + dot(q_cot.astype(bf16), q_weight, (1, 1))
        + jnp.einsum(
            "tkc,dkc->td",
            kv_cot.astype(bf16).reshape(tokens, 2, KVH * HD),
            kv_weight,
            preferred_element_type=f32,
        )
    )
    me_arg = lax.axis_index("tensor").astype(jnp.int32).reshape(1)
    normed_mine, normed_other, near, state_part = call_dense(
        post_kernel,
        "post",
        [
            (half_wide, f32),
            (half_wide, f32),
            ((2 * tokens + STATE_PAD, 128), f32),
            ((STATE_PAD, 128), f32),
        ],
        core_arg,
        (me_arg, normed_grad, hidden, taps_bc_grad, bc_cot, kv_cot),
        (mix_pair[1],),
    )
    zx_own = jnp.concatenate([z_cot, x_cot, q_cot, dt_cot], axis=1)
    zx_got = swap(zx_own, "dp", 1)
    zx_stages = halving(normed_pair, (zx_own, zx_got), True)
    near = swap(near, "tensor", 1)
    (far_own,) = call_dense(
        share_kernel,
        "share",
        [((tokens + STATE_PAD, 128), f32)],
        core_arg,
        (me_arg, near, bc_cot, kv_cot, state_part),
    )
    far = swap(far_own, "tensor", 2)
    (few,) = call_dense(
        few_kernel,
        "few",
        [((tokens + SMALL_ROWS, 128), f32)],
        core_arg,
        (
            me_arg, near, far_own, far, bc_cot, kv_cot, norm_two_grad, taps_x_grad, gain_grad,
            heads_grad,
        ),
    )
    few_got = swap(few, "dp", 1)
    few_stages = halving(normed_pair, (few, few_got), True)
    next(zx_stages)
    next(few_stages)
    normed_mine = normed_mine + swap(normed_other, "tensor", 1)

    gots = {"up": [up_one], "gate": [gate_one]}
    totals = {}
    stage_list = {
        "down": down_stages,
        "gate": gate_stages,
        "up": up_stages,
        "mix": mix_stages,
        "zx": zx_stages,
        "few": few_stages,
    }

    def advance(name, *ahead):
        value, got = stage_list[name].send(ahead)
        gots.setdefault(name, []).append(got)
        totals[name] = value
        return value

    last = advance("up", x_cot)
    last = advance("mix", last, far_own)
    last = advance("gate", last, zx_got)
    last = advance("zx", last)
    last = advance("few", last, few)
    normed_mine, normed_other = tensor_halves(normed_mine, (last,))
    last = normed_mine
    last = advance("down", last)
    last = advance("mix", last)
    last = advance("up", last)
    last = advance("gate", last)
    last = advance("few", last)
    last = advance("down", last)
    last = advance("zx", last)
    last = advance("mix", last)
    last = advance("few", last)
    last = advance("down", last)
    last = advance("zx", last)
    (input_grad,) = call_dense(
        input_grad_kernel,
        "input_grad",
        [(wide, bf16)],
        core_arg,
        (normed_mine, normed_other, resid_grad, hidden, norm_one[None, :]),
        scratch=(wide,),
    )
    (layer_out,) = call_dense(
        layer_out_kernel,
        "layer_out",
        [(wide, bf16)],
        core_arg,
        (*tensor_halves(mlp_mine, (x_cot,)), resid),
        scratch=(wide,),
    )
    for name, stages in stage_list.items():
        for value, _ in stages:
            totals[name] = value
    down_shard, mixed_shard = totals["down"], totals["mix"]
    out_shard, o_shard = mixed_shard[:inner_cols], mixed_shard[inner_cols:]
    gu_shard = jnp.stack([totals["gate"], totals["up"]], axis=1)
    zx_total = totals["zx"]
    zx_shard = zx_total[:, : 2 * inner_cols].reshape(-1, 2, inner_cols)
    few_shard = totals["few"]
    shard_rows = model // lax.axis_size("dp")
    q_shard = zx_total[:, 2 * inner_cols : 2 * inner_cols + query_cols]
    dt_shard = zx_total[:, 2 * inner_cols + query_cols :][:, :head_count]
    own, norm_one_grad, state_grad, norm_two_grad, inner_grad, gain_grad, heads_grad = call_dense(
        unpack_kernel,
        "unpack",
        [
            ((shard_rows, 128), f32),
            ((1, model), f32),
            (conv_state.shape, f32),
            ((1, model), f32),
            (conv_inner.shape, f32),
            ((1, inner_cols), f32),
            ((3, HEAD_PAD), f32),
        ],
        core_arg,
        (few_shard,),
    )
    head_sums = heads_grad[:, :head_count]
    near = swap(own, "tensor", 1)
    bc_shard, *kv_parts = call_dense(
        assemble_kernel,
        "assemble",
        [((shard_rows, 256), f32), ((shard_rows, 128), f32), ((shard_rows, 128), f32)],
        core_arg,
        (me_arg, own, near, swap(own, "tensor", 2), swap(own, "tensor", 3)),
    )
    kv_shard = jnp.stack(kv_parts, axis=1)
    return (
        layer_out,
        input_grad,
        norm_one_grad.reshape(-1),
        zx_shard,
        bc_shard,
        dt_shard,
        inner_grad,
        state_grad,
        head_sums[0],
        head_sums[1],
        head_sums[2],
        gain_grad.reshape(-1),
        out_shard,
        q_shard,
        kv_shard,
        o_shard,
        norm_two_grad.reshape(-1),
        gu_shard,
        down_shard,
    )


def solution(mesh):
    placed = (
        P("dp", None),
        P("dp"),
        P("dp", None),
        P(),
        P(None, None, "tensor"),
        P(),
        P(None, "tensor"),
        P(None, "tensor"),
        P(),
        P("tensor"),
        P("tensor"),
        P("tensor"),
        P("tensor"),
        P("tensor", None),
        P(None, "tensor"),
        P(),
        P("tensor", None),
        P(),
        P(None, None, "tensor"),
        P("tensor", None),
    )
    return jax.shard_map(
        on_device,
        mesh=mesh,
        in_specs=placed,
        out_specs=(
            P("dp", None),
            P("dp", None),
            P(),
            P("dp", None, "tensor"),
            P("dp", None),
            P("dp", "tensor"),
            P(None, "tensor"),
            P(),
            P("tensor"),
            P("tensor"),
            P("tensor"),
            P("tensor"),
            P("tensor", "dp"),
            P("dp", "tensor"),
            P("dp", None, None),
            P("tensor", "dp"),
            P(),
            P("dp", None, "tensor"),
            P("tensor", "dp"),
        ),
        check_vma=False,
    )
```

```python
import functools

import jax
import jax.numpy as jnp
from jax import lax
from jax.experimental import pallas as pl
from jax.experimental.pallas import tpu as pltpu
from jax.sharding import PartitionSpec as P

QH = 8
KVH = 2
HD = 64
HEAD_PAD = 128
STATE_ROWS = 18
STATE_PAD = 24
SMALL_ROWS = 48
COST = 3 * 10**9

epsilon = 1e-05
rope_base = 10000.0
highest = lax.Precision.HIGHEST
bf16 = jnp.bfloat16
f32 = jnp.float32
params = pltpu.CompilerParams(vmem_limit_bytes=40 * 1024 * 1024)


def dot(left, right, dims, precision=None):
    return lax.dot_general(
        left,
        right,
        ((dims[:1], dims[1:]), ((), ())),
        precision=precision,
        preferred_element_type=f32,
    )


def rms_scale(values):
    return lax.rsqrt(jnp.mean(values * values, axis=-1, keepdims=True) + epsilon)


def sigmoid(values):
    return 1.0 / (1.0 + jnp.exp(-values))


def rounded(values):
    return values.astype(bf16).astype(f32)


def cost(flops, read, exps=0):
    return pl.CostEstimate(flops=COST, bytes_accessed=10**6, transcendentals=0)


def call(kernel, name, out_shapes, values, ahead=(), scratch=(), flops=10**6):
    def place(value):
        if value.dtype == jnp.int32 and value.size == 1:
            return pl.BlockSpec(memory_space=pltpu.SMEM)
        return whole(value)

    def whole(value):
        zeros = (0,) * len(value.shape)
        return pl.BlockSpec(value.shape, lambda step: zeros)

    shapes = [jax.ShapeDtypeStruct(shape, kind) for shape, kind in out_shapes]
    return pl.pallas_call(
        kernel,
        grid=(1,),
        in_specs=[place(value) for value in values]
        + [pl.BlockSpec(memory_space=pl.ANY)] * len(ahead),
        out_specs=[whole(shape) for shape in shapes],
        out_shape=shapes,
        scratch_shapes=[pltpu.VMEM(shape, kind) for shape, kind in scratch],
        compiler_params=params,
        cost_estimate=cost(flops, flops),
        name=name,
    )(*values, *ahead)


def swap(values, axis, mask):
    pairs = [(index, index ^ mask) for index in range(lax.axis_size(axis))]
    return lax.ppermute(values, axis, pairs)


def spread_tensor(values):
    return [values] + [swap(values, "tensor", mask) for mask in (1, 2, 3)]


def add_spread(parts):
    return (parts[0] + parts[1]) + (parts[2] + parts[3])


def add_kernel(left_ref, right_ref, *rest):
    rest[-1][...] = left_ref[...] + right_ref[...]


def tensor_halves(mine, ahead=()):
    values = (mine, swap(mine, "tensor", 2))
    (mine,) = call(add_kernel, "add_halves", [(mine.shape, f32)], values, ahead)
    return mine, swap(mine, "tensor", 1)


def swap_shared(values, mask):
    first = swap(values, "dp", mask)
    return first, swap(first, "tensor", 1)


def rows(values, start, size):
    return lax.dynamic_slice_in_dim(values, start, size, 0)


def half_rows(core, size):
    return pl.ds(pl.multiple_of(core * size, size), size)


def halving_order(size, pair):
    order, bits, bit = [0], [], 1
    while bit < size:
        if bit != pair:
            bits.append(bit)
        bit *= 2
    for bit in reversed(bits):
        order = [index ^ bit for index in order] + order
    return order, bits


def pick_blocks(values, offsets):
    width = values.shape[1] // lax.axis_size("dp")
    me = lax.axis_index("dp")
    return jnp.concatenate(
        [
            lax.dynamic_slice_in_dim(values, (me ^ offset) * width, width, 1)
            for offset in offsets
        ],
        axis=1,
    )


def arrange_kernel(order, pair, width, me_ref, *refs):
    count = len(refs) // 2
    me = me_ref[0]
    half = refs[-1].shape[0]
    span = half_rows(me_ref[1], half)
    partner_ref = refs[-1]
    for index in range(count):
        value_ref, own_ref = refs[index], refs[count + index]
        base = index * len(order) * width
        for place, offset in enumerate(order):
            cols = pl.ds(pl.multiple_of((me ^ offset) * width, 128), width)
            own_ref[:, place * width : (place + 1) * width] = value_ref[:, cols].astype(bf16)
            cols = pl.ds(pl.multiple_of((me ^ offset ^ pair) * width, 128), width)
            start = base + place * width
            partner_ref[:, start : start + width] = value_ref[span, cols].astype(f32)


def arrange(pair, *arrays):
    size = lax.axis_size("dp")
    order, _ = halving_order(size, pair)
    tokens, model = arrays[0].shape
    width = model // size
    half = len(order) * width
    if width % 128:
        partner = [index ^ pair for index in order]
        start = lax.axis_index("tensor") % 2 * (tokens // 2)
        sent = [
            rows(pick_blocks(values, partner), start, tokens // 2).astype(f32) for values in arrays
        ]
        return [pick_blocks(values, order) for values in arrays] + [
            jnp.concatenate(sent, axis=1)
        ]
    vmem = pl.BlockSpec(memory_space=pltpu.VMEM)
    me = jnp.stack([lax.axis_index("dp"), lax.axis_index("tensor") % 2]).astype(jnp.int32)
    return pl.pallas_call(
        functools.partial(arrange_kernel, order, pair, width),
        in_specs=[pl.BlockSpec(memory_space=pltpu.SMEM)] + [vmem] * len(arrays),
        out_shape=[jax.ShapeDtypeStruct((tokens, half), bf16) for _ in arrays]
        + [jax.ShapeDtypeStruct((tokens // 2, half * len(arrays)), f32)],
        compiler_params=params,
        cost_estimate=cost(10**6, 8 * tokens * model),
        name="arrange",
    )(me, *arrays)


def pair_product_kernel(low, high, starts, blocks_first, core_ref, *refs):
    own_ref, got_ref, other_ref, side_ref, side_got_ref = refs[:5]
    out_ref, joined_ref = refs[-2:]
    half = got_ref.shape[0]
    tokens = 2 * half
    core = core_ref[0]
    joined_ref[half_rows(core, half), :] = got_ref[:, low:high].astype(bf16)
    joined_ref[half_rows(1 - core, half), :] = other_ref[:, low:high].astype(bf16)
    side_cols = side_ref.shape[1]
    chunk = 384 if side_cols % 384 == 0 else 512 if side_cols % 512 == 0 else side_cols
    added = refs[5 : 5 + len(starts)]
    for at in range(0, side_cols, chunk):
        cols = slice(at, at + chunk)
        total = None
        for block, ref in ((own_ref[:, low:high], side_ref), (joined_ref[...], side_got_ref)):
            side = ref[:tokens, cols].astype(bf16)
            if blocks_first:
                term = dot(block, side, (0, 0))
            else:
                term = dot(side, block, (0, 0))
            total = term if total is None else total + term
        for start, ref in zip(starts, added):
            if blocks_first:
                total = total + ref[low - start : high - start, cols]
            else:
                total = total + ref[cols, low - start : high - start]
        if blocks_first:
            out_ref[: high - low, cols] = total
        else:
            out_ref[cols, :] = total
    if side_ref.shape[0] > tokens:
        extra = side_ref[tokens:, :] + side_got_ref[tokens:, :]
        for ref in added:
            extra = extra + ref[ref.shape[0] - extra.shape[0] :, :]
        out_ref[high - low :, :] = extra


def pair_product(blocks, sides, low, high, received, blocks_first, ahead):
    width = high - low
    rows_in, side_cols = sides[0].shape
    tokens = blocks[0].shape[0]
    extra = rows_in - tokens
    core = (lax.axis_index("tensor") % 2).astype(jnp.int32).reshape(1)
    if low % 128 or high % 128 or any(start % 128 for start, _ in received):
        blocks = [block[:, low:high] for block in blocks]
        cut = []
        for start, values in received:
            if blocks_first:
                tail = values[values.shape[0] - extra :]
                values = jnp.concatenate([values[low - start : high - start], tail], axis=0)
            else:
                values = values[:, low - start : high - start]
            cut.append((0, values))
        received, low, high = cut, 0, width
    shape = (width + extra, side_cols) if blocks_first else (side_cols, width)
    starts = tuple(start for start, _ in received)
    (total,) = call(
        functools.partial(pair_product_kernel, low, high, starts, blocks_first),
        "pair_product",
        [(shape, f32)],
        (core, *blocks, *sides, *[value for _, value in received]),
        ahead,
        [((tokens, width), bf16)],
    )
    return total


def halving(blocks, sides, blocks_first, pair=1):
    order, bits = halving_order(lax.axis_size("dp"), pair)
    width = blocks[0].shape[1] // len(order)
    low, high = 0, len(order)
    received = []
    ahead = yield None
    for bit in bits + [0]:
        middle = (low + high) // 2 if bit else high
        value = pair_product(
            blocks, sides, low * width, middle * width, received, blocks_first, ahead or ()
        )
        got = value
        if bit:
            got = swap(value, "dp", bit)
            received.append((middle * width, got))
        low = middle
        ahead = yield value, got


def as_row(values):
    ones = jnp.ones((8, values.shape[1]), f32)
    return dot(ones, values, (1, 1), highest)[0:1]


def as_column(row):
    length = row.shape[1]
    down = lax.broadcasted_iota(jnp.int32, (length, length), 0)
    across = lax.broadcasted_iota(jnp.int32, (length, length), 1)
    return jnp.sum(jnp.where(down == across, row, 0.0), axis=1, keepdims=True)


def sum_column(refs):
    return as_column((refs[0][...] + refs[1][...]) + (refs[2][...] + refs[3][...]))


def conv_values(values, taps, positions):
    total = taps[4:5] + taps[0:1] * values
    for offset in range(1, 4):
        shifted = pltpu.roll(values, offset, 0)
        total = total + taps[offset : offset + 1] * jnp.where(positions >= offset, shifted, 0.0)
    return total


def conv_back(grad, values, taps, positions):
    total = taps[0:1] * grad
    tap_grads = [jnp.sum(grad * values, axis=0, keepdims=True)]
    for offset in range(1, 4):
        masked = jnp.where(positions >= offset, grad, 0.0)
        shifted = pltpu.roll(masked, masked.shape[0] - offset, 0)
        total = total + taps[offset : offset + 1] * shifted
        tap_grads.append(jnp.sum(shifted * values, axis=0, keepdims=True))
    tap_grads.append(jnp.sum(grad, axis=0, keepdims=True))
    return total, tap_grads


def scan_parts(step_in, decay_row, bias_row):
    raw = step_in + bias_row
    small = jnp.exp(-jnp.abs(raw))
    series = small * (1.0 - small * (0.5 - small * (1.0 / 3.0)))
    step = jnp.maximum(raw, 0.0) + jnp.where(small < 0.01, series, jnp.log(1.0 + small))
    rates = -jnp.exp(decay_row) * step
    length = rates.shape[0]
    row = lax.broadcasted_iota(jnp.int32, (length, length), 0)
    col = lax.broadcasted_iota(jnp.int32, (length, length), 1)
    lower = (row >= col).astype(f32)
    upper = (row <= col).astype(f32)
    cumulative = dot(lower, rates, (1, 0), highest)
    cumulative_t = dot(rates, upper, (0, 0), highest)
    return raw, step, rates, cumulative, cumulative_t, row >= col, upper


def scan_forward_kernel(
    zx_ref, bc_ref, dt_ref, taps_x_ref, taps_bc_ref, heads_ref, pos_ref, seg_col_ref, seg_row_ref,
    y_ref, gated_ref, square_ref, xa_ref, ba_ref,
):
    positions = pos_ref[...]
    conv_x = conv_values(zx_ref[1], taps_x_ref[...], positions)
    x_act = conv_x * sigmoid(conv_x)
    conv_bc = conv_values(bc_ref[...], taps_bc_ref[...], positions)
    bc_act = (conv_bc * sigmoid(conv_bc)).astype(bf16)
    state = bc_act.shape[1] // 2
    xa_ref[...] = x_act
    ba_ref[...] = bc_act
    heads = heads_ref[...]
    _, step, _, cumulative, cumulative_t, causal, _ = scan_parts(
        dt_ref[...], heads[0:1], heads[1:2]
    )
    inside = causal & (seg_col_ref[...] == seg_row_ref[...])
    gram = dot(bc_act[:, state:], bc_act[:, :state], (1, 1))
    length = positions.shape[0]
    lane = lax.broadcasted_iota(jnp.int32, (length, 128), 1)
    low_half = lane < 64
    square = jnp.zeros((length, 128), f32)
    for pair in range(x_act.shape[1] // 128):
        cols = slice(pair * 128, pair * 128 + 128)
        first, second = 2 * pair, 2 * pair + 1
        x_pair = x_act[:, cols]
        dt_pair = jnp.where(low_half, step[:, first : first + 1], step[:, second : second + 1])
        scaled = x_pair * dt_pair
        total = jnp.where(
            low_half, heads[2:3, first : first + 1], heads[2:3, second : second + 1]
        ) * x_pair
        for head, keep in ((first, low_half), (second, ~low_half)):
            gap = cumulative[:, head : head + 1] - cumulative_t[head : head + 1, :]
            mixing = gram * jnp.exp(jnp.where(inside, gap, -1e30))
            total = total + dot(
                mixing.astype(bf16), jnp.where(keep, scaled, 0.0).astype(bf16), (1, 0)
            )
        z_pair = zx_ref[0, :, cols]
        gated = total * (z_pair * sigmoid(z_pair))
        y_ref[:, cols] = total
        gated_ref[:, cols] = gated
        square = square + gated * gated
    square_ref[...] = as_row(square)


def scan_forward(*values):
    tokens, inner = values[0].shape[1:]
    wide = (tokens, inner)
    shapes = [(wide, f32), (wide, f32), ((1, tokens), f32), (wide, f32), (values[1].shape, bf16)]
    return call(scan_forward_kernel, "scan_forward", shapes, values)


def scan_backward_kernel(
    zx_ref, bc_ref, dt_ref, taps_x_ref, taps_bc_ref, heads_ref, pos_ref, seg_col_ref, seg_row_ref,
    y_ref, xa_ref, ba_ref, up_ref, scale_ref, gain_ref, cross_a, cross_b, cross_c, cross_d, *rest
):
    (
        z_cot_ref, x_cot_ref, bc_cot_ref, dt_cot_ref, taps_x_out, taps_bc_out, heads_out, gain_out
    ) = rest[-8:]
    inner_width = y_ref.shape[1] * 4
    positions = pos_ref[...]
    length = positions.shape[0]
    bc_act = ba_ref[...]
    state = bc_act.shape[1] // 2
    heads = heads_ref[...]
    raw, step, rates, cumulative, cumulative_t, causal, upper = scan_parts(
        dt_ref[...], heads[0:1], heads[1:2]
    )
    inside = causal & (seg_col_ref[...] == seg_row_ref[...])
    gram = dot(bc_act[:, state:], bc_act[:, :state], (1, 1))
    lane = lax.broadcasted_iota(jnp.int32, (length, 128), 1)
    low_half = lane < 64
    scale = scale_ref[...]
    cross = sum_column((cross_a, cross_b, cross_c, cross_d)) / inner_width
    pull = scale * scale * scale * cross
    gram_grad = jnp.zeros((length, length), f32)
    head_lane = lax.broadcasted_iota(jnp.int32, (length, HEAD_PAD), 1)
    head_row = lax.broadcasted_iota(jnp.int32, (HEAD_PAD, length), 0)
    head_one = lax.broadcasted_iota(jnp.int32, (1, HEAD_PAD), 1)
    step_grad = jnp.zeros((length, HEAD_PAD), f32)
    row_sums = jnp.zeros((length, HEAD_PAD), f32)
    col_sums = jnp.zeros((HEAD_PAD, length), f32)
    skip_grad = jnp.zeros((1, HEAD_PAD), f32)
    for pair in range(y_ref.shape[1] // 128):
        cols = slice(pair * 128, pair * 128 + 128)
        first, second = 2 * pair, 2 * pair + 1
        z_pair = zx_ref[0, :, cols]
        y_pair = y_ref[:, cols]
        gate = sigmoid(z_pair)
        silu = z_pair * gate
        gated = y_pair * silu
        up = up_ref[:, cols]
        gain_out[:, cols] = jnp.sum(up * gated * scale, axis=0, keepdims=True)
        gated_grad = scale * (up * gain_ref[:, cols]) - gated * pull
        z_cot_ref[:, cols] = rounded(gated_grad * y_pair * (gate * (1.0 + z_pair * (1.0 - gate))))
        y_grad = gated_grad * silu
        x_pair = xa_ref[:, cols]
        dt_pair = jnp.where(low_half, step[:, first : first + 1], step[:, second : second + 1])
        skip_pair = jnp.where(
            low_half, heads[2:3, first : first + 1], heads[2:3, second : second + 1]
        )
        scaled = (x_pair * dt_pair).astype(bf16)
        scaled_grad = jnp.zeros((length, 128), f32)
        skip_product = y_grad * x_pair
        for head, keep in ((first, low_half), (second, ~low_half)):
            gap = cumulative[:, head : head + 1] - cumulative_t[head : head + 1, :]
            decay = jnp.exp(jnp.where(inside, gap, -1e30))
            mixing = gram * decay
            y_head = jnp.where(keep, y_grad, 0.0).astype(bf16)
            mixing_grad = dot(y_head, scaled, (1, 1))
            scaled_grad = scaled_grad + dot(mixing.astype(bf16), y_head, (0, 0))
            gram_grad = gram_grad + mixing_grad * decay
            moved = mixing_grad * mixing
            row_sums = row_sums + jnp.where(
                head_lane == head, jnp.sum(moved, axis=1, keepdims=True), 0.0
            )
            col_sums = col_sums + jnp.where(
                head_row == head, jnp.sum(moved, axis=0, keepdims=True), 0.0
            )
        step_product = scaled_grad * x_pair
        for head, keep in ((first, low_half), (second, ~low_half)):
            step_grad = step_grad + jnp.where(
                head_lane == head,
                jnp.sum(jnp.where(keep, step_product, 0.0), axis=1, keepdims=True),
                0.0,
            )
            skip_sum = jnp.sum(
                jnp.sum(jnp.where(keep, skip_product, 0.0), axis=0, keepdims=True),
                axis=1,
                keepdims=True,
            )
            skip_grad = skip_grad + jnp.where(head_one == head, skip_sum, 0.0)
        x_grad = scaled_grad * dt_pair + skip_pair * y_grad
        conv_x = conv_values(zx_ref[1, :, cols], taps_x_ref[:, cols], positions)
        gate = sigmoid(conv_x)
        conv_grad = x_grad * (gate * (1.0 + conv_x * (1.0 - gate)))
        total, tap_grads = conv_back(
            conv_grad, zx_ref[1, :, cols], taps_x_ref[:, cols], positions
        )
        x_cot_ref[:, cols] = rounded(total)
        for index, value in enumerate(tap_grads):
            taps_x_out[index : index + 1, cols] = value
    rate_grad = dot(upper, row_sums, (1, 0), highest) - dot(upper, col_sums, (1, 1), highest)
    step_grad = step_grad - rate_grad * jnp.exp(heads[0:1])
    raw_grad = step_grad * sigmoid(raw)
    dt_cot_ref[...] = rounded(raw_grad)
    heads_out[0:1, :] = jnp.sum(rate_grad * rates, axis=0, keepdims=True)
    heads_out[1:2, :] = jnp.sum(raw_grad, axis=0, keepdims=True)
    heads_out[2:3, :] = skip_grad
    gram_low = gram_grad.astype(bf16)
    b_grad = dot(gram_low, bc_act[:, state:], (0, 0))
    c_grad = dot(gram_low, bc_act[:, :state], (1, 0))
    for part, grad in enumerate((b_grad, c_grad)):
        cols = slice(part * state, part * state + state)
        conv = conv_values(bc_ref[:, cols], taps_bc_ref[:, cols], positions)
        gate = sigmoid(conv)
        conv_grad = grad * (gate * (1.0 + conv * (1.0 - gate)))
        total, tap_grads = conv_back(conv_grad, bc_ref[:, cols], taps_bc_ref[:, cols], positions)
        bc_cot_ref[:, cols] = rounded(total)
        for index, value in enumerate(tap_grads):
            taps_bc_out[index : index + 1, cols] = value


def scan_backward(*values, ahead=()):
    zx, bc, dt, taps_x, taps_bc = values[:5]
    tokens, inner = zx.shape[1:]
    shapes = [
        (tokens, inner),
        (tokens, inner),
        bc.shape,
        dt.shape,
        taps_x.shape,
        taps_bc.shape,
        (3, HEAD_PAD),
        (1, inner),
    ]
    shapes = [(shape, f32) for shape in shapes]
    return call(scan_backward_kernel, "scan_backward", shapes, values, ahead)


def turn(values, cosine, sine, low_quarter):
    width = values.shape[1]
    partner = jnp.where(
        low_quarter, pltpu.roll(values, width - HD // 2, 1), pltpu.roll(values, HD // 2, 1)
    )
    return values * cosine + partner * sine


def masked_scores(q_head, kv, allowed):
    scores = dot(q_head, kv, (1, 1)) * HD ** (-0.5)
    return jnp.where(allowed, scores, -1e30)


def softmax(scores):
    exponent = jnp.exp(scores - jnp.max(scores, axis=1, keepdims=True))
    return exponent * (1.0 / jnp.sum(exponent, axis=1, keepdims=True))


def attention_masks(length, seg_col_ref, seg_row_ref):
    row = lax.broadcasted_iota(jnp.int32, (length, length), 0)
    col = lax.broadcasted_iota(jnp.int32, (length, length), 1)
    allowed = (col <= row) & (seg_col_ref[...] == seg_row_ref[...])
    lane = lax.broadcasted_iota(jnp.int32, (length, 2 * HD), 1)
    return allowed, lane < HD, (lane % HD) < HD // 2


def to_low(values, head):
    return values if head == 0 else pltpu.roll(values, HD, 1)


def to_high(values, head):
    return values if head == 1 else pltpu.roll(values, HD, 1)


def attention_forward_kernel(
    head_ref, q_ref, kv_ref, cos_ref, sin_ref, seg_col_ref, seg_row_ref, q_out, kv_out, attn_out
):
    length = q_ref.shape[0]
    allowed, low_half, low_quarter = attention_masks(length, seg_col_ref, seg_row_ref)
    cosine, sine = cos_ref[...], sin_ref[...]
    q_rot = rounded(turn(q_ref[...], cosine, sine, low_quarter))
    first = head_ref[0] == 0
    keys = jnp.where(first, kv_ref[0], pltpu.roll(kv_ref[0], HD, 1))
    kv_in = jnp.where(low_half, keys, jnp.where(first, pltpu.roll(kv_ref[1], HD, 1), kv_ref[1]))
    kv = jnp.where(low_half, turn(kv_in, cosine, sine, low_quarter), kv_in).astype(bf16)
    q_out[...] = q_rot
    kv_out[...] = kv
    parts = []
    for head in range(2):
        q_head = jnp.where(low_half, to_low(q_rot, head), 0.0).astype(bf16)
        probability = softmax(masked_scores(q_head, kv, allowed)).astype(bf16)
        parts.append(dot(probability, kv, (1, 0)))
    attn_out[...] = rounded(jnp.where(low_half, pltpu.roll(parts[0], HD, 1), parts[1]))


def attention_forward(*values):
    shape = values[1].shape
    shapes = [(shape, f32), (shape, bf16), (shape, f32)]
    return call(attention_forward_kernel, "attention_forward", shapes, values)


def attention_backward_kernel(
    head_ref, q_ref, kv_ref, grad_ref, cos_ref, sin_ref, seg_col_ref, seg_row_ref, *rest
):
    q_cot, kv_cot = rest[-2:]
    length = q_ref.shape[0]
    allowed, low_half, low_quarter = attention_masks(length, seg_col_ref, seg_row_ref)
    cosine, sine = cos_ref[...], -sin_ref[...]
    q_rot, kv = q_ref[...], kv_ref[...]
    grad = rounded(grad_ref[...])
    parts = []
    kv_grad = jnp.zeros((length, 2 * HD), f32)
    for head in range(2):
        q_head = jnp.where(low_half, to_low(q_rot, head), 0.0)
        probability = softmax(masked_scores(q_head.astype(bf16), kv, allowed))
        g_head = jnp.where(low_half, 0.0, to_high(grad, head)).astype(bf16)
        prob_grad = dot(g_head, kv, (1, 1))
        inner = jnp.sum(probability * prob_grad, axis=1, keepdims=True)
        score_grad = (probability * (prob_grad - inner)).astype(bf16)
        parts.append(dot(score_grad, kv, (1, 0)) * HD ** (-0.5))
        kv_grad = kv_grad + dot(score_grad, (q_head * HD ** (-0.5)).astype(bf16), (0, 0))
        kv_grad = kv_grad + dot(probability.astype(bf16), g_head, (0, 0))
    q_grad = jnp.where(low_half, parts[0], pltpu.roll(parts[1], HD, 1))
    q_cot[...] = rounded(turn(q_grad, cosine, sine, low_quarter))
    kv_grad = rounded(jnp.where(low_half, turn(kv_grad, cosine, sine, low_quarter), kv_grad))
    turned = pltpu.roll(kv_grad, HD, 1)
    first = head_ref[0] == 0
    kept = low_half == first
    kv_cot[:, : 2 * HD] = jnp.where(kept, jnp.where(first, kv_grad, turned), 0.0)
    kv_cot[:, 2 * HD :] = jnp.where(kept, jnp.where(first, turned, kv_grad), 0.0)


def attention_backward(*values, ahead=()):
    shape = values[1].shape
    shapes = [(shape, f32), ((shape[0], KVH * 2 * HD), f32)]
    return call(attention_backward_kernel, "attention_backward", shapes, values, ahead)


def mix_kernel(
    core_ref, gated_ref, gain_ref, attn_ref, out_w_ref, o_w_ref, sq_a, sq_b, sq_c, sq_d, *rest
):
    mixed_ref, scale_ref, other_ref = rest[-3:]
    inner = gated_ref.shape[1]
    half = gated_ref.shape[0] // 2
    scale = lax.rsqrt(sum_column((sq_a, sq_b, sq_c, sq_d)) / (4 * inner) + epsilon)
    scale_ref[...] = scale
    mixed_ref[:, :inner] = rounded(gated_ref[...] * scale * gain_ref[...])
    mixed_ref[:, inner:] = attn_ref[...]
    other_ref[...] = mix_product(mixed_ref, out_w_ref, o_w_ref, half_rows(1 - core_ref[0], half))


def mix_product(mixed_ref, out_w_ref, o_w_ref, span):
    inner = out_w_ref.shape[0]
    part = mixed_ref[span, :].astype(bf16)
    return dot(part[:, :inner], out_w_ref[...], (1, 0)) + dot(part[:, inner:], o_w_ref[...], (1, 0))


def mix_mine_kernel(core_ref, mixed_ref, out_w_ref, o_w_ref, got_ref, mine_ref):
    half = got_ref.shape[0]
    span = half_rows(core_ref[0], half)
    mine_ref[...] = mix_product(mixed_ref, out_w_ref, o_w_ref, span) + got_ref[...]


def feed_product(gate_cot_ref, up_cot_ref, gu_ref, span):
    gate_part = gate_cot_ref[span, :].astype(bf16)
    up_part = up_cot_ref[span, :].astype(bf16)
    return dot(gate_part, gu_ref[0], (1, 1)) + dot(up_part, gu_ref[1], (1, 1))


def feed_kernel(core_ref, mine_ref, got_ref, in_ref, gain_ref, act_grad_ref, gu_ref, *rest):
    resid_ref, scale_ref, normed_ref, act_ref, gate_cot_ref, up_cot_ref, other_ref = rest[-7:]
    core = core_ref[0]
    half = mine_ref.shape[0]
    for which, ref in ((core, mine_ref), (1 - core, got_ref)):
        span = half_rows(which, half)
        resid_ref[span, :] = in_ref[span, :].astype(f32) + ref[...]
    resid = resid_ref[...]
    scale = rms_scale(resid)
    scale_ref[...] = scale
    normed_ref[...] = (resid * scale * gain_ref[...]).astype(bf16)
    normed = normed_ref[...]
    hidden = gu_ref.shape[2]
    for start in range(0, hidden, 256):
        cols = slice(start, start + 256)
        gate = dot(normed, gu_ref[0, :, cols], (1, 0))
        up = dot(normed, gu_ref[1, :, cols], (1, 0))
        slope = sigmoid(gate)
        silu = gate * slope
        act_ref[:, cols] = rounded(silu * up)
        act_grad = act_grad_ref[:, cols]
        gate_cot_ref[:, cols] = rounded(act_grad * up * slope * (1.0 + gate * (1.0 - slope)))
        up_cot_ref[:, cols] = rounded(act_grad * silu)
    other_ref[...] = feed_product(gate_cot_ref, up_cot_ref, gu_ref, half_rows(1 - core, half))


def feed_mine_kernel(core_ref, gate_cot_ref, up_cot_ref, gu_ref, got_ref, *rest):
    span = half_rows(core_ref[0], got_ref.shape[0])
    rest[-1][...] = feed_product(gate_cot_ref, up_cot_ref, gu_ref, span) + got_ref[...]


def mix_back_kernel(
    core_ref, mine_ref, got_ref, resid_ref, scale_ref, gain_ref, out_grad_ref, out_w_ref, o_w_ref,
    gated_ref, gated_gain_ref, *rest,
):
    grad_ref, mix_ref, gain_grad_ref, up_ref, attn_grad_ref, cross_ref = rest[-6:]
    core = core_ref[0]
    half = mine_ref.shape[0]
    for which, ref in ((core, mine_ref), (1 - core, got_ref)):
        grad_ref[half_rows(which, half), :] = ref[...]
    normed_grad = grad_ref[...]
    resid = resid_ref[...]
    scale = scale_ref[...]
    gain_grad_ref[...] = jnp.sum(normed_grad * resid * scale, axis=0, keepdims=True)
    weighted = normed_grad * gain_ref[...]
    mean = jnp.mean(weighted * resid, axis=1, keepdims=True)
    resid_grad = (
        out_grad_ref[...].astype(f32) + scale * weighted - resid * (scale * scale * scale * mean)
    )
    grad_ref[...] = resid_grad
    mix = resid_grad.astype(bf16)
    mix_ref[...] = mix
    up = dot(mix, out_w_ref[...], (1, 1))
    up_ref[...] = up
    attn_grad_ref[...] = dot(mix, o_w_ref[...], (1, 1))
    cross_ref[...] = as_row(up * gated_gain_ref[...] * gated_ref[...])


def call_dense(kernel, name, shapes, core, values, ahead=(), scratch=()):
    scratch = [(shape, f32) for shape in scratch]
    return call(kernel, name, shapes, (core, *values), ahead, scratch)


def chunks(values):
    return [
        (value, row, start)
        for value in values
        for row in range(value.shape[0])
        for start in range(0, value.shape[1], 128)
    ]


def pick(index, blocks):
    total = blocks[0]
    for place in range(1, len(blocks)):
        total = jnp.where(index == place, blocks[place], total)
    return total


def shared_blocks(bc_ref, kv_ref):
    return [ref[:, at : at + 128] for ref in (bc_ref, kv_ref) for at in (0, 128)]


def post_kernel(core_ref, me_ref, grad_ref, in_ref, taps_ref, bc_ref, kv_ref, *rest):
    mine_ref, other_ref, near_ref, state_ref = rest[-4:]
    half = mine_ref.shape[0]
    tokens = 2 * half
    mine_ref[...] = grad_ref[half_rows(core_ref[0], half), :]
    other_ref[...] = grad_ref[half_rows(1 - core_ref[0], half), :]
    inputs = in_ref[...].astype(f32)
    gain = jnp.sum(grad_ref[...] * inputs * rms_scale(inputs), axis=0, keepdims=True)
    state_ref[...] = jnp.zeros_like(state_ref)
    for at, (value, row, start) in enumerate(chunks((gain, taps_ref[...]))):
        state_ref[at : at + 1, :] = value[row : row + 1, start : start + 128]
    blocks = shared_blocks(bc_ref, kv_ref)
    near_ref[:tokens, :] = pick(me_ref[0] ^ 1, blocks)
    near_ref[tokens : 2 * tokens, :] = pick(me_ref[0] ^ 3, blocks)
    near_ref[2 * tokens :, :] = state_ref[...]


def share_kernel(core_ref, me_ref, near_ref, bc_ref, kv_ref, state_ref, far_ref):
    tokens = bc_ref.shape[0]
    blocks = shared_blocks(bc_ref, kv_ref)
    far_ref[:tokens, :] = pick(me_ref[0] ^ 2, blocks) + near_ref[tokens : 2 * tokens, :]
    far_ref[tokens:, :] = state_ref[...] + near_ref[2 * tokens :, :]


def few_kernel(
    core_ref, me_ref, near_ref, far_own_ref, far_ref, bc_ref, kv_ref, gain_two_ref, taps_ref,
    gain_ref, heads_ref, *rest
):
    few_ref = rest[-1]
    tokens = bc_ref.shape[0]
    blocks = shared_blocks(bc_ref, kv_ref)
    few_ref[:tokens, :] = pick(me_ref[0], blocks) + near_ref[:tokens, :] + far_ref[:tokens, :]
    state = far_own_ref[tokens:, :] + far_ref[tokens:, :]
    used = STATE_ROWS
    few_ref[tokens:, :] = jnp.zeros((few_ref.shape[0] - tokens, few_ref.shape[1]), f32)
    values = (state[:used], gain_two_ref[...], taps_ref[...], gain_ref[...], heads_ref[...])
    for at, (value, row, start) in enumerate(chunks(values)):
        place = tokens + at
        few_ref[place : place + 1, :] = value[row : row + 1, start : start + 128]


def unpack_kernel(core_ref, few_ref, own_ref, *refs):
    rows_out = own_ref.shape[0]
    own_ref[...] = few_ref[:rows_out, :]
    for at, (ref, row, start) in enumerate(chunks(refs)):
        place = rows_out + at
        ref[row : row + 1, start : start + 128] = few_ref[place : place + 1, :]


def assemble_kernel(core_ref, me_ref, own_ref, near_ref, far_ref, far_near_ref, bc_ref, *kv_refs):
    blocks = (own_ref[...], near_ref[...], far_ref[...], far_near_ref[...])
    for place in range(4):
        value = pick(me_ref[0] ^ place, blocks)
        if place < 2:
            bc_ref[:, place * 128 : place * 128 + 128] = value
        else:
            kv_refs[place - 2][...] = value


def input_grad_kernel(core_ref, mine_ref, got_ref, grad_ref, in_ref, gain_ref, out_ref, full_ref):
    half = mine_ref.shape[0]
    full_ref[half_rows(core_ref[0], half), :] = mine_ref[...]
    full_ref[half_rows(1 - core_ref[0], half), :] = got_ref[...]
    inputs = in_ref[...].astype(f32)
    scale = rms_scale(inputs)
    weighted = full_ref[...] * gain_ref[...]
    mean = jnp.mean(weighted * inputs, axis=1, keepdims=True)
    total = grad_ref[...] + scale * weighted - inputs * (scale * scale * scale * mean)
    out_ref[...] = total.astype(bf16)


def layer_out_kernel(core_ref, mine_ref, got_ref, resid_ref, out_ref, full_ref):
    half = mine_ref.shape[0]
    full_ref[half_rows(core_ref[0], half), :] = mine_ref[...]
    full_ref[half_rows(1 - core_ref[0], half), :] = got_ref[...]
    out_ref[...] = (resid_ref[...] + full_ref[...]).astype(bf16)


def rotary_tables(positions):
    half = HD // 2
    frequency = rope_base ** (-jnp.arange(half, dtype=f32) / half)
    angles = positions.astype(f32)[:, None] * frequency[None, :]
    cosine, sine = jnp.cos(angles), jnp.sin(angles)
    return (
        jnp.concatenate([cosine] * 4, axis=1),
        jnp.concatenate([-sine, sine, -sine, sine], axis=1),
    )


def on_device(
    hidden,
    positions,
    out_grad,
    norm_one,
    zx_weight,
    bc_weight,
    dt_weight,
    conv_inner,
    conv_state,
    decay_log,
    dt_bias,
    skip_gain,
    gated_gain,
    out_weight,
    q_weight,
    kv_weight,
    o_weight,
    norm_two,
    gu_weight,
    down_weight,
):
    tokens, model = hidden.shape
    head_count = dt_weight.shape[1]
    inner_cols = conv_inner.shape[1]
    hidden_cols = gu_weight.shape[2]
    query_cols = q_weight.shape[1]
    segment = jnp.cumsum((positions == 0).astype(jnp.int32), dtype=jnp.int32)
    seg_col, seg_row, pos_col = segment[:, None], segment[None, :], positions[:, None]
    cosine, sine = rotary_tables(positions)
    head_pad = ((0, 0), (0, HEAD_PAD - head_count))
    heads = jnp.pad(jnp.stack([decay_log, dt_bias, skip_gain]), head_pad)
    dt_wide = jnp.pad(dt_weight, head_pad)

    core = lax.axis_index("tensor").astype(jnp.int32) % 2
    core_arg = core.reshape(1)
    kv_head = (lax.axis_index("tensor") * (query_cols // HD) // (QH // KVH)).astype(jnp.int32)
    kv_head = kv_head.reshape(1)
    half = tokens // 2
    half_model = model // 2
    wide = (tokens, model)
    half_wide = (half, model)

    inputs = hidden.astype(f32)
    scale_one = rms_scale(inputs)
    normed = (inputs * scale_one * norm_one).astype(bf16)
    own_normed, normed_sent = arrange(1, normed)
    normed_pair = (own_normed, *swap_shared(normed_sent, 1))
    own_out, out_sent = arrange(2, out_grad)
    out_pair = (own_out, *swap_shared(out_sent, 2))

    proj_zx = jnp.einsum("td,dkc->ktc", normed, zx_weight, preferred_element_type=f32)
    proj_bc = dot(normed, bc_weight, (1, 0))
    proj_dt = dot(normed, dt_wide, (1, 0))
    scan_args = (
        proj_zx, proj_bc, proj_dt, conv_inner, conv_state, heads, pos_col, seg_col, seg_row
    )
    y, gated, square, x_act, bc_act = scan_forward(*scan_args)
    squares = spread_tensor(square)

    query = dot(normed, q_weight, (1, 0))
    key_value = jnp.einsum("td,dkc->ktc", normed, kv_weight, preferred_element_type=f32)
    q_rot, kv_rot, attn = attention_forward(
        kv_head, query, key_value, cosine, sine, seg_col, seg_row
    )
    act_grad = dot(out_grad, down_weight, (1, 1))
    gu_split = gu_weight.transpose(1, 0, 2)

    gain_row = gated_gain[None, :]
    mixed, gate_scale, other = call_dense(
        mix_kernel,
        "mix",
        [((tokens, inner_cols + query_cols), f32), ((tokens, 1), f32), (half_wide, f32)],
        core_arg,
        (gated, gain_row, attn, out_weight, o_weight, *squares),
        (normed_pair[1],),
    )
    mixed_got = swap(mixed, "dp", 1)
    mixed_pair = (mixed, mixed_got)
    (mine,) = call_dense(
        mix_mine_kernel,
        "mix_mine",
        [(half_wide, f32)],
        core_arg,
        (mixed, out_weight, o_weight, swap(other, "tensor", 1)),
    )
    resid, scale_two, normed_two, act, gate_cot, up_cot, other = call_dense(
        feed_kernel,
        "feed",
        [
            (wide, f32),
            ((tokens, 1), f32),
            (wide, bf16),
            ((tokens, hidden_cols), f32),
            ((tokens, hidden_cols), f32),
            ((tokens, hidden_cols), f32),
            (half_wide, f32),
        ],
        core_arg,
        (
            *tensor_halves(mine, (out_pair[1], mixed_got, act_grad, gu_split)),
            hidden,
            norm_two[None, :],
            act_grad,
            gu_split,
        ),
    )
    (mine,) = call_dense(
        feed_mine_kernel,
        "feed_mine",
        [(half_wide, f32)],
        core_arg,
        (gate_cot, up_cot, gu_split, swap(other, "tensor", 1)),
    )
    act_got = swap(act, "dp", 2)
    own_up, sent_up = arrange(1, normed_two)
    two_up = swap_shared(sent_up, 1)
    own_gate, sent_gate = arrange(2, normed_two)
    two_gate = swap_shared(sent_gate, 2)
    up_got = swap(up_cot, "dp", 1)
    gate_got = swap(gate_cot, "dp", 2)
    down_stages = halving(out_pair, (act, act_got), False, 2)
    gate_stages = halving((own_gate, *two_gate), (gate_cot, gate_got), True, 2)
    up_stages = halving((own_up, *two_up), (up_cot, up_got), True)
    for stages in (down_stages, gate_stages, up_stages):
        next(stages)
    halves = tensor_halves(mine, (act_got, *two_up, *two_gate, up_got))
    up_first, up_one = up_stages.send((halves[0],))
    resid_grad, mix_grad, norm_two_grad, up, attn_grad, cross = call_dense(
        mix_back_kernel,
        "mix_back",
        [
            (wide, f32),
            (wide, bf16),
            ((1, model), f32),
            ((tokens, inner_cols), f32),
            ((tokens, query_cols), f32),
            ((1, tokens), f32),
        ],
        core_arg,
        (
            *halves,
            resid,
            scale_two,
            norm_two[None, :],
            out_grad,
            out_weight,
            o_weight,
            gated,
            gain_row,
        ),
        (up_first,),
    )
    own_mix, sent_mix = arrange(1, mix_grad)
    mix_pair = (own_mix, *swap_shared(sent_mix, 1))
    crosses = spread_tensor(cross)
    last, gate_one = gate_stages.send((up,))
    q_cot, kv_cot = attention_backward(
        kv_head, q_rot, kv_rot, attn_grad, cosine, sine, seg_col, seg_row, ahead=(last, own_mix)
    )

    mix_stages = halving(mix_pair, mixed_pair, False)
    next(mix_stages)
    act_b = act.astype(bf16)
    mlp_other = dot(rows(act_b, (1 - core) * half, half), down_weight, (1, 0))
    mlp_mine = dot(rows(act_b, core * half, half), down_weight, (1, 0)) + swap(
        mlp_other, "tensor", 1
    )

    z_cot, x_cot, bc_cot, dt_cot, taps_x_grad, taps_bc_grad, heads_grad, gain_grad = scan_backward(
        *scan_args, y, x_act, bc_act, up, gate_scale, gain_row, *crosses, ahead=(q_cot,)
    )

    zx_cot = jnp.stack([z_cot, x_cot], axis=1).astype(bf16)
    normed_grad = (
        jnp.einsum("tkc,dkc->td", zx_cot, zx_weight, preferred_element_type=f32)
        + dot(bc_cot.astype(bf16), bc_weight, (1, 1))
        + dot(dt_cot.astype(bf16), dt_wide, (1, 1))
        + dot(q_cot.astype(bf16), q_weight, (1, 1))
        + jnp.einsum(
            "tkc,dkc->td",
            kv_cot.astype(bf16).reshape(tokens, 2, KVH * HD),
            kv_weight,
            preferred_element_type=f32,
        )
    )
    me_arg = lax.axis_index("tensor").astype(jnp.int32).reshape(1)
    normed_mine, normed_other, near, state_part = call_dense(
        post_kernel,
        "post",
        [
            (half_wide, f32),
            (half_wide, f32),
            ((2 * tokens + STATE_PAD, 128), f32),
            ((STATE_PAD, 128), f32),
        ],
        core_arg,
        (me_arg, normed_grad, hidden, taps_bc_grad, bc_cot, kv_cot),
        (mix_pair[1],),
    )
    zx_own = jnp.concatenate([z_cot, x_cot, q_cot, dt_cot], axis=1)
    zx_got = swap(zx_own, "dp", 1)
    zx_stages = halving(normed_pair, (zx_own, zx_got), True)
    near = swap(near, "tensor", 1)
    (far_own,) = call_dense(
        share_kernel,
        "share",
        [((tokens + STATE_PAD, 128), f32)],
        core_arg,
        (me_arg, near, bc_cot, kv_cot, state_part),
    )
    far = swap(far_own, "tensor", 2)
    (few,) = call_dense(
        few_kernel,
        "few",
        [((tokens + SMALL_ROWS, 128), f32)],
        core_arg,
        (
            me_arg, near, far_own, far, bc_cot, kv_cot, norm_two_grad, taps_x_grad, gain_grad,
            heads_grad,
        ),
    )
    few_got = swap(few, "dp", 1)
    few_stages = halving(normed_pair, (few, few_got), True)
    next(zx_stages)
    next(few_stages)
    normed_mine = normed_mine + swap(normed_other, "tensor", 1)

    gots = {"up": [up_one], "gate": [gate_one]}
    totals = {}
    stage_list = {
        "down": down_stages,
        "gate": gate_stages,
        "up": up_stages,
        "mix": mix_stages,
        "zx": zx_stages,
        "few": few_stages,
    }

    def advance(name, *ahead):
        value, got = stage_list[name].send(ahead)
        gots.setdefault(name, []).append(got)
        totals[name] = value
        return value

    last = advance("up", x_cot)
    last = advance("mix", last, far_own)
    last = advance("gate", last, zx_got)
    last = advance("zx", last)
    last = advance("few", last, few)
    normed_mine, normed_other = tensor_halves(normed_mine, (last,))
    last = normed_mine
    last = advance("down", last)
    last = advance("mix", last)
    last = advance("up", last)
    last = advance("gate", last)
    last = advance("few", last)
    last = advance("down", last)
    last = advance("zx", last)
    last = advance("mix", last)
    last = advance("few", last)
    last = advance("down", last)
    last = advance("zx", last)
    (input_grad,) = call_dense(
        input_grad_kernel,
        "input_grad",
        [(wide, bf16)],
        core_arg,
        (normed_mine, normed_other, resid_grad, hidden, norm_one[None, :]),
        scratch=(wide,),
    )
    (layer_out,) = call_dense(
        layer_out_kernel,
        "layer_out",
        [(wide, bf16)],
        core_arg,
        (*tensor_halves(mlp_mine, (x_cot,)), resid),
        scratch=(wide,),
    )
    for name, stages in stage_list.items():
        for value, _ in stages:
            totals[name] = value
    down_shard, mixed_shard = totals["down"], totals["mix"]
    out_shard, o_shard = mixed_shard[:inner_cols], mixed_shard[inner_cols:]
    gu_shard = jnp.stack([totals["gate"], totals["up"]], axis=1)
    zx_total = totals["zx"]
    zx_shard = zx_total[:, : 2 * inner_cols].reshape(-1, 2, inner_cols)
    few_shard = totals["few"]
    shard_rows = model // lax.axis_size("dp")
    q_shard = zx_total[:, 2 * inner_cols : 2 * inner_cols + query_cols]
    dt_shard = zx_total[:, 2 * inner_cols + query_cols :][:, :head_count]
    own, norm_one_grad, state_grad, norm_two_grad, inner_grad, gain_grad, heads_grad = call_dense(
        unpack_kernel,
        "unpack",
        [
            ((shard_rows, 128), f32),
            ((1, model), f32),
            (conv_state.shape, f32),
            ((1, model), f32),
            (conv_inner.shape, f32),
            ((1, inner_cols), f32),
            ((3, HEAD_PAD), f32),
        ],
        core_arg,
        (few_shard,),
    )
    head_sums = heads_grad[:, :head_count]
    near = swap(own, "tensor", 1)
    bc_shard, *kv_parts = call_dense(
        assemble_kernel,
        "assemble",
        [((shard_rows, 256), f32), ((shard_rows, 128), f32), ((shard_rows, 128), f32)],
        core_arg,
        (me_arg, own, near, swap(own, "tensor", 2), swap(own, "tensor", 3)),
    )
    kv_shard = jnp.stack(kv_parts, axis=1)
    return (
        layer_out,
        input_grad,
        norm_one_grad.reshape(-1),
        zx_shard,
        bc_shard,
        dt_shard,
        inner_grad,
        state_grad,
        head_sums[0],
        head_sums[1],
        head_sums[2],
        gain_grad.reshape(-1),
        out_shard,
        q_shard,
        kv_shard,
        o_shard,
        norm_two_grad.reshape(-1),
        gu_shard,
        down_shard,
    )


def solution(mesh):
    placed = (
        P("dp", None),
        P("dp"),
        P("dp", None),
        P(),
        P(None, None, "tensor"),
        P(),
        P(None, "tensor"),
        P(None, "tensor"),
        P(),
        P("tensor"),
        P("tensor"),
        P("tensor"),
        P("tensor"),
        P("tensor", None),
        P(None, "tensor"),
        P(),
        P("tensor", None),
        P(),
        P(None, None, "tensor"),
        P("tensor", None),
    )
    return jax.shard_map(
        on_device,
        mesh=mesh,
        in_specs=placed,
        out_specs=(
            P("dp", None),
            P("dp", None),
            P(),
            P("dp", None, "tensor"),
            P("dp", None),
            P("dp", "tensor"),
            P(None, "tensor"),
            P(),
            P("tensor"),
            P("tensor"),
            P("tensor"),
            P("tensor"),
            P("tensor", "dp"),
            P("dp", "tensor"),
            P("dp", None, None),
            P("tensor", "dp"),
            P(),
            P("dp", None, "tensor"),
            P("tensor", "dp"),
        ),
        check_vma=False,
    )
```
